128 devices in a mesh: row: 4 (over y), col: 32 (over x, z, core).
Axes of the slice: x: 4, y: 4, z: 4, core: 2. Of those that a mesh axis runs over, the one named last changes fastest.
Arguments:
- cov: float32 [18432, 18432], P('row', 'col'), may hold values from -1 to 70, as said below
- weights: float32 [18432], P(('row', 'col')), may hold values from -0.6 to 0.6
- act: bfloat16 [8, 2048, 144], P('row', 'col'), may hold values from -6 to 6
- upstream: bfloat16 [8, 2048, 128], P('row', 'col'), may hold values from -6 to 6
- neighbors: int32 [8, 2048, 138], P('row', 'col'), may hold values from 0 to 2047
- types: int32 [8, 2048], P('row', 'col'), may hold values from 0 to 1
- type_gain: float32 [2, 128], replicated, may hold values from 0.25 to 1.75
- sens: float32 [64, 2048], P('row', 'col'), may hold values from -0.00048828125 to 0.00048828125
- frame_for_measure: int32 [64], P('row'), may hold values from 0 to 1
- noise_variance: float32 [64], replicated, may hold values from 0.5 to 2
- innovation: float32 [64], replicated, may hold values from -6 to 6
Outputs:
- weights_new: float32 [18432], P(('row', 'col'))
- cov_new: float32 [18432, 18432], P('row', 'col')
The draws below stay inside these ranges and needn't reach their ends.
Inputs may be any that keep to these rules, and one draw needn't show every extreme that they name: cov is symmetric and positive definite.
All inputs are finite; a program needn't handle non-finite values. Where the reference program divides by a largest or mean magnitude, that divisor is 1e-20 or more.
Results may differ from the reference program's by a relative error of at most 0.0023.
Values may be sent and summed in bfloat16 or wider, within the bound.
A program may use at most 128 MiB of HBM per device.

```python
import math
import jax
import jax.numpy as jnp
from jax import lax

ACTW = 144
ADJW = 128
NBR = 138
NTYPES = 2
NS_ITERS = 5
FRAME_GROUP = 2
MEASURE_GROUP = 16
BLOCK_WEIGHTS = 18432
ATOM_COUNT = 2048
FRAMES = 8
MEASURE_TOTAL = 64


def draw_cov(key, part):
    noise_key, diag_key, scale_key = jax.random.split(key, 3)
    raw_noise = jax.random.normal(noise_key, (BLOCK_WEIGHTS, BLOCK_WEIGHTS), jnp.float32)
    spread = jax.random.uniform(scale_key, (BLOCK_WEIGHTS,), jnp.float32, 0.0, 2.3025851)
    symmetric = (raw_noise + raw_noise.T) * (0.25 / jnp.sqrt(2.0 * BLOCK_WEIGHTS))
    lifted = 1.0 + jax.random.uniform(diag_key, (BLOCK_WEIGHTS,), jnp.float32)
    diagonal_at = jnp.arange(BLOCK_WEIGHTS, dtype=jnp.int32)
    symmetric = symmetric.at[diagonal_at, diagonal_at].add(lifted)
    scales = jnp.exp(0.5 * spread)
    return symmetric * (scales[:, None] * scales[None, :])


def plant(result, key, low, high):
    extent = result.shape
    index_at = [jax.random.randint(jax.random.fold_in(key, axis), (), 0, extent[axis]) for axis in range(len(extent))]
    result = result.at[tuple(index_at)].set(low)
    longest = extent.index(max(extent))
    index_at[longest] = (index_at[longest] + 1) % extent[longest]
    return result.at[tuple(index_at)].set(high)


def block_levels(rng, dims, cuts, low, high):
    def one(axis_at, parts):
        heights = jax.random.uniform(jax.random.fold_in(jax.random.fold_in(rng, 6), axis_at), (parts,), jnp.float32, low / len(cuts), high / len(cuts))
        return jnp.repeat(jnp.exp(heights), dims[axis_at] // parts).reshape((-1,) + (1,) * (len(dims) - axis_at - 1))

    level = one(*cuts[0])
    for cut in cuts[1:]:
        level = level * one(*cut)
    return level


def scatter_about(key, dims, deviation, most, cuts=(), kind=jnp.bfloat16):
    entries = jax.random.normal(key, dims, jnp.float32) * deviation
    if len(cuts) > 0:
        entries = block_levels(key, dims, cuts, -0.22, 0.18) * entries
    return jnp.clip(entries, min=-most, max=most).astype(kind)


def setup_inputs(seed: int = 0) -> dict:
    splits = jax.random.split(jax.random.key(seed), 12)
    cov = draw_cov(jax.random.fold_in(splits[11], 71), 0)
    weights = scatter_about(splits[1], (BLOCK_WEIGHTS,), 0.1, 0.6, ((0, 128),), jnp.float32)
    act = scatter_about(splits[2], (FRAMES, ATOM_COUNT, ACTW), 1.0, 6.0, ((0, 4), (1, 32)))
    upstream = scatter_about(splits[3], (FRAMES, ATOM_COUNT, ADJW), 1.0, 6.0, ((0, 4), (1, 32)))
    neighbors = plant(jax.random.randint(splits[4], (FRAMES, ATOM_COUNT, NBR), 0, ATOM_COUNT), jax.random.fold_in(splits[4], 1), 0, ATOM_COUNT - 1).astype(jnp.int32)
    types = plant(jax.random.randint(splits[5], (FRAMES, ATOM_COUNT), 0, NTYPES), jax.random.fold_in(splits[5], 1), 0, NTYPES - 1).astype(jnp.int32)
    type_gain = jnp.clip(1.0 + 0.15 * jax.random.normal(splits[6], (NTYPES, ADJW), jnp.float32), 0.25, 1.75)
    sens = scatter_about(splits[7], (MEASURE_TOTAL, ATOM_COUNT), (0.5 / (ATOM_COUNT * BLOCK_WEIGHTS) ** 0.5), 0.00048828125, ((0, 4), (1, 32)), jnp.float32)
    frame_for_measure = plant(jax.random.randint(splits[8], (MEASURE_TOTAL,), 0, FRAME_GROUP), jax.random.fold_in(splits[8], 1), 0, FRAME_GROUP - 1).astype(jnp.int32)
    noise_variance = jnp.clip(jnp.exp(jax.random.uniform(splits[9], (MEASURE_TOTAL,), jnp.float32, math.log(0.5), math.log(2.0))), 0.5, 2.0)
    innovation = scatter_about(splits[10], (MEASURE_TOTAL,), 1.0, 6.0, (), jnp.float32)
    return dict(cov=cov, weights=weights, act=act, upstream=upstream, neighbors=neighbors, types=types, type_gain=type_gain, sens=sens, frame_for_measure=frame_for_measure, noise_variance=noise_variance, innovation=innovation)


FULL_PRECISION = lax.Precision.HIGHEST

def frame_adjoint(pieces):
    lookup, indices, kinds, type_gain = pieces
    picked = jnp.take(lookup, indices, axis=0)
    neighbor_sum = lax.optimization_barrier(jnp.sum(picked, axis=1, dtype=jnp.float32)) * (1.0 / math.sqrt(NBR))
    type_scale = jnp.take(type_gain, kinds, axis=0)
    return type_scale * (lookup.astype(jnp.float32) + neighbor_sum)

def reference(cov, weights, act, upstream, neighbors, types, type_gain, sens, frame_for_measure, noise_variance, innovation):
    adjoint = lax.map(lambda pieces: frame_adjoint((pieces[0], pieces[1], pieces[2], type_gain)), (upstream, neighbors, types))
    frame_numbers = FRAME_GROUP * (jnp.arange(MEASURE_TOTAL, dtype=jnp.int32) // MEASURE_GROUP) + frame_for_measure.astype(jnp.int32)

    def jacobian_row(pieces):
        weight_row, frame_id = pieces
        weighted = (weight_row[:, None] * adjoint[frame_id]).astype(jnp.bfloat16)
        return jnp.dot(weighted.T, act[frame_id], preferred_element_type=jnp.float32).reshape(-1)
    jacobian = lax.map(jacobian_row, (sens, frame_numbers))
    numerator = jnp.dot(cov, jacobian.T, precision=FULL_PRECISION)
    innovation_cov = jnp.dot(jacobian, numerator, precision=FULL_PRECISION) + jnp.diag(noise_variance)
    scale_factor = 1.0 / jnp.max(lax.optimization_barrier(jnp.sum(jnp.abs(innovation_cov), axis=1)))
    inverse_matrix = jnp.eye(MEASURE_TOTAL, dtype=jnp.float32) * scale_factor
    for sweep in range(NS_ITERS):
        inverse_matrix = 2.0 * inverse_matrix - jnp.dot(jnp.dot(inverse_matrix, innovation_cov, precision=FULL_PRECISION), inverse_matrix, precision=FULL_PRECISION)
    gain = jnp.dot(numerator, inverse_matrix, precision=FULL_PRECISION)
    weights_new = weights + jnp.dot(gain, innovation, precision=FULL_PRECISION)
    cov_new = cov - jnp.dot(gain, numerator.T, precision=FULL_PRECISION)
    return (weights_new, cov_new)
```

```python
import functools
import math

import jax
import jax.numpy as jnp
from jax import lax
from jax.experimental import pallas as pl
from jax.experimental.pallas import tpu as pltpu
from jax.sharding import PartitionSpec as P

NS_ITERS = 5
MESH = pl.DeviceIdType.MESH
FULL = lax.Precision.HIGHEST
F32 = jnp.float32
BF16 = jnp.bfloat16
NT = (((1,), (1,)), ((), ()))
TN = (((0,), (0,)), ((), ()))


def gain_kernel(
    rows,
    cols,
    cov_hbm,
    weights_ref,
    act_ref,
    up_ref,
    nb_ref,
    types_ref,
    tgain_ref,
    sens_ref,
    frame_ref,
    noise_ref,
    innov_ref,
    nt_ref,
    g_ref,
    wnew_ref,
    cov_f,
    cov_hi,
    cov_lo,
    nb_all,
    kind_all,
    act_pair,
    sens_pair,
    counts,
    counts_b,
    up_all,
    act_t,
    act_all,
    sens_row,
    sens_all,
    adj_t,
    adj_all,
    w_rows,
    jac_half,
    jac_in,
    jac_piece,
    jac_all,
    n_part,
    n_in,
    n_piece,
    n_col,
    n_slices,
    n_own,
    s_mine,
    s_in,
    cov_sem,
    sib_send,
    sib_recv,
    u_send,
    u_recv,
    a_send,
    a_recv,
    sn_send,
    sn_recv,
    ad_send,
    ad_recv,
    m_send,
    m_recv,
    f_send,
    f_recv,
    y_send,
    y_recv,
    c_send,
    c_recv,
    o_send,
    o_recv,
    s_send,
    s_recv,
):
    r = lax.axis_index("row")
    c = lax.axis_index("col")
    chips = cols // 2
    per = cols // rows
    zs = per // 2
    h = c // 2
    s = c % 2
    x = c // per
    z = (c % per) // 2
    jz = c % per
    other = 1 - s
    sib = c + 1 - 2 * s
    atoms = nb_ref.shape[1]
    pair = 2 * atoms
    nbr = nb_ref.shape[2]
    adjw = up_ref.shape[2]
    actw = act_ref.shape[2]
    mg = sens_ref.shape[0]
    measures = mg * rows
    width = cov_f.shape[1]
    bl = adjw // chips

    def remote(src, dst, ssem, rsem, tr, tc):
        return pltpu.make_async_remote_copy(
            src_ref=src,
            dst_ref=dst,
            send_sem=ssem,
            recv_sem=rsem,
            device_id=(tr, tc),
            device_id_type=MESH,
        )

    cov_in = [
        pltpu.make_async_copy(
            cov_hbm.at[pl.ds(j * width, width)], cov_f.at[j], cov_sem.at[j]
        )
        for j in range(per)
    ]

    sib_copies = [
        remote(nb_ref.at[other], nb_all.at[s], sib_send.at[0], sib_recv.at[0], r, sib),
        remote(act_ref.at[other], act_pair.at[s], sib_send.at[1], sib_recv.at[1], r, sib),
        remote(sens_ref, sens_pair.at[s], sib_send.at[2], sib_recv.at[2], r, sib),
        remote(types_ref.at[other], kind_all.at[s], sib_send.at[3], sib_recv.at[3], r, sib),
    ]
    sib_copies[0].start()
    mine = pl.ds(pl.multiple_of(c * atoms, atoms), atoms)
    own_up = pltpu.make_async_copy(up_ref.at[s], up_all.at[mine], u_recv)
    own_up.start()
    remote(up_ref.at[other], up_all.at[mine], u_send, u_recv, r, sib).start()

    def send_up(k, _):
        to = lax.rem(h + k, chips)
        for f in range(2):
            remote(up_ref.at[f], up_all.at[mine], u_send, u_recv, r, 2 * to + f).start()
        return 0

    lax.fori_loop(1, chips, send_up, 0)
    sib_copies[1].start()
    sib_copies[2].start()
    sib_copies[3].start()
    for copy in cov_in:
        copy.start()

    nb_all[s] = nb_ref[s]
    kind_all[s] = types_ref[s]
    act_pair[s] = act_ref[s]
    sens_pair[s] = sens_ref[...]
    sib_copies[1].wait_recv()
    sib_copies[2].wait_recv()
    act_t[...] = jnp.transpose(
        act_pair[...].reshape(pair, actw).astype(F32)
    ).astype(BF16)
    sens_row[...] = jnp.concatenate([sens_pair[0], sens_pair[1]], axis=1)
    lanes_mine = pl.ds(pl.multiple_of(h * pair, pair), pair)
    own_act = pltpu.make_async_copy(act_t, act_all.at[:, lanes_mine], a_recv)
    own_sens = pltpu.make_async_copy(sens_row, sens_all.at[:, lanes_mine], sn_recv)
    own_act.start()
    own_sens.start()

    def send_act(k, _):
        to = 2 * lax.rem(h + k, chips) + s
        remote(act_t, act_all.at[:, lanes_mine], a_send, a_recv, r, to).start()
        remote(sens_row, sens_all.at[:, lanes_mine], sn_send, sn_recv, r, to).start()
        return 0

    lax.fori_loop(1, chips, send_act, 0)

    sib_copies[0].wait_recv()
    his = counts.shape[0]
    iota_lo = lax.broadcasted_iota(jnp.int32, (128, nbr), 0)
    iota_hi = lax.broadcasted_iota(jnp.int32, (his, nbr), 0)
    unroll = 8

    def count(step, _):
        t = step // (atoms // unroll)
        base = pl.multiple_of(lax.rem(step, atoms // unroll) * unroll, unroll)
        block = nb_all[t, pl.ds(base, unroll), :]
        for u in range(unroll):
            idx = block[u : u + 1, :]
            low = jnp.where((idx & 127) == iota_lo, 1.0, 0.0).astype(BF16)
            high = jnp.where((idx >> 7) == iota_hi, 1.0, 0.0).astype(BF16)
            got = lax.dot_general(high, low, NT, preferred_element_type=F32)
            row = t * atoms + base + u
            counts[:, pl.ds(row, 1), :] = got.reshape(his, 1, 128)
        return 0

    lax.fori_loop(0, pair // unroll, count, 0)
    for k in range(his):
        counts_b[:, k * 128 : (k + 1) * 128] = counts[k].astype(BF16)

    strip = 64

    def split(j):
        def body(i, _):
            at = pl.ds(pl.multiple_of(i * strip, strip), strip)
            value = cov_f[j, at, :]
            high = value.astype(BF16)
            cov_hi[j, at, :] = high
            cov_lo[j, at, :] = (value - high.astype(F32)).astype(BF16)
            return 0

        lax.fori_loop(0, width // strip, body, 0)

    for j in range(per):
        cov_in[j].wait()
        split(j)

    pltpu.make_async_copy(up_all, up_all, u_recv).wait()
    neighbor_sum = jnp.dot(
        counts_b[...], up_all[...], preferred_element_type=F32
    ) * (1.0 / math.sqrt(nbr))
    own = up_all[pl.ds(pl.multiple_of(h * pair, pair), pair), :].astype(F32)
    sib_copies[3].wait_recv()
    kinds = jnp.concatenate([kind_all[0], kind_all[1]], axis=1)
    kinds = jnp.transpose(jnp.broadcast_to(kinds, (adjw, pair)))
    type_scale = jnp.zeros((pair, adjw), F32)
    for kind in range(tgain_ref.shape[0]):
        type_scale = jnp.where(kinds == kind, tgain_ref[kind : kind + 1, :], type_scale)
    adj_t[...] = jnp.transpose(type_scale * (own + neighbor_sum)).reshape(chips, bl, pair)
    own_adj = pltpu.make_async_copy(adj_t.at[h], adj_all.at[:, lanes_mine], ad_recv)
    own_adj.start()

    def send_adj(k, _):
        to = lax.rem(h + k, chips)
        remote(adj_t.at[to], adj_all.at[:, lanes_mine], ad_send, ad_recv, r, 2 * to + s).start()
        return 0

    lax.fori_loop(1, chips, send_adj, 0)

    pltpu.make_async_copy(sens_all, sens_all, sn_recv).wait()
    which = lax.broadcasted_iota(jnp.int32, (mg, 1), 0)
    frame_of = jnp.zeros((mg, 1), jnp.int32)
    for m in range(mg):
        frame_of = jnp.where(which == m, frame_ref[m], frame_of)
    chosen = jnp.where(frame_of == s, 1.0, 0.0).astype(F32)
    sens_all[...] = sens_all[...] * chosen
    pltpu.make_async_copy(act_all, act_all, a_recv).wait()
    pltpu.make_async_copy(adj_all, adj_all, ad_recv).wait()
    for b in range(bl):
        w_rows[mg * b : mg * (b + 1), :] = (sens_all[...] * adj_all[b : b + 1, :]).astype(BF16)
    jac_half[...] = lax.dot_general(
        w_rows[...], act_all[...], NT, preferred_element_type=F32
    ).reshape(2, bl * mg // 2, actw)
    swap = remote(jac_half.at[other], jac_in, sib_send.at[4], sib_recv.at[4], r, sib)
    swap.start()
    swap.wait_recv()
    whole = jac_half[s] + jac_in[...]
    jac_piece[...] = jnp.concatenate(
        [whole[mg * b : mg * (b + 1), :] for b in range(bl // 2)], axis=1
    ).astype(BF16)

    def cast(piece, buf, stage):
        at = pl.ds(pl.multiple_of(mg * r, mg), mg)
        dst = buf.at[jz, at]
        ssem, rsem = m_send.at[stage], m_recv.at[stage, z * rows + r]

        @pl.when(x == r)
        def _():
            pltpu.make_async_copy(piece, dst, rsem).start()

        @pl.when(x != r)
        def _():
            remote(piece, dst, ssem.at[0], rsem, x, c).start()

        def send(k, _):
            to = 2 * lax.rem(h + k, chips) + s
            remote(piece, dst, ssem.at[k], rsem, x, to).start()
            return 0

        lax.fori_loop(1, chips, send, 0)

    def slot(buf, i, core):
        zz = i // rows
        p = lax.rem(i, rows)
        return buf.at[2 * zz + core, pl.ds(pl.multiple_of(mg * p, mg), mg)]

    def relay(buf, stage):
        def step(i, _):
            here = slot(buf, i, s)
            pltpu.make_async_copy(here, here, m_recv.at[stage, i]).wait()
            remote(here, here, f_send.at[stage, i], f_recv.at[stage, i], r, sib).start()
            return 0

        lax.fori_loop(0, chips, step, 0)

    def relayed(buf, stage):
        def step(i, _):
            there = slot(buf, i, other)
            pltpu.make_async_copy(there, there, f_recv.at[stage, i]).wait()
            return 0

        lax.fori_loop(0, chips, step, 0)

    def cast_done(piece, buf, stage):
        @pl.when(x != r)
        def _():
            pltpu.make_async_copy(piece, piece, m_send.at[stage, 0]).wait()

        def step(k, _):
            pltpu.make_async_copy(piece, piece, m_send.at[stage, k]).wait()
            return 0

        lax.fori_loop(1, chips, step, 0)

        def step2(i, _):
            here = slot(buf, i, s)
            pltpu.make_async_copy(here, here, f_send.at[stage, i]).wait()
            return 0

        lax.fori_loop(0, chips, step2, 0)

    cast(jac_piece, jac_all, 0)
    relay(jac_all, 0)

    def times(core):
        def step(zz, _):
            j = 2 * zz + core
            jac = jac_all[j]
            n_part[...] += (
                jnp.dot(jac, cov_hi[j], preferred_element_type=F32)
                + jnp.dot(jac, cov_lo[j], preferred_element_type=F32)
            ).reshape(rows, mg, width)
            return 0

        lax.fori_loop(0, zs, step, 0)

    n_part[...] = jnp.zeros_like(n_part)
    times(s)
    relayed(jac_all, 0)
    times(other)
    for d in range(1, rows):
        to = lax.rem(r + d, rows)
        remote(n_part.at[to], n_in.at[d - 1], y_send.at[d - 1], y_recv.at[d - 1], to, c).start()
    for d in range(1, rows):
        pltpu.make_async_copy(n_in.at[d - 1], n_in.at[d - 1], y_recv.at[d - 1]).wait()
    mine_n = n_part[r]
    for d in range(1, rows):
        mine_n = mine_n + n_in[d - 1]
    n_piece[...] = mine_n.astype(BF16)
    n_col[r] = n_piece[...]
    cast(n_piece, nt_ref, 1)
    for d in range(1, rows):
        to = lax.rem(r + d, rows)
        remote(n_piece, n_col.at[r], c_send.at[d - 1], c_recv.at[d - 1], to, c).start()
    owned = n_slices.shape[2]
    for t in range(width // owned):
        n_slices[t] = mine_n[:, t * owned : (t + 1) * owned]
    for t in range(width // owned):
        to = (width // owned) * jz + t
        here = (x == r) & (to == c)

        @pl.when(here)
        def _():
            pltpu.make_async_copy(n_slices.at[t], n_own.at[r], o_recv.at[r]).start()

        @pl.when(jnp.logical_not(here))
        def _():
            remote(n_slices.at[t], n_own.at[r], o_send.at[t], o_recv.at[r], x, to).start()

    relay(nt_ref, 1)
    relayed(nt_ref, 1)

    def inner(j, acc):
        return acc + lax.dot_general(
            jac_all[j], nt_ref[j], NT, preferred_element_type=F32
        )

    s_mine[...] = lax.fori_loop(0, per, inner, jnp.zeros((measures, measures), F32))
    for d in range(1, rows):
        to = lax.rem(r + d, rows)
        remote(s_mine, s_in.at[d - 1], s_send.at[d - 1], s_recv.at[d - 1], to, c).start()
    for d in range(1, rows):
        pltpu.make_async_copy(s_in.at[d - 1], s_in.at[d - 1], s_recv.at[d - 1]).wait()
    innovation_cov = s_mine[...]
    for d in range(1, rows):
        innovation_cov = innovation_cov + s_in[d - 1]
    i0 = lax.broadcasted_iota(jnp.int32, (measures, measures), 0)
    i1 = lax.broadcasted_iota(jnp.int32, (measures, measures), 1)
    eye = jnp.where(i0 == i1, 1.0, 0.0).astype(F32)
    innovation_cov = innovation_cov + eye * noise_ref[...]
    row_sums = jnp.sum(jnp.abs(innovation_cov), axis=1, keepdims=True)
    first = 1.0 / jnp.max(row_sums, axis=0, keepdims=True)
    inverse = eye * first
    left = eye - innovation_cov * first
    for sweep in range(NS_ITERS):
        inverse = inverse + jnp.dot(inverse, left, precision=FULL, preferred_element_type=F32)
        if sweep < NS_ITERS - 1:
            left = jnp.dot(left, left, precision=FULL, preferred_element_type=F32)
    for d in range(1, rows):
        pltpu.make_async_copy(n_piece, n_piece, c_recv.at[d - 1]).wait()
    n_cols = n_col[...].reshape(measures, width).astype(F32)
    g_ref[...] = jnp.dot(inverse, n_cols, precision=FULL, preferred_element_type=F32).astype(BF16)
    step_col = jnp.sum(inverse * innov_ref[...], axis=1, keepdims=True)
    for p in range(rows):
        pltpu.make_async_copy(n_own.at[p], n_own.at[p], o_recv.at[p]).wait()
    n_mine = n_own[...].reshape(measures, owned)
    wnew_ref[...] = weights_ref[...] + jnp.sum(step_col * n_mine, axis=0, keepdims=True)

    for copy in sib_copies:
        copy.wait_send()
    swap.wait_send()
    sent_up = up_all.at[pl.ds(0, (2 * chips - 1) * atoms)]
    pltpu.make_async_copy(sent_up, sent_up, u_send).wait()
    sent = pl.ds(0, (chips - 1) * pair)
    for buf, sem in ((act_all, a_send), (sens_all, sn_send), (adj_all, ad_send)):
        pltpu.make_async_copy(buf.at[:, sent], buf.at[:, sent], sem).wait()
    cast_done(jac_piece, jac_all, 0)
    cast_done(n_piece, nt_ref, 1)
    for d in range(1, rows):
        pltpu.make_async_copy(n_in.at[0], n_in.at[0], y_send.at[d - 1]).wait()
        pltpu.make_async_copy(n_piece, n_piece, c_send.at[d - 1]).wait()
        pltpu.make_async_copy(s_mine, s_mine, s_send.at[d - 1]).wait()
    for t in range(width // owned):
        to = (width // owned) * jz + t

        @pl.when(jnp.logical_not((x == r) & (to == c)))
        def _():
            pltpu.make_async_copy(n_slices.at[t], n_slices.at[t], o_send.at[t]).wait()


def update_kernel(cov_ref, nt_ref, g_ref, out_ref):
    out_ref[...] = cov_ref[...] - lax.dot_general(
        nt_ref[0], g_ref[...], TN, preferred_element_type=F32
    )


def on_device(
    cov,
    weights,
    act,
    upstream,
    neighbors,
    types,
    type_gain,
    sens,
    frame_for_measure,
    noise_variance,
    innovation,
):
    rows = lax.axis_size("row")
    cols = lax.axis_size("col")
    per = cols // rows
    chips = cols // 2
    frames, atoms, nbr = neighbors.shape
    pair = 2 * atoms
    all_atoms = cols * atoms
    adjw, actw = upstream.shape[2], act.shape[2]
    mg = sens.shape[0]
    measures = mg * rows
    width = cov.shape[1]
    owned = weights.shape[0]
    bl = adjw // chips
    his = all_atoms // 128
    dma = pltpu.SemaphoreType.DMA
    vmem = pl.BlockSpec(memory_space=pltpu.VMEM)
    n_rows, gain, weights_new = pl.pallas_call(
        functools.partial(gain_kernel, rows, cols),
        out_shape=(
            jax.ShapeDtypeStruct((per, measures, width), BF16),
            jax.ShapeDtypeStruct((measures, width), BF16),
            jax.ShapeDtypeStruct((1, owned), F32),
        ),
        in_specs=[pl.BlockSpec(memory_space=pl.ANY)]
        + [vmem] * 7
        + [pl.BlockSpec(memory_space=pltpu.SMEM)]
        + [vmem] * 2,
        out_specs=(vmem,) * 3,
        scratch_shapes=[
            pltpu.VMEM((per, width, width), F32),
            pltpu.VMEM((per, width, width), BF16),
            pltpu.VMEM((per, width, width), BF16),
            pltpu.VMEM((2, atoms, nbr), jnp.int32),
            pltpu.VMEM((2, 1, atoms), jnp.int32),
            pltpu.VMEM((2, atoms, actw), BF16),
            pltpu.VMEM((2, mg, atoms), F32),
            pltpu.VMEM((his, pair, 128), F32),
            pltpu.VMEM((pair, all_atoms), BF16),
            pltpu.VMEM((all_atoms, adjw), BF16),
            pltpu.VMEM((actw, pair), BF16),
            pltpu.VMEM((actw, all_atoms), BF16),
            pltpu.VMEM((mg, pair), F32),
            pltpu.VMEM((mg, all_atoms), F32),
            pltpu.VMEM((chips, bl, pair), F32),
            pltpu.VMEM((bl, all_atoms), F32),
            pltpu.VMEM((bl * mg, all_atoms), BF16),
            pltpu.VMEM((2, bl * mg // 2, actw), F32),
            pltpu.VMEM((bl * mg // 2, actw), F32),
            pltpu.VMEM((mg, width), BF16),
            pltpu.VMEM((per, measures, width), BF16),
            pltpu.VMEM((rows, mg, width), F32),
            pltpu.VMEM((rows - 1, mg, width), F32),
            pltpu.VMEM((mg, width), BF16),
            pltpu.VMEM((rows, mg, width), BF16),
            pltpu.VMEM((width // owned, mg, owned), F32),
            pltpu.VMEM((rows, mg, owned), F32),
            pltpu.VMEM((measures, measures), F32),
            pltpu.VMEM((rows - 1, measures, measures), F32),
            dma((per,)),
            dma((5,)),
            dma((5,)),
            dma,
            dma,
            dma,
            dma,
            dma,
            dma,
            dma,
            dma,
            dma((2, chips)),
            dma((2, chips)),
            dma((2, chips)),
            dma((2, chips)),
            dma((rows - 1,)),
            dma((rows - 1,)),
            dma((rows - 1,)),
            dma((rows - 1,)),
            dma((width // owned,)),
            dma((rows,)),
            dma((rows - 1,)),
            dma((rows - 1,)),
        ],
        compiler_params=pltpu.CompilerParams(
            has_side_effects=True, vmem_limit_bytes=52 * 2**20
        ),
        name="gain",
    )(
        cov,
        weights.reshape(1, owned),
        act,
        upstream,
        neighbors,
        types.reshape(frames, 1, atoms),
        type_gain,
        sens,
        frame_for_measure,
        noise_variance.reshape(1, measures),
        innovation.reshape(1, measures),
    )
    cov_new = pl.pallas_call(
        update_kernel,
        grid=(per,),
        in_specs=[
            pl.BlockSpec((width, width), lambda j: (j, 0)),
            pl.BlockSpec((1, measures, width), lambda j: (j, 0, 0)),
            pl.BlockSpec((measures, width), lambda j: (0, 0)),
        ],
        out_specs=pl.BlockSpec((width, width), lambda j: (j, 0)),
        out_shape=jax.ShapeDtypeStruct(cov.shape, F32),
        compiler_params=pltpu.CompilerParams(vmem_limit_bytes=32 * 2**20),
        name="update",
    )(cov, n_rows, gain)
    return weights_new.reshape(owned), cov_new


def solution(mesh):
    return jax.shard_map(
        on_device,
        mesh=mesh,
        in_specs=(
            P("row", "col"),
            P(("row", "col")),
            P("row", "col", None),
            P("row", "col", None),
            P("row", "col", None),
            P("row", "col"),
            P(),
            P("row", "col"),
            P("row"),
            P(),
            P(),
        ),
        out_specs=(P(("row", "col")), P("row", "col")),
        check_vma=False,
    )
```

```python
import functools
import math

import jax
import jax.numpy as jnp
from jax import lax
from jax.experimental import pallas as pl
from jax.experimental.pallas import tpu as pltpu
from jax.sharding import PartitionSpec as P

NS_ITERS = 5
MESH = pl.DeviceIdType.MESH
FULL = lax.Precision.HIGHEST
F32 = jnp.float32
BF16 = jnp.bfloat16
NT = (((1,), (1,)), ((), ()))


def gain_kernel(
    rows,
    cols,
    cov_hbm,
    weights_ref,
    act_ref,
    up_ref,
    nb_ref,
    types_ref,
    tgain_ref,
    sens_ref,
    frame_ref,
    noise_ref,
    innov_ref,
    nt_ref,
    gt_ref,
    wnew_ref,
    cov_f,
    cov_hi,
    cov_lo,
    nb_all,
    kind_all,
    act_pair,
    sens_pair,
    counts,
    counts_b,
    up_all,
    act_t,
    act_all,
    sens_row,
    sens_all,
    adj_t,
    adj_all,
    w_rows,
    jac_half,
    jac_in,
    jac_piece,
    jac_all,
    n_part,
    n_in,
    n_piece,
    n_pair,
    n_wide,
    n_col,
    n_slices,
    n_own,
    s_mine,
    s_in,
    cov_sem,
    sib_send,
    sib_recv,
    u_send,
    u_recv,
    a_send,
    a_recv,
    sn_send,
    sn_recv,
    ad_send,
    ad_recv,
    m_send,
    m_recv,
    f_send,
    f_recv,
    y_send,
    y_recv,
    c_send,
    c_recv,
    o_send,
    o_recv,
    s_send,
    s_recv,
):
    r = lax.axis_index("row")
    c = lax.axis_index("col")
    chips = cols // 2
    per = cols // rows
    zs = per // 2
    h = c // 2
    s = c % 2
    x = c // per
    z = (c % per) // 2
    jz = c % per
    parity = lax.rem(h + s, 2)
    drains = []
    other = 1 - s
    sib = c + 1 - 2 * s
    atoms = nb_ref.shape[1]
    pair = 2 * atoms
    nbr = nb_ref.shape[2]
    adjw = up_ref.shape[2]
    actw = act_ref.shape[2]
    mg = sens_ref.shape[0]
    measures = mg * rows
    width, chunk = cov_f.shape[1:]
    bl = adjw // chips

    def remote(src, dst, ssem, rsem, tr, tc):
        return pltpu.make_async_remote_copy(
            src_ref=src,
            dst_ref=dst,
            send_sem=ssem,
            recv_sem=rsem,
            device_id=(tr, tc),
            device_id_type=MESH,
        )

    cov_in = [
        pltpu.make_async_copy(
            cov_hbm.at[:, pl.ds(j * chunk, chunk)], cov_f.at[j], cov_sem.at[j]
        )
        for j in range(zs)
    ]

    sib_copies = [
        remote(nb_ref.at[other], nb_all.at[s], sib_send.at[0], sib_recv.at[0], r, sib),
        remote(act_ref.at[other], act_pair.at[s], sib_send.at[1], sib_recv.at[1], r, sib),
        remote(sens_ref, sens_pair.at[s], sib_send.at[2], sib_recv.at[2], r, sib),
        remote(types_ref.at[other], kind_all.at[s], sib_send.at[3], sib_recv.at[3], r, sib),
    ]
    sib_copies[0].start()
    mine = pl.ds(pl.multiple_of(c * atoms, atoms), atoms)
    own_up = pltpu.make_async_copy(up_ref.at[s], up_all.at[mine], u_recv)
    own_up.start()
    remote(up_ref.at[other], up_all.at[mine], u_send, u_recv, r, sib).start()

    def send_up(k, _):
        to = lax.rem(h + k, chips)
        for f in range(2):
            remote(up_ref.at[f], up_all.at[mine], u_send, u_recv, r, 2 * to + f).start()
        return 0

    lax.fori_loop(1, chips, send_up, 0)
    sib_copies[1].start()
    sib_copies[2].start()
    sib_copies[3].start()
    for copy in cov_in:
        copy.start()

    nb_all[s] = nb_ref[s]
    kind_all[s] = types_ref[s]
    act_pair[s] = act_ref[s]
    sens_pair[s] = sens_ref[...]
    sib_copies[1].wait_recv()
    sib_copies[2].wait_recv()
    act_t[...] = jnp.transpose(
        act_pair[...].reshape(pair, actw).astype(F32)
    ).astype(BF16)
    sens_row[...] = jnp.concatenate([sens_pair[0], sens_pair[1]], axis=1)
    lanes_mine = pl.ds(pl.multiple_of(h * pair, pair), pair)
    own_act = pltpu.make_async_copy(act_t, act_all.at[:, lanes_mine], a_recv)
    own_sens = pltpu.make_async_copy(sens_row, sens_all.at[:, lanes_mine], sn_recv)
    own_act.start()
    own_sens.start()

    def send_act(k, _):
        to = 2 * lax.rem(h + k, chips) + s
        remote(act_t, act_all.at[:, lanes_mine], a_send, a_recv, r, to).start()
        remote(sens_row, sens_all.at[:, lanes_mine], sn_send, sn_recv, r, to).start()
        return 0

    lax.fori_loop(1, chips, send_act, 0)

    def drain_first():
        for copy in sib_copies:
            copy.wait_send()
        sent_up = up_all.at[pl.ds(0, (2 * chips - 1) * atoms)]
        pltpu.make_async_copy(sent_up, sent_up, u_send).wait()
        for buf, sem in ((act_all, a_send), (sens_all, sn_send)):
            part = buf.at[:, pl.ds(0, (chips - 1) * pair)]
            pltpu.make_async_copy(part, part, sem).wait()

    drains.append(drain_first)

    sib_copies[0].wait_recv()
    his = counts.shape[0]
    iota_lo = lax.broadcasted_iota(jnp.int32, (128, nbr), 0)
    iota_hi = lax.broadcasted_iota(jnp.int32, (his, nbr), 0)
    unroll = 8

    def count(step, _):
        t = step // (atoms // unroll)
        base = pl.multiple_of(lax.rem(step, atoms // unroll) * unroll, unroll)
        block = nb_all[t, pl.ds(base, unroll), :]
        for u in range(unroll):
            idx = block[u : u + 1, :]
            low = jnp.where((idx & 127) == iota_lo, 1.0, 0.0).astype(BF16)
            high = jnp.where((idx >> 7) == iota_hi, 1.0, 0.0).astype(BF16)
            got = lax.dot_general(high, low, NT, preferred_element_type=F32)
            row = t * atoms + base + u
            counts[:, pl.ds(row, 1), :] = got.reshape(his, 1, 128)
        return 0

    lax.fori_loop(0, pair // unroll, count, 0)
    for k in range(his):
        counts_b[:, k * 128 : (k + 1) * 128] = counts[k].astype(BF16)

    strip = 64

    def split(j):
        def body(i, _):
            at = pl.ds(pl.multiple_of(i * strip, strip), strip)
            value = cov_f[j, at, :]
            high = value.astype(BF16)
            cov_hi[j, at, :] = high
            cov_lo[j, at, :] = (value - high.astype(F32)).astype(BF16)
            return 0

        lax.fori_loop(0, width // strip, body, 0)

    for j in range(zs):
        cov_in[j].wait()
        split(j)

    pltpu.make_async_copy(up_all, up_all, u_recv).wait()
    neighbor_sum = jnp.dot(
        counts_b[...], up_all[...], preferred_element_type=F32
    ) * (1.0 / math.sqrt(nbr))
    own = up_all[pl.ds(pl.multiple_of(h * pair, pair), pair), :].astype(F32)
    sib_copies[3].wait_recv()
    kinds = jnp.concatenate([kind_all[0], kind_all[1]], axis=1)
    kinds = jnp.transpose(jnp.broadcast_to(kinds, (adjw, pair)))
    type_scale = jnp.zeros((pair, adjw), F32)
    for kind in range(tgain_ref.shape[0]):
        type_scale = jnp.where(kinds == kind, tgain_ref[kind : kind + 1, :], type_scale)
    adj_t[...] = jnp.transpose(type_scale * (own + neighbor_sum)).reshape(chips, bl, pair)
    own_adj = pltpu.make_async_copy(adj_t.at[h], adj_all.at[:, lanes_mine], ad_recv)
    own_adj.start()

    def send_adj(k, _):
        to = lax.rem(h + k, chips)
        remote(adj_t.at[to], adj_all.at[:, lanes_mine], ad_send, ad_recv, r, 2 * to + s).start()
        return 0

    lax.fori_loop(1, chips, send_adj, 0)

    def drain_adj():
        part = adj_all.at[:, pl.ds(0, (chips - 1) * pair)]
        pltpu.make_async_copy(part, part, ad_send).wait()

    drains.append(drain_adj)

    pltpu.make_async_copy(sens_all, sens_all, sn_recv).wait()
    which = lax.broadcasted_iota(jnp.int32, (mg, 1), 0)
    frame_of = jnp.zeros((mg, 1), jnp.int32)
    for m in range(mg):
        frame_of = jnp.where(which == m, frame_ref[m], frame_of)
    chosen = jnp.where(frame_of == s, 1.0, 0.0).astype(F32)
    sens_all[...] = sens_all[...] * chosen
    pltpu.make_async_copy(act_all, act_all, a_recv).wait()
    pltpu.make_async_copy(adj_all, adj_all, ad_recv).wait()
    for b in range(bl):
        w_rows[mg * b : mg * (b + 1), :] = (sens_all[...] * adj_all[b : b + 1, :]).astype(BF16)
    jac_half[...] = lax.dot_general(
        w_rows[...], act_all[...], NT, preferred_element_type=F32
    )
    swap = remote(jac_half, jac_in, sib_send.at[4], sib_recv.at[4], r, sib)
    swap.start()
    swap.wait_recv()
    whole = jac_half[...] + jac_in[...]
    jac_piece[...] = jnp.concatenate(
        [whole[mg * b : mg * (b + 1), :] for b in range(bl)], axis=1
    ).astype(BF16)
    drains.append(swap.wait_send)

    half = chips // 2

    def cast(piece, buf, stage):
        at = pl.ds(pl.multiple_of(mg * r, mg), mg)
        lanes = pl.ds(pl.multiple_of(chunk * z, chunk), chunk)
        dst = buf.at[at, lanes]
        rsem = m_recv.at[stage, z * rows + r]
        own = (x == r) & (s == 0)

        @pl.when(own)
        def _():
            pltpu.make_async_copy(piece, dst, rsem).start()

        @pl.when(jnp.logical_not(own))
        def _():
            to = 2 * lax.rem(h + s, chips) + s
            remote(piece, dst, m_send.at[stage, 0], rsem, x, to).start()

        def send(i, _):
            to = 2 * lax.rem(h + 2 * i + s, chips) + s
            remote(piece, dst, m_send.at[stage, i], rsem, x, to).start()
            return 0

        lax.fori_loop(1, half, send, 0)

        def drain():
            @pl.when(jnp.logical_not(own))
            def _():
                pltpu.make_async_copy(piece, piece, m_send.at[stage, 0]).wait()

            def step(i, _):
                pltpu.make_async_copy(piece, piece, m_send.at[stage, i]).wait()
                return 0

            lax.fori_loop(1, half, step, 0)

        drains.append(drain)

    def slot(buf, i, which):
        zz = 2 * (i // rows) + which
        p = lax.rem(i, rows)
        lanes = pl.ds(pl.multiple_of(chunk * zz, chunk), chunk)
        return buf.at[pl.ds(pl.multiple_of(mg * p, mg), mg), lanes], zz * rows + p

    def relay(buf, stage):
        def step(i, _):
            here, k = slot(buf, i, parity)
            pltpu.make_async_copy(here, here, m_recv.at[stage, k]).wait()
            remote(here, here, f_send.at[stage, i], f_recv.at[stage, k], r, sib).start()
            return 0

        lax.fori_loop(0, half, step, 0)

        def drain():
            def step2(i, _):
                here, _ = slot(buf, i, parity)
                pltpu.make_async_copy(here, here, f_send.at[stage, i]).wait()
                return 0

            lax.fori_loop(0, half, step2, 0)

        drains.append(drain)

    def relayed(buf, stage):
        def step(i, _):
            there, k = slot(buf, i, 1 - parity)
            pltpu.make_async_copy(there, there, f_recv.at[stage, k]).wait()
            return 0

        lax.fori_loop(0, half, step, 0)

    cast(jac_piece, jac_all, 0)
    relay(jac_all, 0)

    def times(which):
        def step(i, _):
            zz = 2 * i + which
            jac = jac_all[:, pl.ds(pl.multiple_of(chunk * zz, chunk), chunk)]
            n_part[...] += (
                lax.dot_general(jac, cov_hi[zz], NT, preferred_element_type=F32)
                + lax.dot_general(jac, cov_lo[zz], NT, preferred_element_type=F32)
            ).reshape(rows, mg, width)
            return 0

        lax.fori_loop(0, zs // 2, step, 0)

    n_part[...] = jnp.zeros_like(n_part)
    times(parity)
    relayed(jac_all, 0)
    times(1 - parity)
    for d in range(1, rows):
        to = lax.rem(r + d, rows)
        copy = remote(n_part.at[to], n_in.at[d - 1], y_send.at[d - 1], y_recv.at[d - 1], to, c)
        copy.start()
        drains.append(copy.wait_send)
    for d in range(1, rows):
        pltpu.make_async_copy(n_in.at[d - 1], n_in.at[d - 1], y_recv.at[d - 1]).wait()
    mine_n = n_part[r]
    for d in range(1, rows):
        mine_n = mine_n + n_in[d - 1]
    n_piece[...] = mine_n.astype(BF16)
    swap_n = remote(n_piece, n_pair.at[s], sib_send.at[5], sib_recv.at[5], r, sib)
    swap_n.start()
    drains.append(swap_n.wait_send)
    n_pair[s] = n_piece[...]
    n_col[r] = n_piece[...]
    for d in range(1, rows):
        to = lax.rem(r + d, rows)
        copy = remote(n_piece, n_col.at[r], c_send.at[d - 1], c_recv.at[d - 1], to, c)
        copy.start()
        drains.append(copy.wait_send)
    swap_n.wait_recv()
    n_wide[...] = jnp.concatenate(
        [n_pair[0].astype(F32), n_pair[1].astype(F32)], axis=1
    ).astype(BF16)
    cast(n_wide, nt_ref, 1)
    owned = n_slices.shape[2]
    for t in range(rows):
        n_slices[t] = mine_n[:, t * owned : (t + 1) * owned]
    for t in range(rows):
        to = rows * jz + t
        here = (x == r) & (to == c)

        @pl.when(here)
        def _():
            pltpu.make_async_copy(n_slices.at[t], n_own.at[r], o_recv.at[r]).start()

        @pl.when(jnp.logical_not(here))
        def _():
            remote(n_slices.at[t], n_own.at[r], o_send.at[t], o_recv.at[r], x, to).start()

    relay(nt_ref, 1)
    relayed(nt_ref, 1)

    s_mine[...] = lax.dot_general(
        jac_all[...], nt_ref[...], NT, preferred_element_type=F32
    )
    for d in range(1, rows):
        to = lax.rem(r + d, rows)
        copy = remote(s_mine, s_in.at[d - 1], s_send.at[d - 1], s_recv.at[d - 1], to, c)
        copy.start()
        drains.append(copy.wait_send)
    for d in range(1, rows):
        pltpu.make_async_copy(s_in.at[d - 1], s_in.at[d - 1], s_recv.at[d - 1]).wait()
    innovation_cov = s_mine[...]
    for d in range(1, rows):
        innovation_cov = innovation_cov + s_in[d - 1]
    i0 = lax.broadcasted_iota(jnp.int32, (measures, measures), 0)
    i1 = lax.broadcasted_iota(jnp.int32, (measures, measures), 1)
    eye = jnp.where(i0 == i1, 1.0, 0.0).astype(F32)
    innovation_cov = innovation_cov + eye * noise_ref[...]
    row_sums = jnp.sum(jnp.abs(innovation_cov), axis=1, keepdims=True)
    first = 1.0 / jnp.max(row_sums, axis=0, keepdims=True)
    inverse = eye * first
    left = eye - innovation_cov * first
    for sweep in range(NS_ITERS):
        inverse = inverse + jnp.dot(inverse, left, precision=FULL, preferred_element_type=F32)
        if sweep < NS_ITERS - 1:
            left = jnp.dot(left, left, precision=FULL, preferred_element_type=F32)
    for d in range(1, rows):
        pltpu.make_async_copy(n_piece, n_piece, c_recv.at[d - 1]).wait()
    n_cols = n_col[...].reshape(measures, width).astype(F32)
    gt_ref[...] = jnp.transpose(
        jnp.dot(inverse, n_cols, precision=FULL, preferred_element_type=F32)
    ).astype(BF16)
    step_col = jnp.sum(inverse * innov_ref[...], axis=1, keepdims=True)
    for p in range(rows):
        pltpu.make_async_copy(n_own.at[p], n_own.at[p], o_recv.at[p]).wait()
    n_mine = n_own[...].reshape(measures, owned)
    wnew_ref[...] = weights_ref[...] + jnp.sum(step_col * n_mine, axis=0, keepdims=True)
    for t in range(rows):
        to = rows * jz + t

        @pl.when(jnp.logical_not((x == r) & (to == c)))
        def _():
            pltpu.make_async_copy(n_slices.at[t], n_slices.at[t], o_send.at[t]).wait()

    for drain in drains:
        drain()


def update_kernel(cov_ref, nt_ref, gt_ref, out_ref):
    out_ref[...] = cov_ref[...] - jnp.dot(
        gt_ref[...], nt_ref[...], preferred_element_type=F32
    )


def on_device(
    cov,
    weights,
    act,
    upstream,
    neighbors,
    types,
    type_gain,
    sens,
    frame_for_measure,
    noise_variance,
    innovation,
):
    rows = lax.axis_size("row")
    cols = lax.axis_size("col")
    per = cols // rows
    chips = cols // 2
    frames, atoms, nbr = neighbors.shape
    pair = 2 * atoms
    all_atoms = cols * atoms
    adjw, actw = upstream.shape[2], act.shape[2]
    mg = sens.shape[0]
    measures = mg * rows
    height, width = cov.shape
    zs = per // 2
    chunk = height // zs
    owned = weights.shape[0]
    bl = adjw // chips
    his = all_atoms // 128
    dma = pltpu.SemaphoreType.DMA
    vmem = pl.BlockSpec(memory_space=pltpu.VMEM)
    covariance = cov.T
    n_rows, gain, weights_new = pl.pallas_call(
        functools.partial(gain_kernel, rows, cols),
        out_shape=(
            jax.ShapeDtypeStruct((measures, height), BF16),
            jax.ShapeDtypeStruct((width, measures), BF16),
            jax.ShapeDtypeStruct((1, owned), F32),
        ),
        in_specs=[pl.BlockSpec(memory_space=pl.ANY)]
        + [vmem] * 7
        + [pl.BlockSpec(memory_space=pltpu.SMEM)]
        + [vmem] * 2,
        out_specs=(vmem,) * 3,
        scratch_shapes=[
            pltpu.VMEM((zs, width, chunk), F32),
            pltpu.VMEM((zs, width, chunk), BF16),
            pltpu.VMEM((zs, width, chunk), BF16),
            pltpu.VMEM((2, atoms, nbr), jnp.int32),
            pltpu.VMEM((2, 1, atoms), jnp.int32),
            pltpu.VMEM((2, atoms, actw), BF16),
            pltpu.VMEM((2, mg, atoms), F32),
            pltpu.VMEM((his, pair, 128), F32),
            pltpu.VMEM((pair, all_atoms), BF16),
            pltpu.VMEM((all_atoms, adjw), BF16),
            pltpu.VMEM((actw, pair), BF16),
            pltpu.VMEM((actw, all_atoms), BF16),
            pltpu.VMEM((mg, pair), F32),
            pltpu.VMEM((mg, all_atoms), F32),
            pltpu.VMEM((chips, bl, pair), F32),
            pltpu.VMEM((bl, all_atoms), F32),
            pltpu.VMEM((bl * mg, all_atoms), BF16),
            pltpu.VMEM((bl * mg, actw), F32),
            pltpu.VMEM((bl * mg, actw), F32),
            pltpu.VMEM((mg, chunk), BF16),
            pltpu.VMEM((measures, height), BF16),
            pltpu.VMEM((rows, mg, width), F32),
            pltpu.VMEM((rows - 1, mg, width), F32),
            pltpu.VMEM((mg, width), BF16),
            pltpu.VMEM((2, mg, width), BF16),
            pltpu.VMEM((mg, chunk), BF16),
            pltpu.VMEM((rows, mg, width), BF16),
            pltpu.VMEM((rows, mg, owned), F32),
            pltpu.VMEM((rows, mg, owned), F32),
            pltpu.VMEM((measures, measures), F32),
            pltpu.VMEM((rows - 1, measures, measures), F32),
            dma((zs,)),
            dma((6,)),
            dma((6,)),
            dma,
            dma,
            dma,
            dma,
            dma,
            dma,
            dma,
            dma,
            dma((2, chips // 2)),
            dma((2, zs * rows)),
            dma((2, chips // 2)),
            dma((2, zs * rows)),
            dma((rows - 1,)),
            dma((rows - 1,)),
            dma((rows - 1,)),
            dma((rows - 1,)),
            dma((rows,)),
            dma((rows,)),
            dma((rows - 1,)),
            dma((rows - 1,)),
        ],
        compiler_params=pltpu.CompilerParams(
            has_side_effects=True, vmem_limit_bytes=52 * 2**20
        ),
        name="gain",
    )(
        covariance,
        weights.reshape(1, owned),
        act,
        upstream,
        neighbors,
        types.reshape(frames, 1, atoms),
        type_gain,
        sens,
        frame_for_measure,
        noise_variance.reshape(1, measures),
        innovation.reshape(1, measures),
    )
    tile = width // per
    cov_new = pl.pallas_call(
        update_kernel,
        grid=(per,),
        in_specs=[
            pl.BlockSpec((tile, height), lambda j: (j, 0)),
            pl.BlockSpec((measures, height), lambda j: (0, 0)),
            pl.BlockSpec((tile, measures), lambda j: (j, 0)),
        ],
        out_specs=pl.BlockSpec((tile, height), lambda j: (j, 0)),
        out_shape=jax.ShapeDtypeStruct((width, height), F32),
        compiler_params=pltpu.CompilerParams(vmem_limit_bytes=32 * 2**20),
        name="update",
    )(covariance, n_rows, gain)
    return weights_new.reshape(owned), cov_new.T


def solution(mesh):
    return jax.shard_map(
        on_device,
        mesh=mesh,
        in_specs=(
            P("row", "col"),
            P(("row", "col")),
            P("row", "col", None),
            P("row", "col", None),
            P("row", "col", None),
            P("row", "col"),
            P(),
            P("row", "col"),
            P("row"),
            P(),
            P(),
        ),
        out_specs=(P(("row", "col")), P("row", "col")),
        check_vma=False,
    )
```

```python
import functools
import math

import jax
import jax.numpy as jnp
from jax import lax
from jax.experimental import pallas as pl
from jax.experimental.pallas import tpu as pltpu
from jax.sharding import PartitionSpec as P

NS_ITERS = 5
MESH = pl.DeviceIdType.MESH
FULL = lax.Precision.HIGHEST
F32 = jnp.float32
BF16 = jnp.bfloat16
NT = (((1,), (1,)), ((), ()))


def gain_kernel(
    rows,
    cols,
    cov_hbm,
    weights_hbm,
    act_hbm,
    up_hbm,
    nb_hbm,
    types_hbm,
    tgain_hbm,
    sens_hbm,
    frame_hbm,
    noise_hbm,
    innov_hbm,
    nt_ref,
    gt_ref,
    wnew_ref,
    cov_f,
    weights_ref,
    up_ref,
    tgain_ref,
    frame_ref,
    noise_ref,
    innov_ref,
    cov_hi,
    cov_lo,
    nb_all,
    kind_all,
    act_pair,
    sens_pair,
    counts,
    counts_b,
    up_all,
    act_t,
    act_all,
    sens_row,
    sens_all,
    adj_t,
    adj_all,
    w_rows,
    jac_half,
    jac_in,
    jac_piece,
    jac_all,
    n_part,
    n_in,
    n_piece,
    n_pair,
    n_wide,
    n_col,
    n_slices,
    n_own,
    s_mine,
    s_in,
    load_sem,
    cov_sem,
    row_in,
    sib_send,
    sib_recv,
    u_send,
    u_recv,
    a_send,
    a_recv,
    sn_send,
    sn_recv,
    ad_send,
    ad_recv,
    m_send,
    m_recv,
    f_send,
    f_recv,
    y_send,
    y_recv,
    c_send,
    c_recv,
    o_send,
    o_recv,
    s_send,
    s_recv,
):
    r = lax.axis_index("row")
    c = lax.axis_index("col")
    chips = cols // 2
    per = cols // rows
    zs = per // 2
    h = c // 2
    s = c % 2
    x = c // per
    z = (c % per) // 2
    jz = c % per
    parity = lax.rem(h + s, 2)
    drains = []
    other = 1 - s
    sib = c + 1 - 2 * s
    atoms = nb_hbm.shape[1]
    pair = 2 * atoms
    nbr = nb_hbm.shape[2]
    adjw = up_hbm.shape[2]
    actw = act_hbm.shape[2]
    mg = sens_hbm.shape[0]
    measures = mg * rows
    width, chunk = cov_hi.shape[1:]
    bl = adjw // chips

    def remote(src, dst, ssem, rsem, tr, tc):
        return pltpu.make_async_remote_copy(
            src_ref=src,
            dst_ref=dst,
            send_sem=ssem,
            recv_sem=rsem,
            device_id=(tr, tc),
            device_id_type=MESH,
        )

    cov_in = [
        pltpu.make_async_copy(
            cov_hbm.at[:, pl.ds(j * chunk, chunk)],
            cov_f.at[:, pl.ds(j * chunk, chunk)],
            cov_sem.at[j],
        )
        for j in range(zs)
    ]

    barrier = pltpu.get_barrier_semaphore()

    def greet(k, _):
        to = lax.rem(c + k, cols)
        pl.semaphore_signal(barrier, inc=1, device_id=(r, to), device_id_type=MESH)
        return 0

    lax.fori_loop(1, cols, greet, 0)
    for d in range(1, rows):
        to = lax.rem(r + d, rows)
        pl.semaphore_signal(barrier, inc=1, device_id=(to, c), device_id_type=MESH)
    loads = [
        pltpu.make_async_copy(src, dst, load_sem.at[i])
        for i, (src, dst) in enumerate(
            (
                (up_hbm, up_ref),
                (nb_hbm.at[s], nb_all.at[s]),
                (act_hbm.at[s], act_pair.at[s]),
                (sens_hbm, sens_pair.at[s]),
                (types_hbm.at[s], kind_all.at[s]),
                (tgain_hbm, tgain_ref),
                (frame_hbm, frame_ref),
                (noise_hbm, noise_ref),
                (innov_hbm, innov_ref),
                (weights_hbm, weights_ref),
            )
        )
    ]
    for load in loads:
        load.start()
    loads[0].wait()
    pl.semaphore_wait(barrier, cols - 1 + rows - 1)

    sib_copies = [
        remote(nb_hbm.at[other], nb_all.at[s], sib_send.at[0], sib_recv.at[0], r, sib),
        remote(act_hbm.at[other], act_pair.at[s], sib_send.at[1], sib_recv.at[1], r, sib),
        remote(sens_hbm, sens_pair.at[s], sib_send.at[2], sib_recv.at[2], r, sib),
        remote(types_hbm.at[other], kind_all.at[s], sib_send.at[3], sib_recv.at[3], r, sib),
    ]
    sib_copies[0].start()
    mine = pl.ds(pl.multiple_of(c * atoms, atoms), atoms)
    own_up = pltpu.make_async_copy(up_ref.at[s], up_all.at[mine], u_recv)
    own_up.start()
    remote(up_ref.at[other], up_all.at[mine], u_send, u_recv, r, sib).start()

    def send_up(k, _):
        to = lax.rem(h + k, chips)
        for f in range(2):
            remote(up_ref.at[f], up_all.at[mine], u_send, u_recv, r, 2 * to + f).start()
        return 0

    lax.fori_loop(1, chips, send_up, 0)
    sib_copies[1].start()
    sib_copies[2].start()
    sib_copies[3].start()
    for copy in cov_in:
        copy.start()

    for d in range(1, rows):
        to = lax.rem(r + d, rows)
        pl.semaphore_signal(row_in, inc=1, device_id=(to, c), device_id_type=MESH)
    for load in loads[1:]:
        load.wait()
    sib_copies[1].wait_recv()
    sib_copies[2].wait_recv()
    act_t[...] = jnp.transpose(
        act_pair[...].reshape(pair, actw).astype(F32)
    ).astype(BF16)
    sens_row[...] = jnp.concatenate([sens_pair[0], sens_pair[1]], axis=1)
    lanes_mine = pl.ds(pl.multiple_of(h * pair, pair), pair)
    own_act = pltpu.make_async_copy(act_t, act_all.at[:, lanes_mine], a_recv)
    own_sens = pltpu.make_async_copy(sens_row, sens_all.at[:, lanes_mine], sn_recv)
    own_act.start()
    own_sens.start()

    def send_act(k, _):
        to = 2 * lax.rem(h + k, chips) + s
        remote(act_t, act_all.at[:, lanes_mine], a_send, a_recv, r, to).start()
        remote(sens_row, sens_all.at[:, lanes_mine], sn_send, sn_recv, r, to).start()
        return 0

    lax.fori_loop(1, chips, send_act, 0)

    def drain_first():
        for copy in sib_copies:
            copy.wait_send()
        sent_up = up_all.at[pl.ds(0, (2 * chips - 1) * atoms)]
        pltpu.make_async_copy(sent_up, sent_up, u_send).wait()
        for buf, sem in ((act_all, a_send), (sens_all, sn_send)):
            part = buf.at[:, pl.ds(0, (chips - 1) * pair)]
            pltpu.make_async_copy(part, part, sem).wait()

    drains.append(drain_first)

    sib_copies[0].wait_recv()
    his = counts.shape[0]
    iota_lo = lax.broadcasted_iota(jnp.int32, (128, nbr), 0)
    iota_hi = lax.broadcasted_iota(jnp.int32, (his, nbr), 0)
    unroll = 8

    def count(step, _):
        t = step // (atoms // unroll)
        base = pl.multiple_of(lax.rem(step, atoms // unroll) * unroll, unroll)
        block = nb_all[t, pl.ds(base, unroll), :]
        for u in range(unroll):
            idx = block[u : u + 1, :]
            low = jnp.where((idx & 127) == iota_lo, 1.0, 0.0).astype(BF16)
            high = jnp.where((idx >> 7) == iota_hi, 1.0, 0.0).astype(BF16)
            got = lax.dot_general(high, low, NT, preferred_element_type=F32)
            row = t * atoms + base + u
            counts[:, pl.ds(row, 1), :] = got.reshape(his, 1, 128)
        return 0

    lax.fori_loop(0, pair // unroll, count, 0)
    for k in range(his):
        counts_b[:, k * 128 : (k + 1) * 128] = counts[k].astype(BF16)

    pltpu.make_async_copy(up_all, up_all, u_recv).wait()
    neighbor_sum = jnp.dot(
        counts_b[...], up_all[...], preferred_element_type=F32
    ) * (1.0 / math.sqrt(nbr))
    own = up_all[pl.ds(pl.multiple_of(h * pair, pair), pair), :].astype(F32)
    sib_copies[3].wait_recv()
    kinds = jnp.concatenate([kind_all[0], kind_all[1]], axis=1)
    kinds = jnp.transpose(jnp.broadcast_to(kinds, (adjw, pair)))
    type_scale = jnp.zeros((pair, adjw), F32)
    for kind in range(tgain_ref.shape[0]):
        type_scale = jnp.where(kinds == kind, tgain_ref[kind : kind + 1, :], type_scale)
    adj_t[...] = jnp.transpose(type_scale * (own + neighbor_sum)).reshape(chips, bl, pair)
    own_adj = pltpu.make_async_copy(adj_t.at[h], adj_all.at[:, lanes_mine], ad_recv)
    own_adj.start()

    def send_adj(k, _):
        to = lax.rem(h + k, chips)
        remote(adj_t.at[to], adj_all.at[:, lanes_mine], ad_send, ad_recv, r, 2 * to + s).start()
        return 0

    lax.fori_loop(1, chips, send_adj, 0)

    def drain_adj():
        part = adj_all.at[:, pl.ds(0, (chips - 1) * pair)]
        pltpu.make_async_copy(part, part, ad_send).wait()

    drains.append(drain_adj)

    strip = 64

    def split(j):
        def body(i, _):
            at = pl.ds(pl.multiple_of(i * strip, strip), strip)
            value = cov_f[at, j * chunk : (j + 1) * chunk]
            high = value.astype(BF16)
            cov_hi[j, at, :] = high
            cov_lo[j, at, :] = (value - high.astype(F32)).astype(BF16)
            return 0

        lax.fori_loop(0, width // strip, body, 0)

    for j in range(zs):
        cov_in[j].wait()
        split(j)

    pltpu.make_async_copy(sens_all, sens_all, sn_recv).wait()
    m0 = lax.broadcasted_iota(jnp.int32, (mg, mg), 0)
    m1 = lax.broadcasted_iota(jnp.int32, (mg, mg), 1)
    frame_of = jnp.sum(
        jnp.where(m0 == m1, frame_ref[...].astype(F32), 0.0), axis=1, keepdims=True
    )
    chosen = jnp.where(frame_of == s.astype(F32), 1.0, 0.0)
    sens_all[...] = sens_all[...] * chosen
    pltpu.make_async_copy(act_all, act_all, a_recv).wait()
    pltpu.make_async_copy(adj_all, adj_all, ad_recv).wait()
    for b in range(bl):
        w_rows[mg * b : mg * (b + 1), :] = (sens_all[...] * adj_all[b : b + 1, :]).astype(BF16)
    jac_half[...] = lax.dot_general(
        w_rows[...], act_all[...], NT, preferred_element_type=F32
    )
    swap = remote(jac_half, jac_in, sib_send.at[4], sib_recv.at[4], r, sib)
    swap.start()
    swap.wait_recv()
    whole = jac_half[...] + jac_in[...]
    jac_piece[...] = jnp.concatenate(
        [whole[mg * b : mg * (b + 1), :] for b in range(bl)], axis=1
    ).astype(BF16)
    drains.append(swap.wait_send)

    half = chips // 2

    def cast(piece, buf, stage):
        at = pl.ds(pl.multiple_of(mg * r, mg), mg)
        lanes = pl.ds(pl.multiple_of(chunk * z, chunk), chunk)
        dst = buf.at[at, lanes]
        rsem = m_recv.at[stage, z * rows + r]
        own = (x == r) & (s == 0)

        @pl.when(own)
        def _():
            pltpu.make_async_copy(piece, dst, rsem).start()

        @pl.when(jnp.logical_not(own))
        def _():
            to = 2 * lax.rem(h + s, chips) + s
            remote(piece, dst, m_send.at[stage, 0], rsem, x, to).start()

        def send(i, _):
            to = 2 * lax.rem(h + 2 * i + s, chips) + s
            remote(piece, dst, m_send.at[stage, i], rsem, x, to).start()
            return 0

        lax.fori_loop(1, half, send, 0)

        def drain():
            @pl.when(jnp.logical_not(own))
            def _():
                pltpu.make_async_copy(piece, piece, m_send.at[stage, 0]).wait()

            def step(i, _):
                pltpu.make_async_copy(piece, piece, m_send.at[stage, i]).wait()
                return 0

            lax.fori_loop(1, half, step, 0)

        drains.append(drain)

    def slot(buf, i, which):
        zz = 2 * (i // rows) + which
        p = lax.rem(i, rows)
        lanes = pl.ds(pl.multiple_of(chunk * zz, chunk), chunk)
        return buf.at[pl.ds(pl.multiple_of(mg * p, mg), mg), lanes], zz * rows + p

    def relay(buf, stage):
        def step(i, _):
            here, k = slot(buf, i, parity)
            pltpu.make_async_copy(here, here, m_recv.at[stage, k]).wait()
            remote(here, here, f_send.at[stage, i], f_recv.at[stage, k], r, sib).start()
            return 0

        lax.fori_loop(0, half, step, 0)

        def drain():
            def step2(i, _):
                here, _ = slot(buf, i, parity)
                pltpu.make_async_copy(here, here, f_send.at[stage, i]).wait()
                return 0

            lax.fori_loop(0, half, step2, 0)

        drains.append(drain)

    def relayed(buf, stage):
        def step(i, _):
            there, k = slot(buf, i, 1 - parity)
            pltpu.make_async_copy(there, there, f_recv.at[stage, k]).wait()
            return 0

        lax.fori_loop(0, half, step, 0)

    pl.semaphore_wait(row_in, rows - 1)
    cast(jac_piece, jac_all, 0)
    relay(jac_all, 0)

    def times(which):
        def step(i, _):
            zz = 2 * i + which
            jac = jac_all[:, pl.ds(pl.multiple_of(chunk * zz, chunk), chunk)]
            n_part[...] += (
                lax.dot_general(jac, cov_hi[zz], NT, preferred_element_type=F32)
                + lax.dot_general(jac, cov_lo[zz], NT, preferred_element_type=F32)
            ).reshape(rows, mg, width)
            return 0

        lax.fori_loop(0, zs // 2, step, 0)

    n_part[...] = jnp.zeros_like(n_part)
    times(parity)
    relayed(jac_all, 0)
    times(1 - parity)
    for d in range(1, rows):
        to = lax.rem(r + d, rows)
        copy = remote(n_part.at[to], n_in.at[d - 1], y_send.at[d - 1], y_recv.at[d - 1], to, c)
        copy.start()
        drains.append(copy.wait_send)
    for d in range(1, rows):
        pltpu.make_async_copy(n_in.at[d - 1], n_in.at[d - 1], y_recv.at[d - 1]).wait()
    mine_n = n_part[r]
    for d in range(1, rows):
        mine_n = mine_n + n_in[d - 1]
    n_piece[...] = mine_n.astype(BF16)
    swap_n = remote(n_piece, n_pair.at[s], sib_send.at[5], sib_recv.at[5], r, sib)
    swap_n.start()
    drains.append(swap_n.wait_send)
    n_pair[s] = n_piece[...]
    n_col[r] = n_piece[...]
    for d in range(1, rows):
        to = lax.rem(r + d, rows)
        copy = remote(n_piece, n_col.at[r], c_send.at[d - 1], c_recv.at[d - 1], to, c)
        copy.start()
        drains.append(copy.wait_send)
    swap_n.wait_recv()
    n_wide[...] = jnp.concatenate(
        [n_pair[0].astype(F32), n_pair[1].astype(F32)], axis=1
    ).astype(BF16)
    cast(n_wide, nt_ref, 1)
    owned = n_slices.shape[2]
    for t in range(rows):
        n_slices[t] = mine_n[:, t * owned : (t + 1) * owned]
    for t in range(rows):
        to = rows * jz + t
        here = (x == r) & (to == c)

        @pl.when(here)
        def _():
            pltpu.make_async_copy(n_slices.at[t], n_own.at[r], o_recv.at[r]).start()

        @pl.when(jnp.logical_not(here))
        def _():
            remote(n_slices.at[t], n_own.at[r], o_send.at[t], o_recv.at[r], x, to).start()

    relay(nt_ref, 1)

    partial = jnp.zeros((measures, measures), F32)
    for i in range(zs // 2):
        lanes = pl.ds(pl.multiple_of(chunk * (2 * i + parity), chunk), chunk)
        partial = partial + lax.dot_general(
            jac_all[:, lanes], nt_ref[:, lanes], NT, preferred_element_type=F32
        )
    top = measures // 2
    s_mine[...] = jnp.concatenate([partial[:top], partial[top:]], axis=1)
    group = 2 * rows
    for d in range(1, group):
        to = lax.rem(2 * r + s + d, group)
        copy = remote(
            s_mine, s_in.at[d - 1], s_send.at[d - 1], s_recv.at[d - 1], to // 2, 2 * h + to % 2
        )
        copy.start()
        drains.append(copy.wait_send)
    for d in range(1, group):
        pltpu.make_async_copy(s_in.at[d - 1], s_in.at[d - 1], s_recv.at[d - 1]).wait()
    packed = s_mine[...]
    for d in range(1, group):
        packed = packed + s_in[d - 1]
    innovation_cov = jnp.concatenate(
        [packed[:, :measures], packed[:, measures:]], axis=0
    )
    i0 = lax.broadcasted_iota(jnp.int32, (measures, measures), 0)
    i1 = lax.broadcasted_iota(jnp.int32, (measures, measures), 1)
    eye = jnp.where(i0 == i1, 1.0, 0.0).astype(F32)
    innovation_cov = innovation_cov + eye * noise_ref[...]
    row_sums = jnp.sum(jnp.abs(innovation_cov), axis=1, keepdims=True)
    first = 1.0 / jnp.max(row_sums, axis=0, keepdims=True)
    inverse = eye * first
    left = eye - innovation_cov * first
    for sweep in range(NS_ITERS):
        inverse = inverse + jnp.dot(inverse, left, precision=FULL, preferred_element_type=F32)
        if sweep < NS_ITERS - 1:
            left = jnp.dot(left, left, precision=FULL, preferred_element_type=F32)
    for d in range(1, rows):
        pltpu.make_async_copy(n_piece, n_piece, c_recv.at[d - 1]).wait()
    n_cols = n_col[...].reshape(measures, width).astype(F32)
    gt_ref[...] = jnp.transpose(
        jnp.dot(inverse, n_cols, precision=FULL, preferred_element_type=F32)
    ).astype(BF16)
    step_col = jnp.sum(inverse * innov_ref[...], axis=1, keepdims=True)
    for p in range(rows):
        pltpu.make_async_copy(n_own.at[p], n_own.at[p], o_recv.at[p]).wait()
    n_mine = n_own[...].reshape(measures, owned)
    wnew_ref[...] = weights_ref[...] + jnp.sum(step_col * n_mine, axis=0, keepdims=True)
    for t in range(rows):
        to = rows * jz + t

        @pl.when(jnp.logical_not((x == r) & (to == c)))
        def _():
            pltpu.make_async_copy(n_slices.at[t], n_slices.at[t], o_send.at[t]).wait()

    relayed(nt_ref, 1)
    for drain in drains:
        drain()


def update_kernel(cov_ref, nt_ref, gt_ref, out_ref):
    tile = out_ref.shape[0]
    at = pl.ds(pl.multiple_of(pl.program_id(0) * tile, tile), tile)
    out_ref[...] = cov_ref[at, :] - jnp.dot(
        gt_ref[...], nt_ref[...], preferred_element_type=F32
    )


def on_device(
    cov,
    weights,
    act,
    upstream,
    neighbors,
    types,
    type_gain,
    sens,
    frame_for_measure,
    noise_variance,
    innovation,
):
    rows = lax.axis_size("row")
    cols = lax.axis_size("col")
    per = cols // rows
    chips = cols // 2
    frames, atoms, nbr = neighbors.shape
    pair = 2 * atoms
    all_atoms = cols * atoms
    adjw, actw = upstream.shape[2], act.shape[2]
    mg = sens.shape[0]
    measures = mg * rows
    height, width = cov.shape
    zs = per // 2
    chunk = height // zs
    owned = weights.shape[0]
    bl = adjw // chips
    his = all_atoms // 128
    dma = pltpu.SemaphoreType.DMA
    vmem = pl.BlockSpec(memory_space=pltpu.VMEM)
    n_rows, gain, weights_new, block = pl.pallas_call(
        functools.partial(gain_kernel, rows, cols),
        out_shape=(
            jax.ShapeDtypeStruct((measures, height), BF16),
            jax.ShapeDtypeStruct((width, measures), BF16),
            jax.ShapeDtypeStruct((1, owned), F32),
            jax.ShapeDtypeStruct((width, height), F32),
        ),
        in_specs=[pl.BlockSpec(memory_space=pltpu.HBM)] * 11,
        out_specs=(vmem,) * 4,
        scratch_shapes=[
            pltpu.VMEM((1, owned), F32),
            pltpu.VMEM((frames, atoms, adjw), BF16),
            pltpu.VMEM(type_gain.shape, F32),
            pltpu.VMEM((1, mg), jnp.int32),
            pltpu.VMEM((1, measures), F32),
            pltpu.VMEM((1, measures), F32),
            pltpu.VMEM((zs, width, chunk), BF16),
            pltpu.VMEM((zs, width, chunk), BF16),
            pltpu.VMEM((2, atoms, nbr), jnp.int32),
            pltpu.VMEM((2, 1, atoms), jnp.int32),
            pltpu.VMEM((2, atoms, actw), BF16),
            pltpu.VMEM((2, mg, atoms), F32),
            pltpu.VMEM((his, pair, 128), F32),
            pltpu.VMEM((pair, all_atoms), BF16),
            pltpu.VMEM((all_atoms, adjw), BF16),
            pltpu.VMEM((actw, pair), BF16),
            pltpu.VMEM((actw, all_atoms), BF16),
            pltpu.VMEM((mg, pair), F32),
            pltpu.VMEM((mg, all_atoms), F32),
            pltpu.VMEM((chips, bl, pair), F32),
            pltpu.VMEM((bl, all_atoms), F32),
            pltpu.VMEM((bl * mg, all_atoms), BF16),
            pltpu.VMEM((bl * mg, actw), F32),
            pltpu.VMEM((bl * mg, actw), F32),
            pltpu.VMEM((mg, chunk), BF16),
            pltpu.VMEM((measures, height), BF16),
            pltpu.VMEM((rows, mg, width), F32),
            pltpu.VMEM((rows - 1, mg, width), F32),
            pltpu.VMEM((mg, width), BF16),
            pltpu.VMEM((2, mg, width), BF16),
            pltpu.VMEM((mg, chunk), BF16),
            pltpu.VMEM((rows, mg, width), BF16),
            pltpu.VMEM((rows, mg, owned), F32),
            pltpu.VMEM((rows, mg, owned), F32),
            pltpu.VMEM((measures // 2, 2 * measures), F32),
            pltpu.VMEM((2 * rows - 1, measures // 2, 2 * measures), F32),
            dma((10,)),
            dma((zs,)),
            pltpu.SemaphoreType.REGULAR,
            dma((6,)),
            dma((6,)),
            dma,
            dma,
            dma,
            dma,
            dma,
            dma,
            dma,
            dma,
            dma((2, chips // 2)),
            dma((2, zs * rows)),
            dma((2, chips // 2)),
            dma((2, zs * rows)),
            dma((rows - 1,)),
            dma((rows - 1,)),
            dma((rows - 1,)),
            dma((rows - 1,)),
            dma((rows,)),
            dma((rows,)),
            dma((2 * rows - 1,)),
            dma((2 * rows - 1,)),
        ],
        compiler_params=pltpu.CompilerParams(
            collective_id=0, has_side_effects=True, vmem_limit_bytes=40 * 2**20
        ),
        name="gain",
    )(
        cov.T,
        weights.reshape(1, owned),
        act,
        upstream,
        neighbors,
        types.reshape(frames, 1, atoms),
        type_gain,
        sens,
        frame_for_measure.reshape(1, mg),
        noise_variance.reshape(1, measures),
        innovation.reshape(1, measures),
    )
    tile = width // per
    cov_new = pl.pallas_call(
        update_kernel,
        grid=(per,),
        in_specs=[
            pl.BlockSpec(memory_space=pltpu.VMEM),
            pl.BlockSpec((measures, height), lambda j: (0, 0)),
            pl.BlockSpec((tile, measures), lambda j: (j, 0)),
        ],
        out_specs=pl.BlockSpec((tile, height), lambda j: (j, 0)),
        out_shape=jax.ShapeDtypeStruct((width, height), F32),
        compiler_params=pltpu.CompilerParams(vmem_limit_bytes=32 * 2**20),
        name="update",
    )(block, n_rows, gain)
    return weights_new.reshape(owned), cov_new.T


def solution(mesh):
    return jax.shard_map(
        on_device,
        mesh=mesh,
        in_specs=(
            P("row", "col"),
            P(("row", "col")),
            P("row", "col", None),
            P("row", "col", None),
            P("row", "col", None),
            P("row", "col"),
            P(),
            P("row", "col"),
            P("row"),
            P(),
            P(),
        ),
        out_specs=(P(("row", "col")), P("row", "col")),
        check_vma=False,
    )
```

```python
import functools
import math

import jax
import jax.numpy as jnp
from jax import lax
from jax.experimental import pallas as pl
from jax.experimental.pallas import tpu as pltpu
from jax.sharding import PartitionSpec as P

NS_ITERS = 5
MESH = pl.DeviceIdType.MESH
FULL = lax.Precision.HIGHEST
F32 = jnp.float32
BF16 = jnp.bfloat16
NT = (((1,), (1,)), ((), ()))


def gain_kernel(
    rows,
    cols,
    cov_hbm,
    weights_hbm,
    act_hbm,
    up_hbm,
    nb_hbm,
    types_hbm,
    tgain_hbm,
    sens_hbm,
    frame_hbm,
    noise_hbm,
    innov_hbm,
    nt_ref,
    gt_ref,
    wnew_ref,
    cov_f,
    weights_ref,
    up_ref,
    tgain_ref,
    frame_ref,
    noise_ref,
    innov_ref,
    cov_hi,
    cov_lo,
    nb_all,
    kind_all,
    act_pair,
    sens_pair,
    counts,
    counts_b,
    up_all,
    act_all,
    sens_all,
    adj_t,
    adj_all,
    w_rows,
    jac_half,
    jac_in,
    jac_piece,
    jac_all,
    n_part,
    n_in,
    n_piece,
    n_pair,
    n_wide,
    n_col,
    n_slices,
    n_own,
    jac_own,
    jac_col,
    t_mine,
    t_in,
    t_rows,
    load_sem,
    cov_sem,
    row_in,
    sib_send,
    sib_recv,
    u_send,
    u_recv,
    a_first,
    sn_first,
    a_send,
    a_recv,
    sn_send,
    sn_recv,
    ad_send,
    ad_recv,
    m_send,
    m_recv,
    f_send,
    f_recv,
    y_send,
    y_recv,
    c_send,
    c_recv,
    o_send,
    o_recv,
    j_send,
    j_recv,
    t_send,
    t_recv,
    q_send,
    q_recv,
):
    r = lax.axis_index("row")
    c = lax.axis_index("col")
    chips = cols // 2
    per = cols // rows
    zs = per // 2
    h = c // 2
    s = c % 2
    x = c // per
    z = (c % per) // 2
    jz = c % per
    parity = lax.rem(h + s, 2)
    drains = []
    other = 1 - s
    sib = c + 1 - 2 * s
    atoms = nb_hbm.shape[1]
    pair = 2 * atoms
    nbr = nb_hbm.shape[2]
    adjw = up_hbm.shape[2]
    actw = act_hbm.shape[2]
    mg = sens_hbm.shape[0]
    measures = mg * rows
    width, chunk = cov_hi.shape[1:]
    bl = adjw // chips

    def remote(src, dst, ssem, rsem, tr, tc):
        return pltpu.make_async_remote_copy(
            src_ref=src,
            dst_ref=dst,
            send_sem=ssem,
            recv_sem=rsem,
            device_id=(tr, tc),
            device_id_type=MESH,
        )

    cov_in = [
        pltpu.make_async_copy(
            cov_hbm.at[:, pl.ds(j * chunk, chunk)],
            cov_f.at[:, pl.ds(j * chunk, chunk)],
            cov_sem.at[j],
        )
        for j in range(zs)
    ]

    loads = [
        pltpu.make_async_copy(src, dst, load_sem.at[i])
        for i, (src, dst) in enumerate(
            (
                (up_hbm, up_ref),
                (nb_hbm.at[s], nb_all.at[s]),
                (act_hbm.at[s], act_pair.at[s]),
                (sens_hbm, sens_pair.at[s]),
                (types_hbm.at[s], kind_all.at[s]),
                (tgain_hbm, tgain_ref),
                (frame_hbm, frame_ref),
                (noise_hbm, noise_ref),
                (innov_hbm, innov_ref),
                (weights_hbm, weights_ref),
            )
        )
    ]
    for load in loads:
        load.start()
    barrier = pltpu.get_barrier_semaphore()

    def greet(k, _):
        to = lax.rem(c + k, cols)
        pl.semaphore_signal(barrier, inc=1, device_id=(r, to), device_id_type=MESH)
        return 0

    lax.fori_loop(1, cols, greet, 0)
    for d in range(1, rows):
        to = lax.rem(r + d, rows)
        pl.semaphore_signal(barrier, inc=1, device_id=(to, c), device_id_type=MESH)
    loads[0].wait()
    pl.semaphore_wait(barrier, cols - 1 + rows - 1)

    sib_copies = [
        remote(nb_hbm.at[other], nb_all.at[s], sib_send.at[0], sib_recv.at[0], r, sib),
        remote(act_hbm.at[other], act_pair.at[s], sib_send.at[1], sib_recv.at[1], r, sib),
        remote(sens_hbm, sens_pair.at[s], sib_send.at[2], sib_recv.at[2], r, sib),
        remote(types_hbm.at[other], kind_all.at[s], sib_send.at[3], sib_recv.at[3], r, sib),
    ]
    sib_copies[0].start()
    mine = pl.ds(pl.multiple_of(c * atoms, atoms), atoms)
    own_up = pltpu.make_async_copy(up_ref.at[s], up_all.at[mine], u_recv)
    own_up.start()
    remote(up_ref.at[other], up_all.at[mine], u_send, u_recv, r, sib).start()

    def send_up(k, _):
        to = lax.rem(h + k, chips)
        for f in range(2):
            remote(up_ref.at[f], up_all.at[mine], u_send, u_recv, r, 2 * to + f).start()
        return 0

    lax.fori_loop(1, chips, send_up, 0)
    sib_copies[1].start()
    sib_copies[2].start()
    sib_copies[3].start()
    for copy in cov_in:
        copy.start()

    for d in range(1, rows):
        to = lax.rem(r + d, rows)
        pl.semaphore_signal(row_in, inc=1, device_id=(to, c), device_id_type=MESH)
    for load in loads[1:]:
        load.wait()
    sib_copies[1].wait_recv()
    sib_copies[2].wait_recv()
    def lanes_of(chip):
        return pl.ds(pl.multiple_of(chip * pair, pair), pair)

    lanes_mine = lanes_of(h)
    act_all[:, lanes_mine] = jnp.transpose(
        act_pair[...].reshape(pair, actw).astype(F32)
    ).astype(BF16)
    sens_all[:, lanes_mine] = jnp.concatenate([sens_pair[0], sens_pair[1]], axis=1)

    def along(axis_is_z, d):
        in_z = x * zs + lax.rem(z + d + zs, zs)
        in_x = lax.rem(x + d + zs, zs) * zs + z
        return jnp.where(axis_is_z, in_z, in_x)

    first_z = s == 0
    second_z = s == 1
    tree = ((act_all, a_first, a_send, a_recv), (sens_all, sn_first, sn_send, sn_recv))
    for d in range(1, zs):
        to = 2 * along(first_z, d) + s
        for buf, first, send, recv in tree:
            part = buf.at[:, lanes_mine]
            remote(part, part, send, first.at[d - 1], r, to).start()

    def spread_line(e):
        lanes = lanes_of(along(first_z, -e))
        for buf, first, send, recv in tree:
            part = buf.at[:, lanes]
            if e > 0:
                pltpu.make_async_copy(part, part, first.at[e - 1]).wait()
            for d in range(1, zs):
                to = 2 * along(second_z, d) + s
                remote(part, part, send, recv, r, to).start()

    spread_line(0)

    def drain_first():
        for copy in sib_copies:
            copy.wait_send()
        sent_up = up_all.at[pl.ds(0, (2 * chips - 1) * atoms)]
        pltpu.make_async_copy(sent_up, sent_up, u_send).wait()
        for buf, _, send, _ in tree:
            part = buf.at[:, pl.ds(0, (chips - 1) * pair)]
            pltpu.make_async_copy(part, part, send).wait()

    drains.append(drain_first)

    sib_copies[0].wait_recv()
    his = counts.shape[0]
    iota_lo = lax.broadcasted_iota(jnp.int32, (128, nbr), 0)
    iota_hi = lax.broadcasted_iota(jnp.int32, (his, nbr), 0)
    unroll = 8

    def count(step, _):
        t = step // (atoms // unroll)
        base = pl.multiple_of(lax.rem(step, atoms // unroll) * unroll, unroll)
        block = nb_all[t, pl.ds(base, unroll), :]
        for u in range(unroll):
            idx = block[u : u + 1, :]
            low = jnp.where((idx & 127) == iota_lo, 1.0, 0.0).astype(BF16)
            high = jnp.where((idx >> 7) == iota_hi, 1.0, 0.0).astype(BF16)
            got = lax.dot_general(high, low, NT, preferred_element_type=F32)
            row = t * atoms + base + u
            counts[:, pl.ds(row, 1), :] = got.reshape(his, 1, 128)
        return 0

    lax.fori_loop(0, pair // unroll, count, 0)
    for k in range(his):
        counts_b[:, k * 128 : (k + 1) * 128] = counts[k].astype(BF16)

    for e in range(1, zs):
        spread_line(e)

    pltpu.make_async_copy(up_all, up_all, u_recv).wait()
    neighbor_sum = jnp.dot(
        counts_b[...], up_all[...], preferred_element_type=F32
    ) * (1.0 / math.sqrt(nbr))
    own = up_all[pl.ds(pl.multiple_of(h * pair, pair), pair), :].astype(F32)
    sib_copies[3].wait_recv()
    kinds = jnp.concatenate([kind_all[0], kind_all[1]], axis=1)
    kinds = jnp.transpose(jnp.broadcast_to(kinds, (adjw, pair)))
    type_scale = jnp.zeros((pair, adjw), F32)
    for kind in range(tgain_ref.shape[0]):
        type_scale = jnp.where(kinds == kind, tgain_ref[kind : kind + 1, :], type_scale)
    adj_t[...] = jnp.transpose(type_scale * (own + neighbor_sum)).reshape(chips, bl, pair)
    own_adj = pltpu.make_async_copy(adj_t.at[h], adj_all.at[:, lanes_mine], ad_recv)
    own_adj.start()

    def send_adj(k, _):
        to = lax.rem(h + k, chips)
        remote(adj_t.at[to], adj_all.at[:, lanes_mine], ad_send, ad_recv, r, 2 * to + s).start()
        return 0

    lax.fori_loop(1, chips, send_adj, 0)

    def drain_adj():
        part = adj_all.at[:, pl.ds(0, (chips - 1) * pair)]
        pltpu.make_async_copy(part, part, ad_send).wait()

    drains.append(drain_adj)

    strip = 64

    def split(j):
        def body(i, _):
            at = pl.ds(pl.multiple_of(i * strip, strip), strip)
            value = cov_f[at, j * chunk : (j + 1) * chunk]
            high = value.astype(BF16)
            cov_hi[j, at, :] = high
            cov_lo[j, at, :] = (value - high.astype(F32)).astype(BF16)
            return 0

        lax.fori_loop(0, width // strip, body, 0)

    for j in range(zs):
        cov_in[j].wait()
        split(j)

    for buf, _, _, recv in tree[::-1]:
        part = buf.at[:, pl.ds(0, (chips - zs) * pair)]
        pltpu.make_async_copy(part, part, recv).wait()
    m0 = lax.broadcasted_iota(jnp.int32, (mg, mg), 0)
    m1 = lax.broadcasted_iota(jnp.int32, (mg, mg), 1)
    frame_of = jnp.sum(
        jnp.where(m0 == m1, frame_ref[...].astype(F32), 0.0), axis=1, keepdims=True
    )
    chosen = jnp.where(frame_of == s.astype(F32), 1.0, 0.0)
    sens_own = sens_all[...] * chosen
    pltpu.make_async_copy(adj_all, adj_all, ad_recv).wait()
    for b in range(bl):
        w_rows[mg * b : mg * (b + 1), :] = (sens_own * adj_all[b : b + 1, :]).astype(BF16)
    jac_half[...] = lax.dot_general(
        w_rows[...], act_all[...], NT, preferred_element_type=F32
    )
    swap = remote(jac_half, jac_in, sib_send.at[4], sib_recv.at[4], r, sib)
    swap.start()
    swap.wait_recv()
    whole = jac_half[...] + jac_in[...]
    jac_piece[...] = jnp.concatenate(
        [whole[mg * b : mg * (b + 1), :] for b in range(bl)], axis=1
    ).astype(BF16)
    drains.append(swap.wait_send)
    rows_half = bl * mg // 2
    own_half = jnp.where(s == 0, whole[:rows_half], whole[rows_half:])
    jac_own[...] = jnp.concatenate(
        [own_half[mg * b : mg * (b + 1), :] for b in range(bl // 2)], axis=1
    ).astype(BF16)
    jac_col[r] = jac_own[...]

    half = chips // 2

    def cast(piece, buf, stage):
        at = pl.ds(pl.multiple_of(mg * r, mg), mg)
        lanes = pl.ds(pl.multiple_of(chunk * z, chunk), chunk)
        dst = buf.at[at, lanes]
        rsem = m_recv.at[stage, z * rows + r]
        own = (x == r) & (s == 0)

        @pl.when(own)
        def _():
            pltpu.make_async_copy(piece, dst, rsem).start()

        @pl.when(jnp.logical_not(own))
        def _():
            to = 2 * lax.rem(h + s, chips) + s
            remote(piece, dst, m_send.at[stage, 0], rsem, x, to).start()

        def send(i, _):
            to = 2 * lax.rem(h + 2 * i + s, chips) + s
            remote(piece, dst, m_send.at[stage, i], rsem, x, to).start()
            return 0

        lax.fori_loop(1, half, send, 0)

        def drain():
            @pl.when(jnp.logical_not(own))
            def _():
                pltpu.make_async_copy(piece, piece, m_send.at[stage, 0]).wait()

            def step(i, _):
                pltpu.make_async_copy(piece, piece, m_send.at[stage, i]).wait()
                return 0

            lax.fori_loop(1, half, step, 0)

        drains.append(drain)

    def slot(buf, i, which):
        zz = 2 * (i // rows) + which
        p = lax.rem(i, rows)
        lanes = pl.ds(pl.multiple_of(chunk * zz, chunk), chunk)
        return buf.at[pl.ds(pl.multiple_of(mg * p, mg), mg), lanes], zz * rows + p

    def relay(buf, stage):
        def step(i, _):
            here, k = slot(buf, i, parity)
            pltpu.make_async_copy(here, here, m_recv.at[stage, k]).wait()
            remote(here, here, f_send.at[stage, i], f_recv.at[stage, k], r, sib).start()
            return 0

        lax.fori_loop(0, half, step, 0)

        def drain():
            def step2(i, _):
                here, _ = slot(buf, i, parity)
                pltpu.make_async_copy(here, here, f_send.at[stage, i]).wait()
                return 0

            lax.fori_loop(0, half, step2, 0)

        drains.append(drain)

    def relayed(buf, stage):
        def step(i, _):
            there, k = slot(buf, i, 1 - parity)
            pltpu.make_async_copy(there, there, f_recv.at[stage, k]).wait()
            return 0

        lax.fori_loop(0, half, step, 0)

    pl.semaphore_wait(row_in, rows - 1)
    cast(jac_piece, jac_all, 0)
    for d in range(1, rows):
        to = lax.rem(r + d, rows)
        copy = remote(jac_own, jac_col.at[r], j_send.at[d - 1], j_recv.at[d - 1], to, c)
        copy.start()
        drains.append(copy.wait_send)
    relay(jac_all, 0)

    def times(which):
        def step(i, _):
            zz = 2 * i + which
            jac = jac_all[:, pl.ds(pl.multiple_of(chunk * zz, chunk), chunk)]
            n_part[...] += (
                lax.dot_general(jac, cov_hi[zz], NT, preferred_element_type=F32)
                + lax.dot_general(jac, cov_lo[zz], NT, preferred_element_type=F32)
            ).reshape(rows, mg, width)
            return 0

        lax.fori_loop(0, zs // 2, step, 0)

    n_part[...] = jnp.zeros_like(n_part)
    times(parity)
    relayed(jac_all, 0)
    times(1 - parity)
    for d in range(1, rows):
        to = lax.rem(r + d, rows)
        copy = remote(n_part.at[to], n_in.at[d - 1], y_send.at[d - 1], y_recv.at[d - 1], to, c)
        copy.start()
        drains.append(copy.wait_send)
    for d in range(1, rows):
        pltpu.make_async_copy(n_in.at[d - 1], n_in.at[d - 1], y_recv.at[d - 1]).wait()
    mine_n = n_part[r]
    for d in range(1, rows):
        mine_n = mine_n + n_in[d - 1]
    n_piece[...] = mine_n.astype(BF16)
    swap_n = remote(n_piece, n_pair.at[s], sib_send.at[5], sib_recv.at[5], r, sib)
    swap_n.start()
    drains.append(swap_n.wait_send)
    n_pair[s] = n_piece[...]
    n_col[r] = n_piece[...]
    for d in range(1, rows):
        to = lax.rem(r + d, rows)
        copy = remote(n_piece, n_col.at[r], c_send.at[d - 1], c_recv.at[d - 1], to, c)
        copy.start()
        drains.append(copy.wait_send)
    for d in range(1, rows):
        pltpu.make_async_copy(jac_own, jac_own, j_recv.at[d - 1]).wait()
    n_low = (mine_n - n_piece[...].astype(F32)).astype(BF16)
    jac_here = jac_col[...].reshape(measures, width)
    part = lax.dot_general(
        n_piece[...], jac_here, NT, preferred_element_type=F32
    ) + lax.dot_general(n_low, jac_here, NT, preferred_element_type=F32)
    t_mine[...] = jnp.concatenate([part[: mg // 2], part[mg // 2 :]], axis=1)
    t_in[c] = t_mine[...]

    def send_part(k, _):
        to = lax.rem(c + k, cols)
        remote(t_mine, t_in.at[c], t_send, t_recv, r, to).start()
        return 0

    lax.fori_loop(1, cols, send_part, 0)

    def drain_part():
        sent = t_in.at[pl.ds(0, cols - 1)]
        pltpu.make_async_copy(sent, sent, t_send).wait()

    drains.append(drain_part)
    swap_n.wait_recv()
    n_wide[...] = jnp.concatenate(
        [n_pair[0].astype(F32), n_pair[1].astype(F32)], axis=1
    ).astype(BF16)
    cast(n_wide, nt_ref, 1)
    owned = n_slices.shape[2]
    for t in range(rows):
        n_slices[t] = mine_n[:, t * owned : (t + 1) * owned]
    for t in range(rows):
        to = rows * jz + t
        here = (x == r) & (to == c)

        @pl.when(here)
        def _():
            pltpu.make_async_copy(n_slices.at[t], n_own.at[r], o_recv.at[r]).start()

        @pl.when(jnp.logical_not(here))
        def _():
            remote(n_slices.at[t], n_own.at[r], o_send.at[t], o_recv.at[r], x, to).start()

    arrived = t_in.at[pl.ds(0, cols - 1)]
    pltpu.make_async_copy(arrived, arrived, t_recv).wait()
    t_rows[r] = jnp.sum(t_in[...], axis=0)
    for d in range(1, rows):
        to = lax.rem(r + d, rows)
        copy = remote(t_rows.at[r], t_rows.at[r], q_send.at[d - 1], q_recv.at[d - 1], to, c)
        copy.start()
        drains.append(copy.wait_send)
    relay(nt_ref, 1)
    for d in range(1, rows):
        pltpu.make_async_copy(t_rows.at[0], t_rows.at[0], q_recv.at[d - 1]).wait()
    pieces = []
    for q in range(rows):
        packed = t_rows[q]
        pieces += [packed[:, :measures], packed[:, measures:]]
    innovation_cov = jnp.concatenate(pieces, axis=0)
    i0 = lax.broadcasted_iota(jnp.int32, (measures, measures), 0)
    i1 = lax.broadcasted_iota(jnp.int32, (measures, measures), 1)
    eye = jnp.where(i0 == i1, 1.0, 0.0).astype(F32)
    innovation_cov = innovation_cov + eye * noise_ref[...]
    row_sums = jnp.sum(jnp.abs(innovation_cov), axis=1, keepdims=True)
    first = 1.0 / jnp.max(row_sums, axis=0, keepdims=True)
    inverse = eye * first
    left = eye - innovation_cov * first
    for sweep in range(NS_ITERS):
        inverse = inverse + jnp.dot(inverse, left, precision=FULL, preferred_element_type=F32)
        if sweep < NS_ITERS - 1:
            left = jnp.dot(left, left, precision=FULL, preferred_element_type=F32)
    for d in range(1, rows):
        pltpu.make_async_copy(n_piece, n_piece, c_recv.at[d - 1]).wait()
    n_cols = n_col[...].reshape(measures, width).astype(F32)
    gt_ref[...] = jnp.transpose(
        jnp.dot(inverse, n_cols, precision=FULL, preferred_element_type=F32)
    ).astype(BF16)
    step_col = jnp.sum(inverse * innov_ref[...], axis=1, keepdims=True)
    for p in range(rows):
        pltpu.make_async_copy(n_own.at[p], n_own.at[p], o_recv.at[p]).wait()
    n_mine = n_own[...].reshape(measures, owned)
    wnew_ref[...] = weights_ref[...] + jnp.sum(step_col * n_mine, axis=0, keepdims=True)
    for t in range(rows):
        to = rows * jz + t

        @pl.when(jnp.logical_not((x == r) & (to == c)))
        def _():
            pltpu.make_async_copy(n_slices.at[t], n_slices.at[t], o_send.at[t]).wait()

    relayed(nt_ref, 1)
    for drain in drains:
        drain()


def update_kernel(cov_ref, nt_ref, gt_ref, out_ref):
    out_ref[...] = cov_ref[...] - jnp.dot(
        gt_ref[...], nt_ref[...], preferred_element_type=F32
    )


def on_device(
    cov,
    weights,
    act,
    upstream,
    neighbors,
    types,
    type_gain,
    sens,
    frame_for_measure,
    noise_variance,
    innovation,
):
    rows = lax.axis_size("row")
    cols = lax.axis_size("col")
    per = cols // rows
    chips = cols // 2
    frames, atoms, nbr = neighbors.shape
    pair = 2 * atoms
    all_atoms = cols * atoms
    adjw, actw = upstream.shape[2], act.shape[2]
    mg = sens.shape[0]
    measures = mg * rows
    height, width = cov.shape
    zs = per // 2
    chunk = height // zs
    owned = weights.shape[0]
    bl = adjw // chips
    his = all_atoms // 128
    dma = pltpu.SemaphoreType.DMA
    vmem = pl.BlockSpec(memory_space=pltpu.VMEM)
    n_rows, gain, weights_new, block = pl.pallas_call(
        functools.partial(gain_kernel, rows, cols),
        out_shape=(
            jax.ShapeDtypeStruct((measures, height), BF16),
            jax.ShapeDtypeStruct((width, measures), BF16),
            jax.ShapeDtypeStruct((1, owned), F32),
            jax.ShapeDtypeStruct((width, height), F32),
        ),
        in_specs=[pl.BlockSpec(memory_space=pltpu.HBM)] * 11,
        out_specs=(vmem,) * 4,
        scratch_shapes=[
            pltpu.VMEM((1, owned), F32),
            pltpu.VMEM((frames, atoms, adjw), BF16),
            pltpu.VMEM(type_gain.shape, F32),
            pltpu.VMEM((1, mg), jnp.int32),
            pltpu.VMEM((1, measures), F32),
            pltpu.VMEM((1, measures), F32),
            pltpu.VMEM((zs, width, chunk), BF16),
            pltpu.VMEM((zs, width, chunk), BF16),
            pltpu.VMEM((2, atoms, nbr), jnp.int32),
            pltpu.VMEM((2, 1, atoms), jnp.int32),
            pltpu.VMEM((2, atoms, actw), BF16),
            pltpu.VMEM((2, mg, atoms), F32),
            pltpu.VMEM((his, pair, 128), F32),
            pltpu.VMEM((pair, all_atoms), BF16),
            pltpu.VMEM((all_atoms, adjw), BF16),
            pltpu.VMEM((actw, all_atoms), BF16),
            pltpu.VMEM((mg, all_atoms), F32),
            pltpu.VMEM((chips, bl, pair), F32),
            pltpu.VMEM((bl, all_atoms), F32),
            pltpu.VMEM((bl * mg, all_atoms), BF16),
            pltpu.VMEM((bl * mg, actw), F32),
            pltpu.VMEM((bl * mg, actw), F32),
            pltpu.VMEM((mg, chunk), BF16),
            pltpu.VMEM((measures, height), BF16),
            pltpu.VMEM((rows, mg, width), F32),
            pltpu.VMEM((rows - 1, mg, width), F32),
            pltpu.VMEM((mg, width), BF16),
            pltpu.VMEM((2, mg, width), BF16),
            pltpu.VMEM((mg, chunk), BF16),
            pltpu.VMEM((rows, mg, width), BF16),
            pltpu.VMEM((rows, mg, owned), F32),
            pltpu.VMEM((rows, mg, owned), F32),
            pltpu.VMEM((mg, width), BF16),
            pltpu.VMEM((rows, mg, width), BF16),
            pltpu.VMEM((mg // 2, 2 * measures), F32),
            pltpu.VMEM((cols, mg // 2, 2 * measures), F32),
            pltpu.VMEM((rows, mg // 2, 2 * measures), F32),
            dma((10,)),
            dma((zs,)),
            pltpu.SemaphoreType.REGULAR,
            dma((6,)),
            dma((6,)),
            dma,
            dma,
            dma((zs - 1,)),
            dma((zs - 1,)),
            dma,
            dma,
            dma,
            dma,
            dma,
            dma,
            dma((2, chips // 2)),
            dma((2, zs * rows)),
            dma((2, chips // 2)),
            dma((2, zs * rows)),
            dma((rows - 1,)),
            dma((rows - 1,)),
            dma((rows - 1,)),
            dma((rows - 1,)),
            dma((rows,)),
            dma((rows,)),
            dma((rows - 1,)),
            dma((rows - 1,)),
            dma,
            dma,
            dma((rows - 1,)),
            dma((rows - 1,)),
        ],
        compiler_params=pltpu.CompilerParams(
            collective_id=0, has_side_effects=True, vmem_limit_bytes=40 * 2**20
        ),
        name="gain",
    )(
        *(
            pltpu.with_memory_space_constraint(array, pltpu.HBM)
            for array in (
                cov.T,
                weights.reshape(1, owned),
                act,
                upstream,
                neighbors,
                types.reshape(frames, 1, atoms),
                type_gain,
                sens,
                frame_for_measure.reshape(1, mg),
                noise_variance.reshape(1, measures),
                innovation.reshape(1, measures),
            )
        )
    )
    strip = height // 9
    cov_new = pl.pallas_call(
        update_kernel,
        grid=(9,),
        in_specs=[
            pl.BlockSpec((width, strip), lambda j: (0, j)),
            pl.BlockSpec((measures, strip), lambda j: (0, j)),
            pl.BlockSpec((width, measures), lambda j: (0, 0)),
        ],
        out_specs=pl.BlockSpec((width, strip), lambda j: (0, j)),
        out_shape=jax.ShapeDtypeStruct((width, height), F32),
        compiler_params=pltpu.CompilerParams(vmem_limit_bytes=32 * 2**20),
        name="update",
    )(block, n_rows, gain)
    return weights_new.reshape(owned), cov_new.T


def solution(mesh):
    return jax.shard_map(
        on_device,
        mesh=mesh,
        in_specs=(
            P("row", "col"),
            P(("row", "col")),
            P("row", "col", None),
            P("row", "col", None),
            P("row", "col", None),
            P("row", "col"),
            P(),
            P("row", "col"),
            P("row"),
            P(),
            P(),
        ),
        out_specs=(P(("row", "col")), P("row", "col")),
        check_vma=False,
    )
```

```python
import functools
import math

import jax
import jax.numpy as jnp
from jax import lax
from jax.experimental import pallas as pl
from jax.experimental.pallas import tpu as pltpu
from jax.sharding import PartitionSpec as P

NS_ITERS = 5
MESH = pl.DeviceIdType.MESH
FULL = lax.Precision.HIGHEST
F32 = jnp.float32
BF16 = jnp.bfloat16
NT = (((1,), (1,)), ((), ()))


def gain_kernel(
    rows,
    cols,
    cov_hbm,
    weights_hbm,
    act_hbm,
    up_hbm,
    nb_hbm,
    types_hbm,
    tgain_hbm,
    sens_hbm,
    frame_hbm,
    noise_hbm,
    innov_hbm,
    nt_ref,
    gt_ref,
    wnew_ref,
    cov_f,
    weights_ref,
    tgain_ref,
    frame_ref,
    noise_ref,
    innov_ref,
    cov_hi,
    cov_lo,
    nb_all,
    kind_all,
    act_pair,
    sens_pair,
    counts,
    counts_b,
    up_all,
    act_all,
    sens_all,
    adj_t,
    adj_all,
    w_rows,
    jac_half,
    jac_in,
    jac_piece,
    jac_all,
    n_part,
    n_in,
    n_piece,
    n_pair,
    n_wide,
    n_col,
    n_slices,
    n_own,
    jac_own,
    jac_col,
    t_mine,
    t_in,
    t_rows,
    load_sem,
    cov_sem,
    row_in,
    sib_send,
    sib_recv,
    u_first,
    u_send,
    u_recv,
    a_first,
    sn_first,
    a_send,
    a_recv,
    sn_send,
    sn_recv,
    ad_send,
    ad_recv,
    m_send,
    m_recv,
    f_send,
    f_recv,
    y_send,
    y_recv,
    c_send,
    c_recv,
    o_send,
    o_recv,
    j_send,
    j_recv,
    t_send,
    t_recv,
    q_send,
    q_recv,
):
    r = lax.axis_index("row")
    c = lax.axis_index("col")
    chips = cols // 2
    per = cols // rows
    zs = per // 2
    h = c // 2
    s = c % 2
    x = c // per
    z = (c % per) // 2
    jz = c % per
    parity = lax.rem(h + s, 2)
    drains = []
    other = 1 - s
    sib = c + 1 - 2 * s
    atoms = nb_hbm.shape[1]
    pair = 2 * atoms
    nbr = nb_hbm.shape[2]
    adjw = up_hbm.shape[2]
    actw = act_hbm.shape[2]
    mg = sens_hbm.shape[0]
    measures = mg * rows
    width, chunk = cov_hi.shape[1:]
    bl = adjw // chips

    def remote(src, dst, ssem, rsem, tr, tc):
        return pltpu.make_async_remote_copy(
            src_ref=src,
            dst_ref=dst,
            send_sem=ssem,
            recv_sem=rsem,
            device_id=(tr, tc),
            device_id_type=MESH,
        )

    cov_in = [
        pltpu.make_async_copy(
            cov_hbm.at[:, pl.ds(j * chunk, chunk)],
            cov_f.at[:, pl.ds(j * chunk, chunk)],
            cov_sem.at[j],
        )
        for j in range(zs)
    ]

    mine = pl.ds(pl.multiple_of(c * atoms, atoms), atoms)
    loads = [
        pltpu.make_async_copy(src, dst, load_sem.at[i])
        for i, (src, dst) in enumerate(
            (
                (up_hbm.at[s], up_all.at[mine]),
                (nb_hbm.at[s], nb_all.at[s]),
                (act_hbm.at[s], act_pair.at[s]),
                (sens_hbm, sens_pair.at[s]),
                (types_hbm.at[s], kind_all.at[s]),
                (tgain_hbm, tgain_ref),
                (frame_hbm, frame_ref),
                (noise_hbm, noise_ref),
                (innov_hbm, innov_ref),
                (weights_hbm, weights_ref),
            )
        )
    ]
    barrier = pltpu.get_barrier_semaphore()

    def along(in_z, d):
        z_line = x * zs + lax.rem(z + d + zs, zs)
        x_line = lax.rem(x + d + zs, zs) * zs + z
        return jnp.where(in_z, z_line, x_line)

    line_mates = [(r, sib)]
    for d in range(1, zs):
        line_mates += [(r, 2 * along(True, d) + s), (r, 2 * along(False, d) + s)]
    for d in range(1, rows):
        line_mates.append((lax.rem(r + d, rows), c))
    for mate in line_mates:
        pl.semaphore_signal(barrier, inc=1, device_id=mate, device_id_type=MESH)
    for load in loads + cov_in:
        load.start()
    pl.semaphore_wait(barrier, len(line_mates))

    sib_copies = [
        remote(nb_hbm.at[other], nb_all.at[s], sib_send.at[0], sib_recv.at[0], r, sib),
        remote(act_hbm.at[other], act_pair.at[s], sib_send.at[1], sib_recv.at[1], r, sib),
        remote(sens_hbm, sens_pair.at[s], sib_send.at[2], sib_recv.at[2], r, sib),
        remote(types_hbm.at[other], kind_all.at[s], sib_send.at[3], sib_recv.at[3], r, sib),
    ]
    sib_up = remote(up_hbm.at[other], up_all.at[mine], sib_send.at[6], sib_recv.at[6], r, sib)
    sib_up.start()
    for copy in sib_copies:
        copy.start()

    def lanes_of(chip):
        return pl.ds(pl.multiple_of(chip * pair, pair), pair)

    lanes_mine = lanes_of(h)
    begin_z = s == 0
    then_z = s == 1
    up_tree = (lambda chip: up_all.at[lanes_of(chip)], u_first, u_send, u_recv)
    act_tree = (lambda chip: act_all.at[:, lanes_of(chip)], a_first, a_send, a_recv)
    sens_tree = (lambda chip: sens_all.at[:, lanes_of(chip)], sn_first, sn_send, sn_recv)

    def begin(tree):
        block, first, send, recv = tree
        part = block(h)
        for d in range(1, zs):
            remote(part, part, send, first.at[d - 1], r, 2 * along(begin_z, d) + s).start()

    def spread_line(tree, e):
        block, first, send, recv = tree
        part = block(along(begin_z, -e))
        if e > 0:
            pltpu.make_async_copy(part, part, first.at[e - 1]).wait()
        for d in range(1, zs):
            remote(part, part, send, recv, r, 2 * along(then_z, d) + s).start()

    loads[0].wait()
    sib_up.wait_recv()
    begin(up_tree)
    spread_line(up_tree, 0)
    for load in loads[1:]:
        load.wait()
    sib_copies[1].wait_recv()
    sib_copies[2].wait_recv()
    act_all[:, lanes_mine] = jnp.transpose(
        act_pair[...].reshape(pair, actw).astype(F32)
    ).astype(BF16)
    sens_all[:, lanes_mine] = jnp.concatenate([sens_pair[0], sens_pair[1]], axis=1)
    for e in range(1, zs):
        spread_line(up_tree, e)
    for tree in (act_tree, sens_tree):
        begin(tree)
        spread_line(tree, 0)

    def bulk(count):
        blocks = pl.ds(0, count * pair)
        return ((up_all.at[blocks], u_send, u_recv),) + tuple(
            (buf.at[:, blocks], send, recv)
            for buf, send, recv in ((sens_all, sn_send, sn_recv), (act_all, a_send, a_recv))
        )

    def drain_first():
        for copy in [sib_up, *sib_copies]:
            copy.wait_send()
        for part, send, _ in bulk(chips - 1):
            pltpu.make_async_copy(part, part, send).wait()

    drains.append(drain_first)

    sib_copies[0].wait_recv()
    his = counts.shape[0]
    iota_lo = lax.broadcasted_iota(jnp.int32, (128, nbr), 0)
    iota_hi = lax.broadcasted_iota(jnp.int32, (his, nbr), 0)
    unroll = 8

    def count(step, _):
        t = step // (atoms // unroll)
        base = pl.multiple_of(lax.rem(step, atoms // unroll) * unroll, unroll)
        block = nb_all[t, pl.ds(base, unroll), :]
        for u in range(unroll):
            idx = block[u : u + 1, :]
            low = jnp.where((idx & 127) == iota_lo, 1.0, 0.0).astype(BF16)
            high = jnp.where((idx >> 7) == iota_hi, 1.0, 0.0).astype(BF16)
            got = lax.dot_general(high, low, NT, preferred_element_type=F32)
            row = t * atoms + base + u
            counts[:, pl.ds(row, 1), :] = got.reshape(his, 1, 128)
        return 0

    lax.fori_loop(0, pair // unroll, count, 0)
    for k in range(his):
        counts_b[:, k * 128 : (k + 1) * 128] = counts[k].astype(BF16)

    for e in range(1, zs):
        spread_line(act_tree, e)
        spread_line(sens_tree, e)

    part, _, recv = bulk(chips - zs)[0]
    pltpu.make_async_copy(part, part, recv).wait()
    for d in range(1, rows):
        to = lax.rem(r + d, rows)
        pl.semaphore_signal(row_in, inc=1, device_id=(to, c), device_id_type=MESH)
    neighbor_sum = jnp.dot(
        counts_b[...], up_all[...], preferred_element_type=F32
    ) * (1.0 / math.sqrt(nbr))
    own = up_all[pl.ds(pl.multiple_of(h * pair, pair), pair), :].astype(F32)
    sib_copies[3].wait_recv()
    kinds = jnp.concatenate([kind_all[0], kind_all[1]], axis=1)
    kinds = jnp.transpose(jnp.broadcast_to(kinds, (adjw, pair)))
    type_scale = jnp.zeros((pair, adjw), F32)
    for kind in range(tgain_ref.shape[0]):
        type_scale = jnp.where(kinds == kind, tgain_ref[kind : kind + 1, :], type_scale)
    adj_t[...] = jnp.transpose(type_scale * (own + neighbor_sum)).reshape(chips, bl, pair)
    own_adj = pltpu.make_async_copy(adj_t.at[h], adj_all.at[:, lanes_mine], ad_recv)
    own_adj.start()

    def send_adj(k, _):
        to = lax.rem(h + k, chips)
        remote(adj_t.at[to], adj_all.at[:, lanes_mine], ad_send, ad_recv, r, 2 * to + s).start()
        return 0

    lax.fori_loop(1, chips, send_adj, 0)

    def drain_adj():
        part = adj_all.at[:, pl.ds(0, (chips - 1) * pair)]
        pltpu.make_async_copy(part, part, ad_send).wait()

    drains.append(drain_adj)

    strip = 64

    def split(j):
        def body(i, _):
            at = pl.ds(pl.multiple_of(i * strip, strip), strip)
            value = cov_f[at, j * chunk : (j + 1) * chunk]
            high = value.astype(BF16)
            cov_hi[j, at, :] = high
            cov_lo[j, at, :] = (value - high.astype(F32)).astype(BF16)
            return 0

        lax.fori_loop(0, width // strip, body, 0)

    for j in range(zs):
        cov_in[j].wait()
        split(j)

    for part, _, recv in bulk(chips - zs)[1:]:
        pltpu.make_async_copy(part, part, recv).wait()
    m0 = lax.broadcasted_iota(jnp.int32, (mg, mg), 0)
    m1 = lax.broadcasted_iota(jnp.int32, (mg, mg), 1)
    frame_of = jnp.sum(
        jnp.where(m0 == m1, frame_ref[...].astype(F32), 0.0), axis=1, keepdims=True
    )
    chosen = jnp.where(frame_of == s.astype(F32), 1.0, 0.0)
    sens_own = sens_all[...] * chosen
    pltpu.make_async_copy(adj_all, adj_all, ad_recv).wait()
    for b in range(bl):
        w_rows[mg * b : mg * (b + 1), :] = (sens_own * adj_all[b : b + 1, :]).astype(BF16)
    jac_half[...] = lax.dot_general(
        w_rows[...], act_all[...], NT, preferred_element_type=F32
    )
    swap = remote(jac_half, jac_in, sib_send.at[4], sib_recv.at[4], r, sib)
    swap.start()
    swap.wait_recv()
    whole = jac_half[...] + jac_in[...]
    jac_piece[...] = jnp.concatenate(
        [whole[mg * b : mg * (b + 1), :] for b in range(bl)], axis=1
    ).astype(BF16)
    drains.append(swap.wait_send)
    rows_half = bl * mg // 2
    own_half = jnp.where(s == 0, whole[:rows_half], whole[rows_half:])
    jac_own[...] = jnp.concatenate(
        [own_half[mg * b : mg * (b + 1), :] for b in range(bl // 2)], axis=1
    ).astype(BF16)
    jac_col[r] = jac_own[...]

    half = chips // 2

    def cast(piece, buf, stage):
        at = pl.ds(pl.multiple_of(mg * r, mg), mg)
        lanes = pl.ds(pl.multiple_of(chunk * z, chunk), chunk)
        dst = buf.at[at, lanes]
        rsem = m_recv.at[stage, z * rows + r]
        own = (x == r) & (s == 0)

        @pl.when(own)
        def _():
            pltpu.make_async_copy(piece, dst, rsem).start()

        @pl.when(jnp.logical_not(own))
        def _():
            to = 2 * lax.rem(h + s, chips) + s
            remote(piece, dst, m_send.at[stage, 0], rsem, x, to).start()

        def send(i, _):
            to = 2 * lax.rem(h + 2 * i + s, chips) + s
            remote(piece, dst, m_send.at[stage, i], rsem, x, to).start()
            return 0

        lax.fori_loop(1, half, send, 0)

        def drain():
            @pl.when(jnp.logical_not(own))
            def _():
                pltpu.make_async_copy(piece, piece, m_send.at[stage, 0]).wait()

            def step(i, _):
                pltpu.make_async_copy(piece, piece, m_send.at[stage, i]).wait()
                return 0

            lax.fori_loop(1, half, step, 0)

        drains.append(drain)

    def slot(buf, i, which):
        zz = 2 * (i // rows) + which
        p = lax.rem(i, rows)
        lanes = pl.ds(pl.multiple_of(chunk * zz, chunk), chunk)
        return buf.at[pl.ds(pl.multiple_of(mg * p, mg), mg), lanes], zz * rows + p

    def relay(buf, stage):
        def step(i, _):
            here, k = slot(buf, i, parity)
            pltpu.make_async_copy(here, here, m_recv.at[stage, k]).wait()
            remote(here, here, f_send.at[stage, i], f_recv.at[stage, k], r, sib).start()
            return 0

        lax.fori_loop(0, half, step, 0)

        def drain():
            def step2(i, _):
                here, _ = slot(buf, i, parity)
                pltpu.make_async_copy(here, here, f_send.at[stage, i]).wait()
                return 0

            lax.fori_loop(0, half, step2, 0)

        drains.append(drain)

    def relayed(buf, stage):
        def step(i, _):
            there, k = slot(buf, i, 1 - parity)
            pltpu.make_async_copy(there, there, f_recv.at[stage, k]).wait()
            return 0

        lax.fori_loop(0, half, step, 0)

    pl.semaphore_wait(row_in, rows - 1)
    cast(jac_piece, jac_all, 0)
    for d in range(1, rows):
        to = lax.rem(r + d, rows)
        copy = remote(jac_own, jac_col.at[r], j_send.at[d - 1], j_recv.at[d - 1], to, c)
        copy.start()
        drains.append(copy.wait_send)
    relay(jac_all, 0)

    def times(which):
        def step(i, _):
            zz = 2 * i + which
            jac = jac_all[:, pl.ds(pl.multiple_of(chunk * zz, chunk), chunk)]
            n_part[...] += (
                lax.dot_general(jac, cov_hi[zz], NT, preferred_element_type=F32)
                + lax.dot_general(jac, cov_lo[zz], NT, preferred_element_type=F32)
            ).reshape(rows, mg, width)
            return 0

        lax.fori_loop(0, zs // 2, step, 0)

    n_part[...] = jnp.zeros_like(n_part)
    times(parity)
    relayed(jac_all, 0)
    times(1 - parity)
    for d in range(1, rows):
        to = lax.rem(r + d, rows)
        copy = remote(n_part.at[to], n_in.at[d - 1], y_send.at[d - 1], y_recv.at[d - 1], to, c)
        copy.start()
        drains.append(copy.wait_send)
    for d in range(1, rows):
        pltpu.make_async_copy(n_in.at[d - 1], n_in.at[d - 1], y_recv.at[d - 1]).wait()
    mine_n = n_part[r]
    for d in range(1, rows):
        mine_n = mine_n + n_in[d - 1]
    n_piece[...] = mine_n.astype(BF16)
    swap_n = remote(n_piece, n_pair.at[s], sib_send.at[5], sib_recv.at[5], r, sib)
    swap_n.start()
    drains.append(swap_n.wait_send)
    n_pair[s] = n_piece[...]
    n_col[r] = n_piece[...]
    for d in range(1, rows):
        to = lax.rem(r + d, rows)
        copy = remote(n_piece, n_col.at[r], c_send.at[d - 1], c_recv.at[d - 1], to, c)
        copy.start()
        drains.append(copy.wait_send)
    for d in range(1, rows):
        pltpu.make_async_copy(jac_own, jac_own, j_recv.at[d - 1]).wait()
    n_low = (mine_n - n_piece[...].astype(F32)).astype(BF16)
    jac_here = jac_col[...].reshape(measures, width)
    part = lax.dot_general(
        n_piece[...], jac_here, NT, preferred_element_type=F32
    ) + lax.dot_general(n_low, jac_here, NT, preferred_element_type=F32)
    t_mine[...] = jnp.concatenate([part[: mg // 2], part[mg // 2 :]], axis=1)
    t_in[c] = t_mine[...]

    swap_n.wait_recv()
    n_wide[...] = jnp.concatenate(
        [n_pair[0].astype(F32), n_pair[1].astype(F32)], axis=1
    ).astype(BF16)
    cast(n_wide, nt_ref, 1)

    def send_part(k, _):
        to = lax.rem(c + k, cols)
        remote(t_mine, t_in.at[c], t_send, t_recv, r, to).start()
        return 0

    lax.fori_loop(1, cols, send_part, 0)

    def drain_part():
        sent = t_in.at[pl.ds(0, cols - 1)]
        pltpu.make_async_copy(sent, sent, t_send).wait()

    drains.append(drain_part)
    owned = n_slices.shape[2]
    for t in range(rows):
        n_slices[t] = mine_n[:, t * owned : (t + 1) * owned]
    for t in range(rows):
        to = rows * jz + t
        here = (x == r) & (to == c)

        @pl.when(here)
        def _():
            pltpu.make_async_copy(n_slices.at[t], n_own.at[r], o_recv.at[r]).start()

        @pl.when(jnp.logical_not(here))
        def _():
            remote(n_slices.at[t], n_own.at[r], o_send.at[t], o_recv.at[r], x, to).start()

    arrived = t_in.at[pl.ds(0, cols - 1)]
    pltpu.make_async_copy(arrived, arrived, t_recv).wait()
    t_rows[r] = jnp.sum(t_in[...], axis=0)
    for d in range(1, rows):
        to = lax.rem(r + d, rows)
        copy = remote(t_rows.at[r], t_rows.at[r], q_send.at[d - 1], q_recv.at[d - 1], to, c)
        copy.start()
        drains.append(copy.wait_send)
    relay(nt_ref, 1)
    for d in range(1, rows):
        pltpu.make_async_copy(t_rows.at[0], t_rows.at[0], q_recv.at[d - 1]).wait()
    pieces = []
    for q in range(rows):
        packed = t_rows[q]
        pieces += [packed[:, :measures], packed[:, measures:]]
    innovation_cov = jnp.concatenate(pieces, axis=0)
    i0 = lax.broadcasted_iota(jnp.int32, (measures, measures), 0)
    i1 = lax.broadcasted_iota(jnp.int32, (measures, measures), 1)
    eye = jnp.where(i0 == i1, 1.0, 0.0).astype(F32)
    innovation_cov = innovation_cov + eye * noise_ref[...]
    row_sums = jnp.sum(jnp.abs(innovation_cov), axis=1, keepdims=True)
    first = 1.0 / jnp.max(row_sums, axis=0, keepdims=True)
    inverse = eye * first
    left = eye - innovation_cov * first
    for sweep in range(NS_ITERS):
        inverse = inverse + jnp.dot(inverse, left, precision=FULL, preferred_element_type=F32)
        if sweep < NS_ITERS - 1:
            left = jnp.dot(left, left, precision=FULL, preferred_element_type=F32)
    for d in range(1, rows):
        pltpu.make_async_copy(n_piece, n_piece, c_recv.at[d - 1]).wait()
    n_cols = n_col[...].reshape(measures, width).astype(F32)
    gt_ref[...] = jnp.transpose(
        jnp.dot(inverse, n_cols, precision=FULL, preferred_element_type=F32)
    ).astype(BF16)
    step_col = jnp.sum(inverse * innov_ref[...], axis=1, keepdims=True)
    for p in range(rows):
        pltpu.make_async_copy(n_own.at[p], n_own.at[p], o_recv.at[p]).wait()
    n_mine = n_own[...].reshape(measures, owned)
    wnew_ref[...] = weights_ref[...] + jnp.sum(step_col * n_mine, axis=0, keepdims=True)
    for t in range(rows):
        to = rows * jz + t

        @pl.when(jnp.logical_not((x == r) & (to == c)))
        def _():
            pltpu.make_async_copy(n_slices.at[t], n_slices.at[t], o_send.at[t]).wait()

    relayed(nt_ref, 1)
    for drain in drains:
        drain()


def update_kernel(parts, cov_ref, nt_ref, gt_ref, out_hbm, made, out_sem):
    tile = made.shape[0] // parts
    copies = []
    for i in range(parts):
        at = pl.ds(i * tile, tile)
        made[at, :] = cov_ref[at, :] - jnp.dot(
            gt_ref[at, :], nt_ref[...], preferred_element_type=F32
        )
        copies.append(pltpu.make_async_copy(made.at[at], out_hbm.at[at], out_sem.at[i]))
        copies[-1].start()
    for copy in copies:
        copy.wait()


def on_device(
    cov,
    weights,
    act,
    upstream,
    neighbors,
    types,
    type_gain,
    sens,
    frame_for_measure,
    noise_variance,
    innovation,
):
    rows = lax.axis_size("row")
    cols = lax.axis_size("col")
    per = cols // rows
    chips = cols // 2
    frames, atoms, nbr = neighbors.shape
    pair = 2 * atoms
    all_atoms = cols * atoms
    adjw, actw = upstream.shape[2], act.shape[2]
    mg = sens.shape[0]
    measures = mg * rows
    height, width = cov.shape
    zs = per // 2
    chunk = height // zs
    owned = weights.shape[0]
    bl = adjw // chips
    his = all_atoms // 128
    dma = pltpu.SemaphoreType.DMA
    vmem = pl.BlockSpec(memory_space=pltpu.VMEM)
    n_rows, gain, weights_new, block = pl.pallas_call(
        functools.partial(gain_kernel, rows, cols),
        out_shape=(
            jax.ShapeDtypeStruct((measures, height), BF16),
            jax.ShapeDtypeStruct((width, measures), BF16),
            jax.ShapeDtypeStruct((1, owned), F32),
            jax.ShapeDtypeStruct((width, height), F32),
        ),
        in_specs=[pl.BlockSpec(memory_space=pltpu.HBM)] * 11,
        out_specs=(vmem,) * 4,
        scratch_shapes=[
            pltpu.VMEM((1, owned), F32),
            pltpu.VMEM(type_gain.shape, F32),
            pltpu.VMEM((1, mg), jnp.int32),
            pltpu.VMEM((1, measures), F32),
            pltpu.VMEM((1, measures), F32),
            pltpu.VMEM((zs, width, chunk), BF16),
            pltpu.VMEM((zs, width, chunk), BF16),
            pltpu.VMEM((2, atoms, nbr), jnp.int32),
            pltpu.VMEM((2, 1, atoms), jnp.int32),
            pltpu.VMEM((2, atoms, actw), BF16),
            pltpu.VMEM((2, mg, atoms), F32),
            pltpu.VMEM((his, pair, 128), F32),
            pltpu.VMEM((pair, all_atoms), BF16),
            pltpu.VMEM((all_atoms, adjw), BF16),
            pltpu.VMEM((actw, all_atoms), BF16),
            pltpu.VMEM((mg, all_atoms), F32),
            pltpu.VMEM((chips, bl, pair), F32),
            pltpu.VMEM((bl, all_atoms), F32),
            pltpu.VMEM((bl * mg, all_atoms), BF16),
            pltpu.VMEM((bl * mg, actw), F32),
            pltpu.VMEM((bl * mg, actw), F32),
            pltpu.VMEM((mg, chunk), BF16),
            pltpu.VMEM((measures, height), BF16),
            pltpu.VMEM((rows, mg, width), F32),
            pltpu.VMEM((rows - 1, mg, width), F32),
            pltpu.VMEM((mg, width), BF16),
            pltpu.VMEM((2, mg, width), BF16),
            pltpu.VMEM((mg, chunk), BF16),
            pltpu.VMEM((rows, mg, width), BF16),
            pltpu.VMEM((rows, mg, owned), F32),
            pltpu.VMEM((rows, mg, owned), F32),
            pltpu.VMEM((mg, width), BF16),
            pltpu.VMEM((rows, mg, width), BF16),
            pltpu.VMEM((mg // 2, 2 * measures), F32),
            pltpu.VMEM((cols, mg // 2, 2 * measures), F32),
            pltpu.VMEM((rows, mg // 2, 2 * measures), F32),
            dma((10,)),
            dma((zs,)),
            pltpu.SemaphoreType.REGULAR,
            dma((7,)),
            dma((7,)),
            dma((zs - 1,)),
            dma,
            dma,
            dma((zs - 1,)),
            dma((zs - 1,)),
            dma,
            dma,
            dma,
            dma,
            dma,
            dma,
            dma((2, chips // 2)),
            dma((2, zs * rows)),
            dma((2, chips // 2)),
            dma((2, zs * rows)),
            dma((rows - 1,)),
            dma((rows - 1,)),
            dma((rows - 1,)),
            dma((rows - 1,)),
            dma((rows,)),
            dma((rows,)),
            dma((rows - 1,)),
            dma((rows - 1,)),
            dma,
            dma,
            dma((rows - 1,)),
            dma((rows - 1,)),
        ],
        compiler_params=pltpu.CompilerParams(
            collective_id=0, has_side_effects=True, vmem_limit_bytes=40 * 2**20
        ),
        name="gain",
    )(
        *(
            pltpu.with_memory_space_constraint(array, pltpu.HBM)
            for array in (
                cov.T,
                weights.reshape(1, owned),
                act,
                upstream,
                neighbors,
                types.reshape(frames, 1, atoms),
                type_gain,
                sens,
                frame_for_measure.reshape(1, mg),
                noise_variance.reshape(1, measures),
                innovation.reshape(1, measures),
            )
        )
    )
    parts = width // (8 * math.gcd(width // 8, 9))
    cov_new = pl.pallas_call(
        functools.partial(update_kernel, parts),
        in_specs=[vmem] * 3,
        out_specs=pl.BlockSpec(memory_space=pltpu.HBM),
        out_shape=jax.ShapeDtypeStruct((width, height), F32),
        scratch_shapes=[pltpu.VMEM((width, height), F32), dma((parts,))],
        compiler_params=pltpu.CompilerParams(vmem_limit_bytes=36 * 2**20),
        name="update",
    )(block, n_rows, gain)
    return weights_new.reshape(owned), cov_new.T


def solution(mesh):
    return jax.shard_map(
        on_device,
        mesh=mesh,
        in_specs=(
            P("row", "col"),
            P(("row", "col")),
            P("row", "col", None),
            P("row", "col", None),
            P("row", "col", None),
            P("row", "col"),
            P(),
            P("row", "col"),
            P("row"),
            P(),
            P(),
        ),
        out_specs=(P(("row", "col")), P("row", "col")),
        check_vma=False,
    )
```

```python
import functools
import math

import jax
import jax.numpy as jnp
from jax import lax
from jax.experimental import pallas as pl
from jax.experimental.pallas import tpu as pltpu
from jax.sharding import PartitionSpec as P

NS_ITERS = 5
MESH = pl.DeviceIdType.MESH
FULL = lax.Precision.HIGHEST
F32 = jnp.float32
BF16 = jnp.bfloat16
NT = (((1,), (1,)), ((), ()))


def gain_kernel(
    rows,
    cols,
    cov_hbm,
    weights_hbm,
    act_hbm,
    up_hbm,
    nb_hbm,
    types_hbm,
    tgain_hbm,
    sens_hbm,
    frame_hbm,
    noise_hbm,
    innov_hbm,
    nt_ref,
    gt_ref,
    wnew_ref,
    cov_f,
    weights_ref,
    tgain_ref,
    frame_ref,
    noise_ref,
    innov_ref,
    cov_hi,
    cov_lo,
    nb_all,
    kind_all,
    act_pair,
    sens_pair,
    counts,
    counts_b,
    up_all,
    act_all,
    sens_all,
    adj_t,
    adj_all,
    w_rows,
    jac_half,
    jac_in,
    jac_piece,
    jac_all,
    n_part,
    n_in,
    n_piece,
    n_pair,
    n_wide,
    n_col,
    n_slices,
    n_own,
    jac_own,
    jac_col,
    t_mine,
    t_in,
    t_rows,
    load_sem,
    cov_sem,
    row_in,
    sib_send,
    sib_recv,
    u_first,
    u_send,
    u_recv,
    a_first,
    sn_first,
    a_send,
    a_recv,
    sn_send,
    sn_recv,
    ad_send,
    ad_recv,
    m_send,
    m_recv,
    f_send,
    f_recv,
    y_send,
    y_recv,
    c_send,
    c_recv,
    o_send,
    o_recv,
    j_send,
    j_recv,
    t_send,
    t_recv,
    q_send,
    q_recv,
):
    r = lax.axis_index("row")
    c = lax.axis_index("col")
    chips = cols // 2
    per = cols // rows
    zs = per // 2
    h = c // 2
    s = c % 2
    x = c // per
    z = (c % per) // 2
    jz = c % per
    parity = lax.rem(h + s, 2)
    drains = []
    other = 1 - s
    sib = c + 1 - 2 * s
    atoms = nb_hbm.shape[1]
    pair = 2 * atoms
    nbr = nb_hbm.shape[2]
    adjw = up_hbm.shape[2]
    actw = act_hbm.shape[2]
    mg = sens_hbm.shape[0]
    measures = mg * rows
    width, chunk = cov_hi.shape[1:]
    bl = adjw // chips

    def remote(src, dst, ssem, rsem, tr, tc):
        return pltpu.make_async_remote_copy(
            src_ref=src,
            dst_ref=dst,
            send_sem=ssem,
            recv_sem=rsem,
            device_id=(tr, tc),
            device_id_type=MESH,
        )

    cov_in = [
        pltpu.make_async_copy(
            cov_hbm.at[:, pl.ds(j * chunk, chunk)],
            cov_f.at[:, pl.ds(j * chunk, chunk)],
            cov_sem.at[j],
        )
        for j in range(zs)
    ]

    mine = pl.ds(pl.multiple_of(c * atoms, atoms), atoms)
    loads = [
        pltpu.make_async_copy(src, dst, load_sem.at[i])
        for i, (src, dst) in enumerate(
            (
                (up_hbm.at[s], up_all.at[mine]),
                (nb_hbm.at[s], nb_all.at[s]),
                (act_hbm.at[s], act_pair.at[s]),
                (sens_hbm, sens_pair.at[s]),
                (types_hbm.at[s], kind_all.at[s]),
                (tgain_hbm, tgain_ref),
                (frame_hbm, frame_ref),
                (noise_hbm, noise_ref),
                (innov_hbm, innov_ref),
                (weights_hbm, weights_ref),
            )
        )
    ]
    barrier = pltpu.get_barrier_semaphore()

    def along(in_z, d):
        z_line = x * zs + lax.rem(z + d + zs, zs)
        x_line = lax.rem(x + d + zs, zs) * zs + z
        return jnp.where(in_z, z_line, x_line)

    line_mates = [(r, sib)]
    for d in range(1, zs):
        line_mates += [(r, 2 * along(True, d) + s), (r, 2 * along(False, d) + s)]
    for d in range(1, rows):
        line_mates.append((lax.rem(r + d, rows), c))
    for mate in line_mates:
        pl.semaphore_signal(barrier, inc=1, device_id=mate, device_id_type=MESH)
    for load in loads + cov_in:
        load.start()
    pl.semaphore_wait(barrier, len(line_mates))

    sib_copies = [
        remote(nb_hbm.at[other], nb_all.at[s], sib_send.at[0], sib_recv.at[0], r, sib),
        remote(act_hbm.at[other], act_pair.at[s], sib_send.at[1], sib_recv.at[1], r, sib),
        remote(sens_hbm, sens_pair.at[s], sib_send.at[2], sib_recv.at[2], r, sib),
        remote(types_hbm.at[other], kind_all.at[s], sib_send.at[3], sib_recv.at[3], r, sib),
    ]
    sib_up = remote(up_hbm.at[other], up_all.at[mine], sib_send.at[6], sib_recv.at[6], r, sib)
    sib_up.start()
    for copy in sib_copies:
        copy.start()

    def lanes_of(chip):
        return pl.ds(pl.multiple_of(chip * pair, pair), pair)

    lanes_mine = lanes_of(h)
    begin_z = s == 0
    then_z = s == 1
    up_tree = (lambda chip: up_all.at[lanes_of(chip)], u_first, u_send, u_recv)
    act_tree = (lambda chip: act_all.at[:, lanes_of(chip)], a_first, a_send, a_recv)
    sens_tree = (lambda chip: sens_all.at[:, lanes_of(chip)], sn_first, sn_send, sn_recv)

    def begin(tree):
        block, first, send, recv = tree
        part = block(h)
        for d in range(1, zs):
            remote(part, part, send, first.at[d - 1], r, 2 * along(begin_z, d) + s).start()

    def spread_line(tree, e):
        block, first, send, recv = tree
        part = block(along(begin_z, -e))
        if e > 0:
            pltpu.make_async_copy(part, part, first.at[e - 1]).wait()
        for d in range(1, zs):
            remote(part, part, send, recv, r, 2 * along(then_z, d) + s).start()

    loads[0].wait()
    sib_up.wait_recv()
    begin(up_tree)
    spread_line(up_tree, 0)
    for load in loads[1:]:
        load.wait()
    sib_copies[1].wait_recv()
    sib_copies[2].wait_recv()
    act_all[:, lanes_mine] = jnp.transpose(
        act_pair[...].reshape(pair, actw).astype(F32)
    ).astype(BF16)
    sens_all[:, lanes_mine] = jnp.concatenate([sens_pair[0], sens_pair[1]], axis=1)
    for tree in (act_tree, sens_tree):
        begin(tree)
    for e in range(1, zs):
        spread_line(up_tree, e)
    for tree in (act_tree, sens_tree):
        spread_line(tree, 0)

    def bulk(count):
        blocks = pl.ds(0, count * pair)
        return ((up_all.at[blocks], u_send, u_recv),) + tuple(
            (buf.at[:, blocks], send, recv)
            for buf, send, recv in ((sens_all, sn_send, sn_recv), (act_all, a_send, a_recv))
        )

    def drain_first():
        for copy in [sib_up, *sib_copies]:
            copy.wait_send()
        for part, send, _ in bulk(chips - 1):
            pltpu.make_async_copy(part, part, send).wait()

    drains.append(drain_first)

    sib_copies[0].wait_recv()
    his = counts.shape[0]
    iota_lo = lax.broadcasted_iota(jnp.int32, (128, nbr), 0)
    iota_hi = lax.broadcasted_iota(jnp.int32, (his, nbr), 0)
    unroll = 8

    def count(step, _):
        t = step // (atoms // unroll)
        base = pl.multiple_of(lax.rem(step, atoms // unroll) * unroll, unroll)
        block = nb_all[t, pl.ds(base, unroll), :]
        for u in range(unroll):
            idx = block[u : u + 1, :]
            low = jnp.where((idx & 127) == iota_lo, 1.0, 0.0).astype(BF16)
            high = jnp.where((idx >> 7) == iota_hi, 1.0, 0.0).astype(BF16)
            got = lax.dot_general(high, low, NT, preferred_element_type=F32)
            row = t * atoms + base + u
            counts[:, pl.ds(row, 1), :] = got.reshape(his, 1, 128)
        return 0

    steps = pair // unroll
    for e in range(zs):
        if e > 0:
            spread_line(act_tree, e)
            spread_line(sens_tree, e)
        lax.fori_loop(steps * e // zs, steps * (e + 1) // zs, count, 0)
    for k in range(his):
        counts_b[:, k * 128 : (k + 1) * 128] = counts[k].astype(BF16)


    part, _, recv = bulk(chips - zs)[0]
    pltpu.make_async_copy(part, part, recv).wait()
    for d in range(1, rows):
        to = lax.rem(r + d, rows)
        pl.semaphore_signal(row_in, inc=1, device_id=(to, c), device_id_type=MESH)
    neighbor_sum = jnp.dot(
        counts_b[...], up_all[...], preferred_element_type=F32
    ) * (1.0 / math.sqrt(nbr))
    own = up_all[pl.ds(pl.multiple_of(h * pair, pair), pair), :].astype(F32)
    sib_copies[3].wait_recv()
    kinds = jnp.concatenate([kind_all[0], kind_all[1]], axis=1)
    kinds = jnp.transpose(jnp.broadcast_to(kinds, (adjw, pair)))
    type_scale = jnp.zeros((pair, adjw), F32)
    for kind in range(tgain_ref.shape[0]):
        type_scale = jnp.where(kinds == kind, tgain_ref[kind : kind + 1, :], type_scale)
    adj_t[...] = jnp.transpose(type_scale * (own + neighbor_sum)).reshape(chips, bl, pair)
    own_adj = pltpu.make_async_copy(adj_t.at[h], adj_all.at[:, lanes_mine], ad_recv)
    own_adj.start()

    def send_adj(k, _):
        to = lax.rem(h + k, chips)
        remote(adj_t.at[to], adj_all.at[:, lanes_mine], ad_send, ad_recv, r, 2 * to + s).start()
        return 0

    lax.fori_loop(1, chips, send_adj, 0)

    def drain_adj():
        part = adj_all.at[:, pl.ds(0, (chips - 1) * pair)]
        pltpu.make_async_copy(part, part, ad_send).wait()

    drains.append(drain_adj)

    strip = 64

    def split(j):
        def body(i, _):
            at = pl.ds(pl.multiple_of(i * strip, strip), strip)
            value = cov_f[at, j * chunk : (j + 1) * chunk]
            high = value.astype(BF16)
            cov_hi[j, at, :] = high
            cov_lo[j, at, :] = (value - high.astype(F32)).astype(BF16)
            return 0

        lax.fori_loop(0, width // strip, body, 0)

    for j in range(zs):
        cov_in[j].wait()
        split(j)

    for part, _, recv in bulk(chips - zs)[1:]:
        pltpu.make_async_copy(part, part, recv).wait()
    m0 = lax.broadcasted_iota(jnp.int32, (mg, mg), 0)
    m1 = lax.broadcasted_iota(jnp.int32, (mg, mg), 1)
    frame_of = jnp.sum(
        jnp.where(m0 == m1, frame_ref[...].astype(F32), 0.0), axis=1, keepdims=True
    )
    chosen = jnp.where(frame_of == s.astype(F32), 1.0, 0.0)
    sens_own = sens_all[...] * chosen
    pltpu.make_async_copy(adj_all, adj_all, ad_recv).wait()
    for b in range(bl):
        w_rows[mg * b : mg * (b + 1), :] = (sens_own * adj_all[b : b + 1, :]).astype(BF16)
    jac_half[...] = lax.dot_general(
        w_rows[...], act_all[...], NT, preferred_element_type=F32
    )
    swap = remote(jac_half, jac_in, sib_send.at[4], sib_recv.at[4], r, sib)
    swap.start()
    swap.wait_recv()
    whole = jac_half[...] + jac_in[...]
    jac_piece[...] = jnp.concatenate(
        [whole[mg * b : mg * (b + 1), :] for b in range(bl)], axis=1
    ).astype(BF16)
    drains.append(swap.wait_send)
    rows_half = bl * mg // 2
    own_half = jnp.where(s == 0, whole[:rows_half], whole[rows_half:])
    jac_own[...] = jnp.concatenate(
        [own_half[mg * b : mg * (b + 1), :] for b in range(bl // 2)], axis=1
    ).astype(BF16)
    jac_col[r] = jac_own[...]

    half = chips // 2

    def cast(piece, buf, stage):
        at = pl.ds(pl.multiple_of(mg * r, mg), mg)
        lanes = pl.ds(pl.multiple_of(chunk * z, chunk), chunk)
        dst = buf.at[at, lanes]
        rsem = m_recv.at[stage, z * rows + r]
        own = (x == r) & (s == 0)

        @pl.when(own)
        def _():
            pltpu.make_async_copy(piece, dst, rsem).start()

        @pl.when(jnp.logical_not(own))
        def _():
            to = 2 * lax.rem(h + s, chips) + s
            remote(piece, dst, m_send.at[stage, 0], rsem, x, to).start()

        def send(i, _):
            to = 2 * lax.rem(h + 2 * i + s, chips) + s
            remote(piece, dst, m_send.at[stage, i], rsem, x, to).start()
            return 0

        lax.fori_loop(1, half, send, 0)

        def drain():
            @pl.when(jnp.logical_not(own))
            def _():
                pltpu.make_async_copy(piece, piece, m_send.at[stage, 0]).wait()

            def step(i, _):
                pltpu.make_async_copy(piece, piece, m_send.at[stage, i]).wait()
                return 0

            lax.fori_loop(1, half, step, 0)

        drains.append(drain)

    def slot(buf, i, which):
        zz = 2 * (i // rows) + which
        p = lax.rem(i, rows)
        lanes = pl.ds(pl.multiple_of(chunk * zz, chunk), chunk)
        return buf.at[pl.ds(pl.multiple_of(mg * p, mg), mg), lanes], zz * rows + p

    def relay(buf, stage):
        def step(i, _):
            here, k = slot(buf, i, parity)
            pltpu.make_async_copy(here, here, m_recv.at[stage, k]).wait()
            remote(here, here, f_send.at[stage, i], f_recv.at[stage, k], r, sib).start()
            return 0

        lax.fori_loop(0, half, step, 0)

        def drain():
            def step2(i, _):
                here, _ = slot(buf, i, parity)
                pltpu.make_async_copy(here, here, f_send.at[stage, i]).wait()
                return 0

            lax.fori_loop(0, half, step2, 0)

        drains.append(drain)

    def relayed(buf, stage):
        def step(i, _):
            there, k = slot(buf, i, 1 - parity)
            pltpu.make_async_copy(there, there, f_recv.at[stage, k]).wait()
            return 0

        lax.fori_loop(0, half, step, 0)

    pl.semaphore_wait(row_in, rows - 1)
    cast(jac_piece, jac_all, 0)
    for d in range(1, rows):
        to = lax.rem(r + d, rows)
        copy = remote(jac_own, jac_col.at[r], j_send.at[d - 1], j_recv.at[d - 1], to, c)
        copy.start()
        drains.append(copy.wait_send)
    relay(jac_all, 0)

    def times(which):
        def step(i, _):
            zz = 2 * i + which
            jac = jac_all[:, pl.ds(pl.multiple_of(chunk * zz, chunk), chunk)]
            n_part[...] += (
                lax.dot_general(jac, cov_hi[zz], NT, preferred_element_type=F32)
                + lax.dot_general(jac, cov_lo[zz], NT, preferred_element_type=F32)
            ).reshape(rows, mg, width)
            return 0

        lax.fori_loop(0, zs // 2, step, 0)

    n_part[...] = jnp.zeros_like(n_part)
    times(parity)
    relayed(jac_all, 0)
    times(1 - parity)
    for d in range(1, rows):
        to = lax.rem(r + d, rows)
        copy = remote(n_part.at[to], n_in.at[d - 1], y_send.at[d - 1], y_recv.at[d - 1], to, c)
        copy.start()
        drains.append(copy.wait_send)
    for d in range(1, rows):
        pltpu.make_async_copy(n_in.at[d - 1], n_in.at[d - 1], y_recv.at[d - 1]).wait()
    mine_n = n_part[r]
    for d in range(1, rows):
        mine_n = mine_n + n_in[d - 1]
    n_piece[...] = mine_n.astype(BF16)
    swap_n = remote(n_piece, n_pair.at[s], sib_send.at[5], sib_recv.at[5], r, sib)
    swap_n.start()
    drains.append(swap_n.wait_send)
    n_pair[s] = n_piece[...]
    n_col[r] = n_piece[...]
    for d in range(1, rows):
        pltpu.make_async_copy(jac_own, jac_own, j_recv.at[d - 1]).wait()
    n_low = (mine_n - n_piece[...].astype(F32)).astype(BF16)
    jac_here = jac_col[...].reshape(measures, width)
    part = lax.dot_general(
        n_piece[...], jac_here, NT, preferred_element_type=F32
    ) + lax.dot_general(n_low, jac_here, NT, preferred_element_type=F32)
    t_mine[...] = jnp.concatenate([part[: mg // 2], part[mg // 2 :]], axis=1)
    t_in[c] = t_mine[...]

    def send_part(k, _):
        to = lax.rem(c + k, cols)
        remote(t_mine, t_in.at[c], t_send, t_recv, r, to).start()
        return 0

    lax.fori_loop(1, cols, send_part, 0)

    def drain_part():
        sent = t_in.at[pl.ds(0, cols - 1)]
        pltpu.make_async_copy(sent, sent, t_send).wait()

    drains.append(drain_part)
    swap_n.wait_recv()
    n_wide[...] = jnp.concatenate(
        [n_pair[0].astype(F32), n_pair[1].astype(F32)], axis=1
    ).astype(BF16)
    cast(n_wide, nt_ref, 1)
    for d in range(1, rows):
        to = lax.rem(r + d, rows)
        copy = remote(n_piece, n_col.at[r], c_send.at[d - 1], c_recv.at[d - 1], to, c)
        copy.start()
        drains.append(copy.wait_send)

    owned = n_slices.shape[2]
    for t in range(rows):
        n_slices[t] = mine_n[:, t * owned : (t + 1) * owned]
    for t in range(rows):
        to = rows * jz + t
        here = (x == r) & (to == c)

        @pl.when(here)
        def _():
            pltpu.make_async_copy(n_slices.at[t], n_own.at[r], o_recv.at[r]).start()

        @pl.when(jnp.logical_not(here))
        def _():
            remote(n_slices.at[t], n_own.at[r], o_send.at[t], o_recv.at[r], x, to).start()

    arrived = t_in.at[pl.ds(0, cols - 1)]
    pltpu.make_async_copy(arrived, arrived, t_recv).wait()
    t_rows[r] = jnp.sum(t_in[...], axis=0)
    for d in range(1, rows):
        to = lax.rem(r + d, rows)
        copy = remote(t_rows.at[r], t_rows.at[r], q_send.at[d - 1], q_recv.at[d - 1], to, c)
        copy.start()
        drains.append(copy.wait_send)
    relay(nt_ref, 1)
    for d in range(1, rows):
        pltpu.make_async_copy(t_rows.at[0], t_rows.at[0], q_recv.at[d - 1]).wait()
    pieces = []
    for q in range(rows):
        packed = t_rows[q]
        pieces += [packed[:, :measures], packed[:, measures:]]
    innovation_cov = jnp.concatenate(pieces, axis=0)
    i0 = lax.broadcasted_iota(jnp.int32, (measures, measures), 0)
    i1 = lax.broadcasted_iota(jnp.int32, (measures, measures), 1)
    eye = jnp.where(i0 == i1, 1.0, 0.0).astype(F32)
    innovation_cov = innovation_cov + eye * noise_ref[...]
    row_sums = jnp.sum(jnp.abs(innovation_cov), axis=1, keepdims=True)
    first = 1.0 / jnp.max(row_sums, axis=0, keepdims=True)
    inverse = eye * first
    left = eye - innovation_cov * first
    for sweep in range(NS_ITERS):
        inverse = inverse + jnp.dot(inverse, left, precision=FULL, preferred_element_type=F32)
        if sweep < NS_ITERS - 1:
            left = jnp.dot(left, left, precision=FULL, preferred_element_type=F32)
    for d in range(1, rows):
        pltpu.make_async_copy(n_piece, n_piece, c_recv.at[d - 1]).wait()
    n_cols = n_col[...].reshape(measures, width).astype(F32)
    gt_ref[...] = jnp.transpose(
        jnp.dot(inverse, n_cols, precision=FULL, preferred_element_type=F32)
    ).astype(BF16)
    step_col = jnp.sum(inverse * innov_ref[...], axis=1, keepdims=True)
    for p in range(rows):
        pltpu.make_async_copy(n_own.at[p], n_own.at[p], o_recv.at[p]).wait()
    n_mine = n_own[...].reshape(measures, owned)
    wnew_ref[...] = weights_ref[...] + jnp.sum(step_col * n_mine, axis=0, keepdims=True)
    for t in range(rows):
        to = rows * jz + t

        @pl.when(jnp.logical_not((x == r) & (to == c)))
        def _():
            pltpu.make_async_copy(n_slices.at[t], n_slices.at[t], o_send.at[t]).wait()

    relayed(nt_ref, 1)
    for drain in drains:
        drain()


def update_kernel(parts, cov_ref, nt_ref, gt_ref, out_hbm, made, out_sem):
    tile = made.shape[0] // parts
    copies = []
    for i in range(parts):
        at = pl.ds(i * tile, tile)
        made[at, :] = cov_ref[at, :] - jnp.dot(
            gt_ref[at, :], nt_ref[...], preferred_element_type=F32
        )
        copies.append(pltpu.make_async_copy(made.at[at], out_hbm.at[at], out_sem.at[i]))
        copies[-1].start()
    for copy in copies:
        copy.wait()


def on_device(
    cov,
    weights,
    act,
    upstream,
    neighbors,
    types,
    type_gain,
    sens,
    frame_for_measure,
    noise_variance,
    innovation,
):
    rows = lax.axis_size("row")
    cols = lax.axis_size("col")
    per = cols // rows
    chips = cols // 2
    frames, atoms, nbr = neighbors.shape
    pair = 2 * atoms
    all_atoms = cols * atoms
    adjw, actw = upstream.shape[2], act.shape[2]
    mg = sens.shape[0]
    measures = mg * rows
    height, width = cov.shape
    zs = per // 2
    chunk = height // zs
    owned = weights.shape[0]
    bl = adjw // chips
    his = all_atoms // 128
    dma = pltpu.SemaphoreType.DMA
    vmem = pl.BlockSpec(memory_space=pltpu.VMEM)
    n_rows, gain, weights_new, block = pl.pallas_call(
        functools.partial(gain_kernel, rows, cols),
        out_shape=(
            jax.ShapeDtypeStruct((measures, height), BF16),
            jax.ShapeDtypeStruct((width, measures), BF16),
            jax.ShapeDtypeStruct((1, owned), F32),
            jax.ShapeDtypeStruct((width, height), F32),
        ),
        in_specs=[pl.BlockSpec(memory_space=pltpu.HBM)] * 11,
        out_specs=(vmem,) * 4,
        scratch_shapes=[
            pltpu.VMEM((1, owned), F32),
            pltpu.VMEM(type_gain.shape, F32),
            pltpu.VMEM((1, mg), jnp.int32),
            pltpu.VMEM((1, measures), F32),
            pltpu.VMEM((1, measures), F32),
            pltpu.VMEM((zs, width, chunk), BF16),
            pltpu.VMEM((zs, width, chunk), BF16),
            pltpu.VMEM((2, atoms, nbr), jnp.int32),
            pltpu.VMEM((2, 1, atoms), jnp.int32),
            pltpu.VMEM((2, atoms, actw), BF16),
            pltpu.VMEM((2, mg, atoms), F32),
            pltpu.VMEM((his, pair, 128), F32),
            pltpu.VMEM((pair, all_atoms), BF16),
            pltpu.VMEM((all_atoms, adjw), BF16),
            pltpu.VMEM((actw, all_atoms), BF16),
            pltpu.VMEM((mg, all_atoms), F32),
            pltpu.VMEM((chips, bl, pair), F32),
            pltpu.VMEM((bl, all_atoms), F32),
            pltpu.VMEM((bl * mg, all_atoms), BF16),
            pltpu.VMEM((bl * mg, actw), F32),
            pltpu.VMEM((bl * mg, actw), F32),
            pltpu.VMEM((mg, chunk), BF16),
            pltpu.VMEM((measures, height), BF16),
            pltpu.VMEM((rows, mg, width), F32),
            pltpu.VMEM((rows - 1, mg, width), F32),
            pltpu.VMEM((mg, width), BF16),
            pltpu.VMEM((2, mg, width), BF16),
            pltpu.VMEM((mg, chunk), BF16),
            pltpu.VMEM((rows, mg, width), BF16),
            pltpu.VMEM((rows, mg, owned), F32),
            pltpu.VMEM((rows, mg, owned), F32),
            pltpu.VMEM((mg, width), BF16),
            pltpu.VMEM((rows, mg, width), BF16),
            pltpu.VMEM((mg // 2, 2 * measures), F32),
            pltpu.VMEM((cols, mg // 2, 2 * measures), F32),
            pltpu.VMEM((rows, mg // 2, 2 * measures), F32),
            dma((10,)),
            dma((zs,)),
            pltpu.SemaphoreType.REGULAR,
            dma((7,)),
            dma((7,)),
            dma((zs - 1,)),
            dma,
            dma,
            dma((zs - 1,)),
            dma((zs - 1,)),
            dma,
            dma,
            dma,
            dma,
            dma,
            dma,
            dma((2, chips // 2)),
            dma((2, zs * rows)),
            dma((2, chips // 2)),
            dma((2, zs * rows)),
            dma((rows - 1,)),
            dma((rows - 1,)),
            dma((rows - 1,)),
            dma((rows - 1,)),
            dma((rows,)),
            dma((rows,)),
            dma((rows - 1,)),
            dma((rows - 1,)),
            dma,
            dma,
            dma((rows - 1,)),
            dma((rows - 1,)),
        ],
        compiler_params=pltpu.CompilerParams(
            collective_id=0, has_side_effects=True, vmem_limit_bytes=40 * 2**20
        ),
        name="gain",
    )(
        *(
            pltpu.with_memory_space_constraint(array, pltpu.HBM)
            for array in (
                cov.T,
                weights.reshape(1, owned),
                act,
                upstream,
                neighbors,
                types.reshape(frames, 1, atoms),
                type_gain,
                sens,
                frame_for_measure.reshape(1, mg),
                noise_variance.reshape(1, measures),
                innovation.reshape(1, measures),
            )
        )
    )
    parts = width // (8 * math.gcd(width // 8, 9))
    cov_new = pl.pallas_call(
        functools.partial(update_kernel, parts),
        in_specs=[vmem] * 3,
        out_specs=pl.BlockSpec(memory_space=pltpu.HBM),
        out_shape=jax.ShapeDtypeStruct((width, height), F32),
        scratch_shapes=[pltpu.VMEM((width, height), F32), dma((parts,))],
        compiler_params=pltpu.CompilerParams(vmem_limit_bytes=36 * 2**20),
        name="update",
    )(block, n_rows, gain)
    return weights_new.reshape(owned), cov_new.T


def solution(mesh):
    return jax.shard_map(
        on_device,
        mesh=mesh,
        in_specs=(
            P("row", "col"),
            P(("row", "col")),
            P("row", "col", None),
            P("row", "col", None),
            P("row", "col", None),
            P("row", "col"),
            P(),
            P("row", "col"),
            P("row"),
            P(),
            P(),
        ),
        out_specs=(P(("row", "col")), P("row", "col")),
        check_vma=False,
    )
```

```python
import functools
import math

import jax
import jax.numpy as jnp
from jax import lax
from jax.experimental import pallas as pl
from jax.experimental.pallas import tpu as pltpu
from jax.sharding import PartitionSpec as P

NS_ITERS = 5
MESH = pl.DeviceIdType.MESH
FULL = lax.Precision.HIGHEST
F32 = jnp.float32
BF16 = jnp.bfloat16
NT = (((1,), (1,)), ((), ()))


def gain_kernel(
    rows,
    cols,
    cov_hbm,
    weights_hbm,
    act_hbm,
    up_hbm,
    nb_hbm,
    types_hbm,
    tgain_hbm,
    sens_hbm,
    frame_hbm,
    noise_hbm,
    innov_hbm,
    nt_ref,
    gt_ref,
    wnew_ref,
    cov_f,
    weights_ref,
    tgain_ref,
    frame_ref,
    noise_ref,
    innov_ref,
    cov_hi,
    cov_lo,
    nb_all,
    kind_all,
    act_pair,
    sens_pair,
    counts,
    counts_b,
    up_all,
    act_all,
    sens_all,
    adj_t,
    adj_all,
    w_rows,
    jac_half,
    jac_in,
    jac_piece,
    jac_all,
    n_part,
    n_in,
    n_piece,
    n_pair,
    n_wide,
    n_col,
    n_slices,
    n_own,
    jac_own,
    jac_col,
    t_mine,
    t_in,
    t_rows,
    load_sem,
    cov_sem,
    row_in,
    sib_send,
    sib_recv,
    u_first,
    u_send,
    u_recv,
    a_first,
    sn_first,
    a_send,
    a_recv,
    sn_send,
    sn_recv,
    ad_send,
    ad_recv,
    m_send,
    m_recv,
    f_send,
    f_recv,
    y_send,
    y_recv,
    c_send,
    c_recv,
    o_send,
    o_recv,
    j_send,
    j_recv,
    t_send,
    t_recv,
    q_send,
    q_recv,
):
    r = lax.axis_index("row")
    c = lax.axis_index("col")
    chips = cols // 2
    per = cols // rows
    zs = per // 2
    h = c // 2
    s = c % 2
    x = c // per
    z = (c % per) // 2
    jz = c % per
    parity = lax.rem(h + s, 2)
    drains = []
    other = 1 - s
    sib = c + 1 - 2 * s
    atoms = nb_hbm.shape[1]
    pair = 2 * atoms
    nbr = nb_hbm.shape[2]
    adjw = up_hbm.shape[2]
    actw = act_hbm.shape[2]
    mg = sens_hbm.shape[0]
    measures = mg * rows
    width, chunk = cov_hi.shape[1:]
    bl = adjw // chips

    def remote(src, dst, ssem, rsem, tr, tc):
        return pltpu.make_async_remote_copy(
            src_ref=src,
            dst_ref=dst,
            send_sem=ssem,
            recv_sem=rsem,
            device_id=(tr, tc),
            device_id_type=MESH,
        )

    cov_in = [
        pltpu.make_async_copy(
            cov_hbm.at[:, pl.ds(j * chunk, chunk)],
            cov_f.at[:, pl.ds(j * chunk, chunk)],
            cov_sem.at[j],
        )
        for j in range(zs)
    ]

    mine = pl.ds(pl.multiple_of(c * atoms, atoms), atoms)
    loads = [
        pltpu.make_async_copy(src, dst, load_sem.at[i])
        for i, (src, dst) in enumerate(
            (
                (up_hbm.at[s], up_all.at[mine]),
                (nb_hbm.at[s], nb_all.at[s]),
                (act_hbm.at[s], act_pair.at[s]),
                (sens_hbm, sens_pair.at[s]),
                (types_hbm.at[s], kind_all.at[s]),
                (tgain_hbm, tgain_ref),
                (frame_hbm, frame_ref),
                (noise_hbm, noise_ref),
                (innov_hbm, innov_ref),
                (weights_hbm, weights_ref),
            )
        )
    ]
    barrier = pltpu.get_barrier_semaphore()

    def along(in_z, d):
        z_line = x * zs + lax.rem(z + d + zs, zs)
        x_line = lax.rem(x + d + zs, zs) * zs + z
        return jnp.where(in_z, z_line, x_line)

    line_mates = [(r, sib)]
    for d in range(1, zs):
        line_mates += [(r, 2 * along(True, d) + s), (r, 2 * along(False, d) + s)]
    for d in range(1, rows):
        line_mates.append((lax.rem(r + d, rows), c))
    loads[0].start()
    for mate in line_mates:
        pl.semaphore_signal(barrier, inc=1, device_id=mate, device_id_type=MESH)
    for load in loads[1:] + cov_in:
        load.start()
    pl.semaphore_wait(barrier, len(line_mates))

    sib_copies = [
        remote(nb_hbm.at[other], nb_all.at[s], sib_send.at[0], sib_recv.at[0], r, sib),
        remote(act_hbm.at[other], act_pair.at[s], sib_send.at[1], sib_recv.at[1], r, sib),
        remote(sens_hbm, sens_pair.at[s], sib_send.at[2], sib_recv.at[2], r, sib),
        remote(types_hbm.at[other], kind_all.at[s], sib_send.at[3], sib_recv.at[3], r, sib),
    ]
    sib_up = remote(up_hbm.at[other], up_all.at[mine], sib_send.at[6], sib_recv.at[6], r, sib)
    sib_up.start()
    for copy in sib_copies:
        copy.start()

    def lanes_of(chip):
        return pl.ds(pl.multiple_of(chip * pair, pair), pair)

    lanes_mine = lanes_of(h)
    begin_z = s == 0
    then_z = s == 1
    up_tree = (lambda chip: up_all.at[lanes_of(chip)], u_first, u_send, u_recv)
    act_tree = (lambda chip: act_all.at[:, lanes_of(chip)], a_first, a_send, a_recv)
    sens_tree = (lambda chip: sens_all.at[:, lanes_of(chip)], sn_first, sn_send, sn_recv)

    def begin(tree):
        block, first, send, recv = tree
        part = block(h)
        for d in range(1, zs):
            remote(part, part, send, first.at[d - 1], r, 2 * along(begin_z, d) + s).start()

    def spread_line(tree, e):
        block, first, send, recv = tree
        part = block(along(begin_z, -e))
        if e > 0:
            pltpu.make_async_copy(part, part, first.at[e - 1]).wait()
        for d in range(1, zs):
            remote(part, part, send, recv, r, 2 * along(then_z, d) + s).start()

    loads[0].wait()
    sib_up.wait_recv()
    begin(up_tree)
    spread_line(up_tree, 0)
    for load in loads[1:]:
        load.wait()
    sib_copies[1].wait_recv()
    sib_copies[2].wait_recv()
    act_all[:, lanes_mine] = jnp.transpose(
        act_pair[...].reshape(pair, actw).astype(F32)
    ).astype(BF16)
    sens_all[:, lanes_mine] = jnp.concatenate([sens_pair[0], sens_pair[1]], axis=1)
    for tree in (act_tree, sens_tree):
        begin(tree)
    for e in range(1, zs):
        spread_line(up_tree, e)
    for tree in (act_tree, sens_tree):
        spread_line(tree, 0)

    def bulk(count):
        blocks = pl.ds(0, count * pair)
        return ((up_all.at[blocks], u_send, u_recv),) + tuple(
            (buf.at[:, blocks], send, recv)
            for buf, send, recv in ((sens_all, sn_send, sn_recv), (act_all, a_send, a_recv))
        )

    def drain_first():
        for copy in [sib_up, *sib_copies]:
            copy.wait_send()
        for part, send, _ in bulk(chips - 1):
            pltpu.make_async_copy(part, part, send).wait()

    drains.append(drain_first)

    sib_copies[0].wait_recv()
    his = counts.shape[0]
    iota_lo = lax.broadcasted_iota(jnp.int32, (128, nbr), 0)
    iota_hi = lax.broadcasted_iota(jnp.int32, (his, nbr), 0)
    unroll = 8

    def count(step, _):
        t = step // (atoms // unroll)
        base = pl.multiple_of(lax.rem(step, atoms // unroll) * unroll, unroll)
        block = nb_all[t, pl.ds(base, unroll), :]
        for u in range(unroll):
            idx = block[u : u + 1, :]
            low = jnp.where((idx & 127) == iota_lo, 1.0, 0.0).astype(BF16)
            high = jnp.where((idx >> 7) == iota_hi, 1.0, 0.0).astype(BF16)
            got = lax.dot_general(high, low, NT, preferred_element_type=F32)
            row = t * atoms + base + u
            counts[:, pl.ds(row, 1), :] = got.reshape(his, 1, 128)
        return 0

    steps = pair // unroll
    for e in range(zs):
        if e > 0:
            spread_line(act_tree, e)
            spread_line(sens_tree, e)
        lax.fori_loop(steps * e // zs, steps * (e + 1) // zs, count, 0)
    for k in range(his):
        counts_b[:, k * 128 : (k + 1) * 128] = counts[k].astype(BF16)


    part, _, recv = bulk(chips - zs)[0]
    pltpu.make_async_copy(part, part, recv).wait()
    for d in range(1, rows):
        to = lax.rem(r + d, rows)
        pl.semaphore_signal(row_in, inc=1, device_id=(to, c), device_id_type=MESH)
    neighbor_sum = jnp.dot(
        counts_b[...], up_all[...], preferred_element_type=F32
    ) * (1.0 / math.sqrt(nbr))
    own = up_all[pl.ds(pl.multiple_of(h * pair, pair), pair), :].astype(F32)
    sib_copies[3].wait_recv()
    kinds = jnp.concatenate([kind_all[0], kind_all[1]], axis=1)
    kinds = jnp.transpose(jnp.broadcast_to(kinds, (adjw, pair)))
    type_scale = jnp.zeros((pair, adjw), F32)
    for kind in range(tgain_ref.shape[0]):
        type_scale = jnp.where(kinds == kind, tgain_ref[kind : kind + 1, :], type_scale)
    adj_t[...] = jnp.transpose(type_scale * (own + neighbor_sum)).reshape(chips, bl, pair)
    own_adj = pltpu.make_async_copy(adj_t.at[h], adj_all.at[:, lanes_mine], ad_recv)
    own_adj.start()

    def send_adj(k, _):
        to = lax.rem(h + k, chips)
        remote(adj_t.at[to], adj_all.at[:, lanes_mine], ad_send, ad_recv, r, 2 * to + s).start()
        return 0

    lax.fori_loop(1, chips, send_adj, 0)

    def drain_adj():
        part = adj_all.at[:, pl.ds(0, (chips - 1) * pair)]
        pltpu.make_async_copy(part, part, ad_send).wait()

    drains.append(drain_adj)

    strip = 64

    def split(j):
        def body(i, _):
            at = pl.ds(pl.multiple_of(i * strip, strip), strip)
            value = cov_f[at, j * chunk : (j + 1) * chunk]
            high = value.astype(BF16)
            cov_hi[j, at, :] = high
            cov_lo[j, at, :] = (value - high.astype(F32)).astype(BF16)
            return 0

        lax.fori_loop(0, width // strip, body, 0)

    for j in range(zs):
        cov_in[j].wait()
        split(j)

    for part, _, recv in bulk(chips - zs)[1:]:
        pltpu.make_async_copy(part, part, recv).wait()
    m0 = lax.broadcasted_iota(jnp.int32, (mg, mg), 0)
    m1 = lax.broadcasted_iota(jnp.int32, (mg, mg), 1)
    frame_of = jnp.sum(
        jnp.where(m0 == m1, frame_ref[...].astype(F32), 0.0), axis=1, keepdims=True
    )
    chosen = jnp.where(frame_of == s.astype(F32), 1.0, 0.0)
    sens_own = sens_all[...] * chosen
    pltpu.make_async_copy(adj_all, adj_all, ad_recv).wait()
    for b in range(bl):
        w_rows[mg * b : mg * (b + 1), :] = (sens_own * adj_all[b : b + 1, :]).astype(BF16)
    jac_half[...] = lax.dot_general(
        w_rows[...], act_all[...], NT, preferred_element_type=F32
    )
    swap = remote(jac_half, jac_in, sib_send.at[4], sib_recv.at[4], r, sib)
    swap.start()
    swap.wait_recv()
    whole = jac_half[...] + jac_in[...]
    jac_piece[...] = jnp.concatenate(
        [whole[mg * b : mg * (b + 1), :] for b in range(bl)], axis=1
    ).astype(BF16)
    drains.append(swap.wait_send)
    rows_half = bl * mg // 2
    own_half = jnp.where(s == 0, whole[:rows_half], whole[rows_half:])
    jac_own[...] = jnp.concatenate(
        [own_half[mg * b : mg * (b + 1), :] for b in range(bl // 2)], axis=1
    ).astype(BF16)
    jac_col[r] = jac_own[...]

    half = chips // 2

    def cast(piece, buf, stage):
        at = pl.ds(pl.multiple_of(mg * r, mg), mg)
        lanes = pl.ds(pl.multiple_of(chunk * z, chunk), chunk)
        dst = buf.at[at, lanes]
        rsem = m_recv.at[stage, z * rows + r]
        own = (x == r) & (s == 0)

        @pl.when(own)
        def _():
            pltpu.make_async_copy(piece, dst, rsem).start()

        @pl.when(jnp.logical_not(own))
        def _():
            to = 2 * lax.rem(h + s, chips) + s
            remote(piece, dst, m_send.at[stage, 0], rsem, x, to).start()

        def send(i, _):
            to = 2 * lax.rem(h + 2 * i + s, chips) + s
            remote(piece, dst, m_send.at[stage, i], rsem, x, to).start()
            return 0

        lax.fori_loop(1, half, send, 0)

        def drain():
            @pl.when(jnp.logical_not(own))
            def _():
                pltpu.make_async_copy(piece, piece, m_send.at[stage, 0]).wait()

            def step(i, _):
                pltpu.make_async_copy(piece, piece, m_send.at[stage, i]).wait()
                return 0

            lax.fori_loop(1, half, step, 0)

        drains.append(drain)

    def slot(buf, i, which):
        zz = 2 * (i // rows) + which
        p = lax.rem(i, rows)
        lanes = pl.ds(pl.multiple_of(chunk * zz, chunk), chunk)
        return buf.at[pl.ds(pl.multiple_of(mg * p, mg), mg), lanes], zz * rows + p

    def relay(buf, stage):
        def step(i, _):
            here, k = slot(buf, i, parity)
            pltpu.make_async_copy(here, here, m_recv.at[stage, k]).wait()
            remote(here, here, f_send.at[stage, i], f_recv.at[stage, k], r, sib).start()
            return 0

        lax.fori_loop(0, half, step, 0)

        def drain():
            def step2(i, _):
                here, _ = slot(buf, i, parity)
                pltpu.make_async_copy(here, here, f_send.at[stage, i]).wait()
                return 0

            lax.fori_loop(0, half, step2, 0)

        drains.append(drain)

    def relayed(buf, stage):
        def step(i, _):
            there, k = slot(buf, i, 1 - parity)
            pltpu.make_async_copy(there, there, f_recv.at[stage, k]).wait()
            return 0

        lax.fori_loop(0, half, step, 0)

    pl.semaphore_wait(row_in, rows - 1)
    cast(jac_piece, jac_all, 0)
    for d in range(1, rows):
        to = lax.rem(r + d, rows)
        copy = remote(jac_own, jac_col.at[r], j_send.at[d - 1], j_recv.at[d - 1], to, c)
        copy.start()
        drains.append(copy.wait_send)
    relay(jac_all, 0)

    def times(which):
        def step(i, _):
            zz = 2 * i + which
            jac = jac_all[:, pl.ds(pl.multiple_of(chunk * zz, chunk), chunk)]
            n_part[...] += (
                lax.dot_general(jac, cov_hi[zz], NT, preferred_element_type=F32)
                + lax.dot_general(jac, cov_lo[zz], NT, preferred_element_type=F32)
            ).reshape(rows, mg, width)
            return 0

        lax.fori_loop(0, zs // 2, step, 0)

    n_part[...] = jnp.zeros_like(n_part)
    times(parity)
    relayed(jac_all, 0)
    times(1 - parity)
    for d in range(1, rows):
        to = lax.rem(r + d, rows)
        copy = remote(n_part.at[to], n_in.at[d - 1], y_send.at[d - 1], y_recv.at[d - 1], to, c)
        copy.start()
        drains.append(copy.wait_send)
    for d in range(1, rows):
        pltpu.make_async_copy(n_in.at[d - 1], n_in.at[d - 1], y_recv.at[d - 1]).wait()
    mine_n = n_part[r]
    for d in range(1, rows):
        mine_n = mine_n + n_in[d - 1]
    n_piece[...] = mine_n.astype(BF16)
    swap_n = remote(n_piece, n_pair.at[s], sib_send.at[5], sib_recv.at[5], r, sib)
    swap_n.start()
    drains.append(swap_n.wait_send)
    n_pair[s] = n_piece[...]
    n_col[r] = n_piece[...]
    for d in range(1, rows):
        pltpu.make_async_copy(jac_own, jac_own, j_recv.at[d - 1]).wait()
    n_low = (mine_n - n_piece[...].astype(F32)).astype(BF16)
    jac_here = jac_col[...].reshape(measures, width)
    part = lax.dot_general(
        n_piece[...], jac_here, NT, preferred_element_type=F32
    ) + lax.dot_general(n_low, jac_here, NT, preferred_element_type=F32)
    t_mine[...] = jnp.concatenate([part[: mg // 2], part[mg // 2 :]], axis=1)
    t_in[c] = t_mine[...]

    def send_part(k, _):
        to = lax.rem(c + k, cols)
        remote(t_mine, t_in.at[c], t_send, t_recv, r, to).start()
        return 0

    lax.fori_loop(1, cols, send_part, 0)

    def drain_part():
        sent = t_in.at[pl.ds(0, cols - 1)]
        pltpu.make_async_copy(sent, sent, t_send).wait()

    drains.append(drain_part)
    swap_n.wait_recv()
    n_wide[...] = jnp.concatenate(
        [n_pair[0].astype(F32), n_pair[1].astype(F32)], axis=1
    ).astype(BF16)
    cast(n_wide, nt_ref, 1)
    for d in range(1, rows):
        to = lax.rem(r + d, rows)
        copy = remote(n_piece, n_col.at[r], c_send.at[d - 1], c_recv.at[d - 1], to, c)
        copy.start()
        drains.append(copy.wait_send)

    owned = n_slices.shape[2]
    for t in range(rows):
        n_slices[t] = mine_n[:, t * owned : (t + 1) * owned]
    for t in range(rows):
        to = rows * jz + t
        here = (x == r) & (to == c)

        @pl.when(here)
        def _():
            pltpu.make_async_copy(n_slices.at[t], n_own.at[r], o_recv.at[r]).start()

        @pl.when(jnp.logical_not(here))
        def _():
            remote(n_slices.at[t], n_own.at[r], o_send.at[t], o_recv.at[r], x, to).start()

    arrived = t_in.at[pl.ds(0, cols - 1)]
    pltpu.make_async_copy(arrived, arrived, t_recv).wait()
    t_rows[r] = jnp.sum(t_in[...], axis=0)
    for d in range(1, rows):
        to = lax.rem(r + d, rows)
        copy = remote(t_rows.at[r], t_rows.at[r], q_send.at[d - 1], q_recv.at[d - 1], to, c)
        copy.start()
        drains.append(copy.wait_send)
    relay(nt_ref, 1)
    for d in range(1, rows):
        pltpu.make_async_copy(t_rows.at[0], t_rows.at[0], q_recv.at[d - 1]).wait()
    pieces = []
    for q in range(rows):
        packed = t_rows[q]
        pieces += [packed[:, :measures], packed[:, measures:]]
    innovation_cov = jnp.concatenate(pieces, axis=0)
    i0 = lax.broadcasted_iota(jnp.int32, (measures, measures), 0)
    i1 = lax.broadcasted_iota(jnp.int32, (measures, measures), 1)
    eye = jnp.where(i0 == i1, 1.0, 0.0).astype(F32)
    innovation_cov = innovation_cov + eye * noise_ref[...]
    row_sums = jnp.sum(jnp.abs(innovation_cov), axis=1, keepdims=True)
    first = 1.0 / jnp.max(row_sums, axis=0, keepdims=True)
    inverse = eye * first
    left = eye - innovation_cov * first
    for sweep in range(NS_ITERS):
        if sweep == NS_ITERS - 1:
            both = inverse
        else:
            both = jnp.concatenate([inverse, left], axis=0)
        both = jnp.dot(both, left, precision=FULL, preferred_element_type=F32)
        inverse = inverse + both[:measures]
        left = both[measures:]
    for d in range(1, rows):
        pltpu.make_async_copy(n_piece, n_piece, c_recv.at[d - 1]).wait()
    n_cols = n_col[...].reshape(measures, width).astype(F32)
    gt_ref[...] = jnp.transpose(
        jnp.dot(inverse, n_cols, precision=FULL, preferred_element_type=F32)
    ).astype(BF16)
    step_col = jnp.sum(inverse * innov_ref[...], axis=1, keepdims=True)
    for p in range(rows):
        pltpu.make_async_copy(n_own.at[p], n_own.at[p], o_recv.at[p]).wait()
    n_mine = n_own[...].reshape(measures, owned)
    wnew_ref[...] = weights_ref[...] + jnp.sum(step_col * n_mine, axis=0, keepdims=True)
    for t in range(rows):
        to = rows * jz + t

        @pl.when(jnp.logical_not((x == r) & (to == c)))
        def _():
            pltpu.make_async_copy(n_slices.at[t], n_slices.at[t], o_send.at[t]).wait()

    relayed(nt_ref, 1)
    for drain in drains:
        drain()


def update_kernel(parts, cov_ref, nt_ref, gt_ref, out_hbm, made, out_sem):
    tile = made.shape[0] // parts
    copies = []
    for i in range(parts):
        at = pl.ds(i * tile, tile)
        made[at, :] = cov_ref[at, :] - jnp.dot(
            gt_ref[at, :], nt_ref[...], preferred_element_type=F32
        )
        copies.append(pltpu.make_async_copy(made.at[at], out_hbm.at[at], out_sem.at[i]))
        copies[-1].start()
    for copy in copies:
        copy.wait()


def on_device(
    cov,
    weights,
    act,
    upstream,
    neighbors,
    types,
    type_gain,
    sens,
    frame_for_measure,
    noise_variance,
    innovation,
):
    rows = lax.axis_size("row")
    cols = lax.axis_size("col")
    per = cols // rows
    chips = cols // 2
    frames, atoms, nbr = neighbors.shape
    pair = 2 * atoms
    all_atoms = cols * atoms
    adjw, actw = upstream.shape[2], act.shape[2]
    mg = sens.shape[0]
    measures = mg * rows
    height, width = cov.shape
    zs = per // 2
    chunk = height // zs
    owned = weights.shape[0]
    bl = adjw // chips
    his = all_atoms // 128
    dma = pltpu.SemaphoreType.DMA
    vmem = pl.BlockSpec(memory_space=pltpu.VMEM)
    n_rows, gain, weights_new, block = pl.pallas_call(
        functools.partial(gain_kernel, rows, cols),
        out_shape=(
            jax.ShapeDtypeStruct((measures, height), BF16),
            jax.ShapeDtypeStruct((width, measures), BF16),
            jax.ShapeDtypeStruct((1, owned), F32),
            jax.ShapeDtypeStruct((width, height), F32),
        ),
        in_specs=[pl.BlockSpec(memory_space=pltpu.HBM)] * 11,
        out_specs=(vmem,) * 4,
        scratch_shapes=[
            pltpu.VMEM((1, owned), F32),
            pltpu.VMEM(type_gain.shape, F32),
            pltpu.VMEM((1, mg), jnp.int32),
            pltpu.VMEM((1, measures), F32),
            pltpu.VMEM((1, measures), F32),
            pltpu.VMEM((zs, width, chunk), BF16),
            pltpu.VMEM((zs, width, chunk), BF16),
            pltpu.VMEM((2, atoms, nbr), jnp.int32),
            pltpu.VMEM((2, 1, atoms), jnp.int32),
            pltpu.VMEM((2, atoms, actw), BF16),
            pltpu.VMEM((2, mg, atoms), F32),
            pltpu.VMEM((his, pair, 128), F32),
            pltpu.VMEM((pair, all_atoms), BF16),
            pltpu.VMEM((all_atoms, adjw), BF16),
            pltpu.VMEM((actw, all_atoms), BF16),
            pltpu.VMEM((mg, all_atoms), F32),
            pltpu.VMEM((chips, bl, pair), F32),
            pltpu.VMEM((bl, all_atoms), F32),
            pltpu.VMEM((bl * mg, all_atoms), BF16),
            pltpu.VMEM((bl * mg, actw), F32),
            pltpu.VMEM((bl * mg, actw), F32),
            pltpu.VMEM((mg, chunk), BF16),
            pltpu.VMEM((measures, height), BF16),
            pltpu.VMEM((rows, mg, width), F32),
            pltpu.VMEM((rows - 1, mg, width), F32),
            pltpu.VMEM((mg, width), BF16),
            pltpu.VMEM((2, mg, width), BF16),
            pltpu.VMEM((mg, chunk), BF16),
            pltpu.VMEM((rows, mg, width), BF16),
            pltpu.VMEM((rows, mg, owned), F32),
            pltpu.VMEM((rows, mg, owned), F32),
            pltpu.VMEM((mg, width), BF16),
            pltpu.VMEM((rows, mg, width), BF16),
            pltpu.VMEM((mg // 2, 2 * measures), F32),
            pltpu.VMEM((cols, mg // 2, 2 * measures), F32),
            pltpu.VMEM((rows, mg // 2, 2 * measures), F32),
            dma((10,)),
            dma((zs,)),
            pltpu.SemaphoreType.REGULAR,
            dma((7,)),
            dma((7,)),
            dma((zs - 1,)),
            dma,
            dma,
            dma((zs - 1,)),
            dma((zs - 1,)),
            dma,
            dma,
            dma,
            dma,
            dma,
            dma,
            dma((2, chips // 2)),
            dma((2, zs * rows)),
            dma((2, chips // 2)),
            dma((2, zs * rows)),
            dma((rows - 1,)),
            dma((rows - 1,)),
            dma((rows - 1,)),
            dma((rows - 1,)),
            dma((rows,)),
            dma((rows,)),
            dma((rows - 1,)),
            dma((rows - 1,)),
            dma,
            dma,
            dma((rows - 1,)),
            dma((rows - 1,)),
        ],
        compiler_params=pltpu.CompilerParams(
            collective_id=0, has_side_effects=True, vmem_limit_bytes=40 * 2**20
        ),
        name="gain",
    )(
        *(
            pltpu.with_memory_space_constraint(array, pltpu.HBM)
            for array in (
                cov.T,
                weights.reshape(1, owned),
                act,
                upstream,
                neighbors,
                types.reshape(frames, 1, atoms),
                type_gain,
                sens,
                frame_for_measure.reshape(1, mg),
                noise_variance.reshape(1, measures),
                innovation.reshape(1, measures),
            )
        )
    )
    parts = width // (8 * math.gcd(width // 8, 9))
    cov_new = pl.pallas_call(
        functools.partial(update_kernel, parts),
        in_specs=[vmem] * 3,
        out_specs=pl.BlockSpec(memory_space=pltpu.HBM),
        out_shape=jax.ShapeDtypeStruct((width, height), F32),
        scratch_shapes=[pltpu.VMEM((width, height), F32), dma((parts,))],
        compiler_params=pltpu.CompilerParams(vmem_limit_bytes=36 * 2**20),
        name="update",
    )(block, n_rows, gain)
    return weights_new.reshape(owned), cov_new.T


def solution(mesh):
    return jax.shard_map(
        on_device,
        mesh=mesh,
        in_specs=(
            P("row", "col"),
            P(("row", "col")),
            P("row", "col", None),
            P("row", "col", None),
            P("row", "col", None),
            P("row", "col"),
            P(),
            P("row", "col"),
            P("row"),
            P(),
            P(),
        ),
        out_specs=(P(("row", "col")), P("row", "col")),
        check_vma=False,
    )
```

```python
import functools
import math

import jax
import jax.numpy as jnp
from jax import lax
from jax.experimental import pallas as pl
from jax.experimental.pallas import tpu as pltpu
from jax.sharding import PartitionSpec as P

NS_ITERS = 5
MESH = pl.DeviceIdType.MESH
FULL = lax.Precision.HIGHEST
F32 = jnp.float32
BF16 = jnp.bfloat16
NT = (((1,), (1,)), ((), ()))


def gain_kernel(
    rows,
    cols,
    cov_hbm,
    weights_hbm,
    act_hbm,
    up_hbm,
    nb_hbm,
    types_hbm,
    tgain_hbm,
    sens_hbm,
    frame_hbm,
    noise_hbm,
    innov_hbm,
    nt_ref,
    gt_ref,
    wnew_ref,
    cov_f,
    weights_ref,
    tgain_ref,
    frame_ref,
    noise_ref,
    innov_ref,
    cov_hi,
    cov_lo,
    nb_all,
    kind_all,
    act_pair,
    sens_pair,
    counts,
    counts_b,
    up_all,
    act_all,
    sens_all,
    adj_t,
    adj_all,
    w_rows,
    jac_half,
    jac_in,
    jac_piece,
    jac_all,
    n_part,
    n_in,
    n_piece,
    n_pair,
    n_wide,
    n_col,
    n_slices,
    n_own,
    jac_own,
    jac_col,
    t_mine,
    t_other,
    t_in,
    t_rows,
    load_sem,
    cov_sem,
    row_in,
    sib_send,
    sib_recv,
    u_first,
    u_send,
    u_recv,
    a_first,
    sn_first,
    a_send,
    a_recv,
    sn_send,
    sn_recv,
    ad_send,
    ad_recv,
    m_send,
    m_recv,
    f_send,
    f_recv,
    y_send,
    y_recv,
    c_send,
    c_recv,
    o_send,
    o_recv,
    j_send,
    j_recv,
    t_send,
    t_recv,
    q_send,
    q_recv,
):
    r = lax.axis_index("row")
    c = lax.axis_index("col")
    chips = cols // 2
    per = cols // rows
    zs = per // 2
    h = c // 2
    s = c % 2
    x = c // per
    z = (c % per) // 2
    jz = c % per
    parity = lax.rem(h + s, 2)
    drains = []
    other = 1 - s
    sib = c + 1 - 2 * s
    atoms = nb_hbm.shape[1]
    pair = 2 * atoms
    nbr = nb_hbm.shape[2]
    adjw = up_hbm.shape[2]
    actw = act_hbm.shape[2]
    mg = sens_hbm.shape[0]
    measures = mg * rows
    width, chunk = cov_hi.shape[1:]
    bl = adjw // chips

    def remote(src, dst, ssem, rsem, tr, tc):
        return pltpu.make_async_remote_copy(
            src_ref=src,
            dst_ref=dst,
            send_sem=ssem,
            recv_sem=rsem,
            device_id=(tr, tc),
            device_id_type=MESH,
        )

    cov_in = [
        pltpu.make_async_copy(
            cov_hbm.at[:, pl.ds(j * chunk, chunk)],
            cov_f.at[:, pl.ds(j * chunk, chunk)],
            cov_sem.at[j],
        )
        for j in range(zs)
    ]

    mine = pl.ds(pl.multiple_of(c * atoms, atoms), atoms)
    loads = [
        pltpu.make_async_copy(src, dst, load_sem.at[i])
        for i, (src, dst) in enumerate(
            (
                (up_hbm.at[s], up_all.at[mine]),
                (nb_hbm.at[s], nb_all.at[s]),
                (act_hbm.at[s], act_pair.at[s]),
                (sens_hbm, sens_pair.at[s]),
                (types_hbm.at[s], kind_all.at[s]),
                (tgain_hbm, tgain_ref),
                (frame_hbm, frame_ref),
                (noise_hbm, noise_ref),
                (innov_hbm, innov_ref),
                (weights_hbm, weights_ref),
            )
        )
    ]
    barrier = pltpu.get_barrier_semaphore()

    def along(in_z, d):
        z_line = x * zs + lax.rem(z + d + zs, zs)
        x_line = lax.rem(x + d + zs, zs) * zs + z
        return jnp.where(in_z, z_line, x_line)

    line_mates = [(r, sib)]
    for d in range(1, zs):
        line_mates += [(r, 2 * along(True, d) + s), (r, 2 * along(False, d) + s)]
    for d in range(1, rows):
        line_mates.append((lax.rem(r + d, rows), c))
    loads[0].start()
    for mate in line_mates:
        pl.semaphore_signal(barrier, inc=1, device_id=mate, device_id_type=MESH)
    for load in loads[1:] + cov_in:
        load.start()
    pl.semaphore_wait(barrier, len(line_mates))

    sib_copies = [
        remote(nb_hbm.at[other], nb_all.at[s], sib_send.at[0], sib_recv.at[0], r, sib),
        remote(act_hbm.at[other], act_pair.at[s], sib_send.at[1], sib_recv.at[1], r, sib),
        remote(sens_hbm, sens_pair.at[s], sib_send.at[2], sib_recv.at[2], r, sib),
        remote(types_hbm.at[other], kind_all.at[s], sib_send.at[3], sib_recv.at[3], r, sib),
    ]
    sib_up = remote(up_hbm.at[other], up_all.at[mine], sib_send.at[6], sib_recv.at[6], r, sib)
    sib_up.start()
    for copy in sib_copies:
        copy.start()

    def lanes_of(chip):
        return pl.ds(pl.multiple_of(chip * pair, pair), pair)

    lanes_mine = lanes_of(h)
    begin_z = s == 0
    then_z = s == 1
    up_tree = (lambda chip: up_all.at[lanes_of(chip)], u_first, u_send, u_recv)
    act_tree = (lambda chip: act_all.at[:, lanes_of(chip)], a_first, a_send, a_recv)
    sens_tree = (lambda chip: sens_all.at[:, lanes_of(chip)], sn_first, sn_send, sn_recv)

    def begin(tree):
        block, first, send, recv = tree
        part = block(h)
        for d in range(1, zs):
            remote(part, part, send, first.at[d - 1], r, 2 * along(begin_z, d) + s).start()

    def spread_line(tree, e):
        block, first, send, recv = tree
        part = block(along(begin_z, -e))
        if e > 0:
            pltpu.make_async_copy(part, part, first.at[e - 1]).wait()
        for d in range(1, zs):
            remote(part, part, send, recv, r, 2 * along(then_z, d) + s).start()

    loads[0].wait()
    sib_up.wait_recv()
    begin(up_tree)
    spread_line(up_tree, 0)
    for load in loads[1:]:
        load.wait()
    sib_copies[1].wait_recv()
    sib_copies[2].wait_recv()
    act_all[:, lanes_mine] = jnp.transpose(
        act_pair[...].reshape(pair, actw).astype(F32)
    ).astype(BF16)
    sens_all[:, lanes_mine] = jnp.concatenate([sens_pair[0], sens_pair[1]], axis=1)
    for tree in (act_tree, sens_tree):
        begin(tree)
    for e in range(1, zs):
        spread_line(up_tree, e)
    for tree in (act_tree, sens_tree):
        spread_line(tree, 0)

    def bulk(count):
        blocks = pl.ds(0, count * pair)
        return ((up_all.at[blocks], u_send, u_recv),) + tuple(
            (buf.at[:, blocks], send, recv)
            for buf, send, recv in ((sens_all, sn_send, sn_recv), (act_all, a_send, a_recv))
        )

    def drain_first():
        for copy in [sib_up, *sib_copies]:
            copy.wait_send()
        for part, send, _ in bulk(chips - 1):
            pltpu.make_async_copy(part, part, send).wait()

    drains.append(drain_first)

    sib_copies[0].wait_recv()
    his = counts.shape[0]
    iota_lo = lax.broadcasted_iota(jnp.int32, (128, nbr), 0)
    iota_hi = lax.broadcasted_iota(jnp.int32, (his, nbr), 0)
    unroll = 8

    def count(step, _):
        t = step // (atoms // unroll)
        base = pl.multiple_of(lax.rem(step, atoms // unroll) * unroll, unroll)
        block = nb_all[t, pl.ds(base, unroll), :]
        for u in range(unroll):
            idx = block[u : u + 1, :]
            low = jnp.where((idx & 127) == iota_lo, 1.0, 0.0).astype(BF16)
            high = jnp.where((idx >> 7) == iota_hi, 1.0, 0.0).astype(BF16)
            got = lax.dot_general(high, low, NT, preferred_element_type=F32)
            row = t * atoms + base + u
            counts[:, pl.ds(row, 1), :] = got.reshape(his, 1, 128)
        return 0

    steps = pair // unroll
    for e in range(zs):
        if e > 0:
            spread_line(act_tree, e)
            spread_line(sens_tree, e)
        lax.fori_loop(steps * e // zs, steps * (e + 1) // zs, count, 0)
    for k in range(his):
        counts_b[:, k * 128 : (k + 1) * 128] = counts[k].astype(BF16)


    part, _, recv = bulk(chips - zs)[0]
    pltpu.make_async_copy(part, part, recv).wait()
    for d in range(1, rows):
        to = lax.rem(r + d, rows)
        pl.semaphore_signal(row_in, inc=1, device_id=(to, c), device_id_type=MESH)
    neighbor_sum = jnp.dot(
        counts_b[...], up_all[...], preferred_element_type=F32
    ) * (1.0 / math.sqrt(nbr))
    own = up_all[pl.ds(pl.multiple_of(h * pair, pair), pair), :].astype(F32)
    sib_copies[3].wait_recv()
    kinds = jnp.concatenate([kind_all[0], kind_all[1]], axis=1)
    kinds = jnp.transpose(jnp.broadcast_to(kinds, (adjw, pair)))
    type_scale = jnp.zeros((pair, adjw), F32)
    for kind in range(tgain_ref.shape[0]):
        type_scale = jnp.where(kinds == kind, tgain_ref[kind : kind + 1, :], type_scale)
    adj_t[...] = jnp.transpose(type_scale * (own + neighbor_sum)).reshape(chips, bl, pair)
    own_adj = pltpu.make_async_copy(adj_t.at[h], adj_all.at[:, lanes_mine], ad_recv)
    own_adj.start()

    def send_adj(k, _):
        to = lax.rem(h + k, chips)
        remote(adj_t.at[to], adj_all.at[:, lanes_mine], ad_send, ad_recv, r, 2 * to + s).start()
        return 0

    lax.fori_loop(1, chips, send_adj, 0)

    def drain_adj():
        part = adj_all.at[:, pl.ds(0, (chips - 1) * pair)]
        pltpu.make_async_copy(part, part, ad_send).wait()

    drains.append(drain_adj)

    strip = 64

    def split(j):
        def body(i, _):
            at = pl.ds(pl.multiple_of(i * strip, strip), strip)
            value = cov_f[at, j * chunk : (j + 1) * chunk]
            high = value.astype(BF16)
            cov_hi[j, at, :] = high
            cov_lo[j, at, :] = (value - high.astype(F32)).astype(BF16)
            return 0

        lax.fori_loop(0, width // strip, body, 0)

    for j in range(zs):
        cov_in[j].wait()
        split(j)

    for part, _, recv in bulk(chips - zs)[1:]:
        pltpu.make_async_copy(part, part, recv).wait()
    m0 = lax.broadcasted_iota(jnp.int32, (mg, mg), 0)
    m1 = lax.broadcasted_iota(jnp.int32, (mg, mg), 1)
    frame_of = jnp.sum(
        jnp.where(m0 == m1, frame_ref[...].astype(F32), 0.0), axis=1, keepdims=True
    )
    chosen = jnp.where(frame_of == s.astype(F32), 1.0, 0.0)
    sens_own = sens_all[...] * chosen
    pltpu.make_async_copy(adj_all, adj_all, ad_recv).wait()
    for b in range(bl):
        w_rows[mg * b : mg * (b + 1), :] = (sens_own * adj_all[b : b + 1, :]).astype(BF16)
    jac_half[...] = lax.dot_general(
        w_rows[...], act_all[...], NT, preferred_element_type=F32
    )
    swap = remote(jac_half, jac_in, sib_send.at[4], sib_recv.at[4], r, sib)
    swap.start()
    swap.wait_recv()
    whole = jac_half[...] + jac_in[...]
    jac_piece[...] = jnp.concatenate(
        [whole[mg * b : mg * (b + 1), :] for b in range(bl)], axis=1
    ).astype(BF16)
    drains.append(swap.wait_send)
    rows_half = bl * mg // 2
    own_half = jnp.where(s == 0, whole[:rows_half], whole[rows_half:])
    jac_own[...] = jnp.concatenate(
        [own_half[mg * b : mg * (b + 1), :] for b in range(bl // 2)], axis=1
    ).astype(BF16)
    jac_col[r] = jac_own[...]

    half = chips // 2

    def cast(piece, buf, stage):
        at = pl.ds(pl.multiple_of(mg * r, mg), mg)
        lanes = pl.ds(pl.multiple_of(chunk * z, chunk), chunk)
        dst = buf.at[at, lanes]
        rsem = m_recv.at[stage, z * rows + r]
        own = (x == r) & (s == 0)

        @pl.when(own)
        def _():
            pltpu.make_async_copy(piece, dst, rsem).start()

        @pl.when(jnp.logical_not(own))
        def _():
            to = 2 * lax.rem(h + s, chips) + s
            remote(piece, dst, m_send.at[stage, 0], rsem, x, to).start()

        def send(i, _):
            to = 2 * lax.rem(h + 2 * i + s, chips) + s
            remote(piece, dst, m_send.at[stage, i], rsem, x, to).start()
            return 0

        lax.fori_loop(1, half, send, 0)

        def drain():
            @pl.when(jnp.logical_not(own))
            def _():
                pltpu.make_async_copy(piece, piece, m_send.at[stage, 0]).wait()

            def step(i, _):
                pltpu.make_async_copy(piece, piece, m_send.at[stage, i]).wait()
                return 0

            lax.fori_loop(1, half, step, 0)

        drains.append(drain)

    def slot(buf, i, which):
        zz = 2 * (i // rows) + which
        p = lax.rem(i, rows)
        lanes = pl.ds(pl.multiple_of(chunk * zz, chunk), chunk)
        return buf.at[pl.ds(pl.multiple_of(mg * p, mg), mg), lanes], zz * rows + p

    def relay(buf, stage):
        def step(i, _):
            here, k = slot(buf, i, parity)
            pltpu.make_async_copy(here, here, m_recv.at[stage, k]).wait()
            remote(here, here, f_send.at[stage, i], f_recv.at[stage, k], r, sib).start()
            return 0

        lax.fori_loop(0, half, step, 0)

        def drain():
            def step2(i, _):
                here, _ = slot(buf, i, parity)
                pltpu.make_async_copy(here, here, f_send.at[stage, i]).wait()
                return 0

            lax.fori_loop(0, half, step2, 0)

        drains.append(drain)

    def relayed(buf, stage):
        def step(i, _):
            there, k = slot(buf, i, 1 - parity)
            pltpu.make_async_copy(there, there, f_recv.at[stage, k]).wait()
            return 0

        lax.fori_loop(0, half, step, 0)

    pl.semaphore_wait(row_in, rows - 1)
    cast(jac_piece, jac_all, 0)
    for d in range(1, rows):
        to = lax.rem(r + d, rows)
        copy = remote(jac_own, jac_col.at[r], j_send.at[d - 1], j_recv.at[d - 1], to, c)
        copy.start()
        drains.append(copy.wait_send)
    relay(jac_all, 0)

    def times(which):
        def step(i, _):
            zz = 2 * i + which
            jac = jac_all[:, pl.ds(pl.multiple_of(chunk * zz, chunk), chunk)]
            n_part[...] += (
                lax.dot_general(jac, cov_hi[zz], NT, preferred_element_type=F32)
                + lax.dot_general(jac, cov_lo[zz], NT, preferred_element_type=F32)
            ).reshape(rows, mg, width)
            return 0

        lax.fori_loop(0, zs // 2, step, 0)

    n_part[...] = jnp.zeros_like(n_part)
    times(parity)
    relayed(jac_all, 0)
    times(1 - parity)
    for d in range(1, rows):
        to = lax.rem(r + d, rows)
        copy = remote(n_part.at[to], n_in.at[d - 1], y_send.at[d - 1], y_recv.at[d - 1], to, c)
        copy.start()
        drains.append(copy.wait_send)
    for d in range(1, rows):
        pltpu.make_async_copy(n_in.at[d - 1], n_in.at[d - 1], y_recv.at[d - 1]).wait()
    mine_n = n_part[r]
    for d in range(1, rows):
        mine_n = mine_n + n_in[d - 1]
    n_piece[...] = mine_n.astype(BF16)
    swap_n = remote(n_piece, n_pair.at[s], sib_send.at[5], sib_recv.at[5], r, sib)
    swap_n.start()
    drains.append(swap_n.wait_send)
    n_pair[s] = n_piece[...]
    n_col[r] = n_piece[...]
    for d in range(1, rows):
        pltpu.make_async_copy(jac_own, jac_own, j_recv.at[d - 1]).wait()
    n_low = (mine_n - n_piece[...].astype(F32)).astype(BF16)
    jac_here = jac_col[...].reshape(measures, width)
    part = lax.dot_general(
        n_piece[...], jac_here, NT, preferred_element_type=F32
    ) + lax.dot_general(n_low, jac_here, NT, preferred_element_type=F32)
    t_mine[...] = jnp.concatenate([part[: mg // 2], part[mg // 2 :]], axis=1)
    swap_t = remote(t_mine, t_other, sib_send.at[7], sib_recv.at[7], r, sib)
    swap_t.start()
    drains.append(swap_t.wait_send)
    swap_t.wait_recv()
    t_in[h] = t_mine[...] + t_other[...]

    def send_part(k, _):
        to = 2 * lax.rem(h + k, chips) + s
        remote(t_in.at[h], t_in.at[h], t_send, t_recv, r, to).start()
        return 0

    lax.fori_loop(1, chips, send_part, 0)

    def drain_part():
        sent = t_in.at[pl.ds(0, chips - 1)]
        pltpu.make_async_copy(sent, sent, t_send).wait()

    drains.append(drain_part)
    swap_n.wait_recv()
    n_wide[...] = jnp.concatenate(
        [n_pair[0].astype(F32), n_pair[1].astype(F32)], axis=1
    ).astype(BF16)
    cast(n_wide, nt_ref, 1)
    for d in range(1, rows):
        to = lax.rem(r + d, rows)
        copy = remote(n_piece, n_col.at[r], c_send.at[d - 1], c_recv.at[d - 1], to, c)
        copy.start()
        drains.append(copy.wait_send)

    owned = n_slices.shape[2]
    for t in range(rows):
        n_slices[t] = mine_n[:, t * owned : (t + 1) * owned]
    for t in range(rows):
        to = rows * jz + t
        here = (x == r) & (to == c)

        @pl.when(here)
        def _():
            pltpu.make_async_copy(n_slices.at[t], n_own.at[r], o_recv.at[r]).start()

        @pl.when(jnp.logical_not(here))
        def _():
            remote(n_slices.at[t], n_own.at[r], o_send.at[t], o_recv.at[r], x, to).start()

    arrived = t_in.at[pl.ds(0, chips - 1)]
    pltpu.make_async_copy(arrived, arrived, t_recv).wait()
    t_rows[r] = jnp.sum(t_in[...], axis=0)
    for d in range(1, rows):
        to = lax.rem(r + d, rows)
        copy = remote(t_rows.at[r], t_rows.at[r], q_send.at[d - 1], q_recv.at[d - 1], to, c)
        copy.start()
        drains.append(copy.wait_send)
    relay(nt_ref, 1)
    for d in range(1, rows):
        pltpu.make_async_copy(t_rows.at[0], t_rows.at[0], q_recv.at[d - 1]).wait()
    pieces = []
    for q in range(rows):
        packed = t_rows[q]
        pieces += [packed[:, :measures], packed[:, measures:]]
    innovation_cov = jnp.concatenate(pieces, axis=0)
    i0 = lax.broadcasted_iota(jnp.int32, (measures, measures), 0)
    i1 = lax.broadcasted_iota(jnp.int32, (measures, measures), 1)
    eye = jnp.where(i0 == i1, 1.0, 0.0).astype(F32)
    innovation_cov = innovation_cov + eye * noise_ref[...]
    row_sums = jnp.sum(jnp.abs(innovation_cov), axis=1, keepdims=True)
    first = 1.0 / jnp.max(row_sums, axis=0, keepdims=True)
    inverse = eye * first
    left = eye - innovation_cov * first
    for sweep in range(NS_ITERS):
        if sweep == NS_ITERS - 1:
            both = inverse
        else:
            both = jnp.concatenate([inverse, left], axis=0)
        both = jnp.dot(both, left, precision=FULL, preferred_element_type=F32)
        inverse = inverse + both[:measures]
        left = both[measures:]
    for d in range(1, rows):
        pltpu.make_async_copy(n_piece, n_piece, c_recv.at[d - 1]).wait()
    n_cols = n_col[...].reshape(measures, width).astype(F32)
    gt_ref[...] = jnp.transpose(
        jnp.dot(inverse, n_cols, precision=FULL, preferred_element_type=F32)
    ).astype(BF16)
    step_col = jnp.sum(inverse * innov_ref[...], axis=1, keepdims=True)
    for p in range(rows):
        pltpu.make_async_copy(n_own.at[p], n_own.at[p], o_recv.at[p]).wait()
    n_mine = n_own[...].reshape(measures, owned)
    wnew_ref[...] = weights_ref[...] + jnp.sum(step_col * n_mine, axis=0, keepdims=True)
    for t in range(rows):
        to = rows * jz + t

        @pl.when(jnp.logical_not((x == r) & (to == c)))
        def _():
            pltpu.make_async_copy(n_slices.at[t], n_slices.at[t], o_send.at[t]).wait()

    relayed(nt_ref, 1)
    for drain in drains:
        drain()


def update_kernel(parts, cov_ref, nt_ref, gt_ref, out_hbm, made, out_sem):
    tile = made.shape[0] // parts
    copies = []
    for i in range(parts):
        at = pl.ds(i * tile, tile)
        made[at, :] = cov_ref[at, :] - jnp.dot(
            gt_ref[at, :], nt_ref[...], preferred_element_type=F32
        )
        copies.append(pltpu.make_async_copy(made.at[at], out_hbm.at[at], out_sem.at[i]))
        copies[-1].start()
    for copy in copies:
        copy.wait()


def on_device(
    cov,
    weights,
    act,
    upstream,
    neighbors,
    types,
    type_gain,
    sens,
    frame_for_measure,
    noise_variance,
    innovation,
):
    rows = lax.axis_size("row")
    cols = lax.axis_size("col")
    per = cols // rows
    chips = cols // 2
    frames, atoms, nbr = neighbors.shape
    pair = 2 * atoms
    all_atoms = cols * atoms
    adjw, actw = upstream.shape[2], act.shape[2]
    mg = sens.shape[0]
    measures = mg * rows
    height, width = cov.shape
    zs = per // 2
    chunk = height // zs
    owned = weights.shape[0]
    bl = adjw // chips
    his = all_atoms // 128
    dma = pltpu.SemaphoreType.DMA
    vmem = pl.BlockSpec(memory_space=pltpu.VMEM)
    n_rows, gain, weights_new, block = pl.pallas_call(
        functools.partial(gain_kernel, rows, cols),
        out_shape=(
            jax.ShapeDtypeStruct((measures, height), BF16),
            jax.ShapeDtypeStruct((width, measures), BF16),
            jax.ShapeDtypeStruct((1, owned), F32),
            jax.ShapeDtypeStruct((width, height), F32),
        ),
        in_specs=[pl.BlockSpec(memory_space=pltpu.HBM)] * 11,
        out_specs=(vmem,) * 4,
        scratch_shapes=[
            pltpu.VMEM((1, owned), F32),
            pltpu.VMEM(type_gain.shape, F32),
            pltpu.VMEM((1, mg), jnp.int32),
            pltpu.VMEM((1, measures), F32),
            pltpu.VMEM((1, measures), F32),
            pltpu.VMEM((zs, width, chunk), BF16),
            pltpu.VMEM((zs, width, chunk), BF16),
            pltpu.VMEM((2, atoms, nbr), jnp.int32),
            pltpu.VMEM((2, 1, atoms), jnp.int32),
            pltpu.VMEM((2, atoms, actw), BF16),
            pltpu.VMEM((2, mg, atoms), F32),
            pltpu.VMEM((his, pair, 128), F32),
            pltpu.VMEM((pair, all_atoms), BF16),
            pltpu.VMEM((all_atoms, adjw), BF16),
            pltpu.VMEM((actw, all_atoms), BF16),
            pltpu.VMEM((mg, all_atoms), F32),
            pltpu.VMEM((chips, bl, pair), F32),
            pltpu.VMEM((bl, all_atoms), F32),
            pltpu.VMEM((bl * mg, all_atoms), BF16),
            pltpu.VMEM((bl * mg, actw), F32),
            pltpu.VMEM((bl * mg, actw), F32),
            pltpu.VMEM((mg, chunk), BF16),
            pltpu.VMEM((measures, height), BF16),
            pltpu.VMEM((rows, mg, width), F32),
            pltpu.VMEM((rows - 1, mg, width), F32),
            pltpu.VMEM((mg, width), BF16),
            pltpu.VMEM((2, mg, width), BF16),
            pltpu.VMEM((mg, chunk), BF16),
            pltpu.VMEM((rows, mg, width), BF16),
            pltpu.VMEM((rows, mg, owned), F32),
            pltpu.VMEM((rows, mg, owned), F32),
            pltpu.VMEM((mg, width), BF16),
            pltpu.VMEM((rows, mg, width), BF16),
            pltpu.VMEM((mg // 2, 2 * measures), F32),
            pltpu.VMEM((mg // 2, 2 * measures), F32),
            pltpu.VMEM((chips, mg // 2, 2 * measures), F32),
            pltpu.VMEM((rows, mg // 2, 2 * measures), F32),
            dma((10,)),
            dma((zs,)),
            pltpu.SemaphoreType.REGULAR,
            dma((8,)),
            dma((8,)),
            dma((zs - 1,)),
            dma,
            dma,
            dma((zs - 1,)),
            dma((zs - 1,)),
            dma,
            dma,
            dma,
            dma,
            dma,
            dma,
            dma((2, chips // 2)),
            dma((2, zs * rows)),
            dma((2, chips // 2)),
            dma((2, zs * rows)),
            dma((rows - 1,)),
            dma((rows - 1,)),
            dma((rows - 1,)),
            dma((rows - 1,)),
            dma((rows,)),
            dma((rows,)),
            dma((rows - 1,)),
            dma((rows - 1,)),
            dma,
            dma,
            dma((rows - 1,)),
            dma((rows - 1,)),
        ],
        compiler_params=pltpu.CompilerParams(
            collective_id=0, has_side_effects=True, vmem_limit_bytes=40 * 2**20
        ),
        name="gain",
    )(
        *(
            pltpu.with_memory_space_constraint(array, pltpu.HBM)
            for array in (
                cov.T,
                weights.reshape(1, owned),
                act,
                upstream,
                neighbors,
                types.reshape(frames, 1, atoms),
                type_gain,
                sens,
                frame_for_measure.reshape(1, mg),
                noise_variance.reshape(1, measures),
                innovation.reshape(1, measures),
            )
        )
    )
    parts = width // (8 * math.gcd(width // 8, 9))
    cov_new = pl.pallas_call(
        functools.partial(update_kernel, parts),
        in_specs=[vmem] * 3,
        out_specs=pl.BlockSpec(memory_space=pltpu.HBM),
        out_shape=jax.ShapeDtypeStruct((width, height), F32),
        scratch_shapes=[pltpu.VMEM((width, height), F32), dma((parts,))],
        compiler_params=pltpu.CompilerParams(vmem_limit_bytes=36 * 2**20),
        name="update",
    )(block, n_rows, gain)
    return weights_new.reshape(owned), cov_new.T


def solution(mesh):
    return jax.shard_map(
        on_device,
        mesh=mesh,
        in_specs=(
            P("row", "col"),
            P(("row", "col")),
            P("row", "col", None),
            P("row", "col", None),
            P("row", "col", None),
            P("row", "col"),
            P(),
            P("row", "col"),
            P("row"),
            P(),
            P(),
        ),
        out_specs=(P(("row", "col")), P("row", "col")),
        check_vma=False,
    )
```
